32 devices in a mesh: dp: 4 (over y, x), row: 4 (over z), col: 2 (over core).
Axes of the slice: x: 2, y: 2, z: 4, core: 2. Of those that a mesh axis runs over, the one named last changes fastest.
Arguments:
- queries: bfloat16 [4, 48, 32, 1024], P('dp', 'row', 'col'), may hold values from -6 to 6
- keyvals: bfloat16 [4, 2, 48, 32, 1024], P('dp', None, 'row', 'col'), may hold values from -6 to 6
- out_weight: bfloat16 [4, 1024, 2048], P('dp', ('row', 'col')), may hold values from -0.75 to 0.75
- gate_weight: bfloat16 [4, 2048, 2048], P('dp', ('row', 'col')), may hold values from -0.125 to 0.125
- class_table: bfloat16 [4, 1000, 2048], P('dp', None, ('row', 'col')), may hold values from -5 to 5
- labels: int32 [4], P('dp'), may hold values from 0 to 999
- timesteps: int32 [4], P('dp'), may hold values from 0 to 999
- round_index: int32 [1], replicated, may hold values from 0 to 996
Outputs:
- update: bfloat16 [4, 48, 32, 2048], P('dp', 'row', 'col')
The draws below stay inside these ranges and needn't reach their ends.
All inputs are finite; a program needn't handle non-finite values.
Results may differ from the reference program's by a relative error of at most 0.0081.
Values may be sent and summed in bfloat16 or wider, within the bound.
A program may use at most 64 MiB of HBM per device.

```python
import math
import jax
import jax.numpy as jnp
from jax import lax

D = 2048
HEADS = 8
HDIM = 128
CLASSES = 1000
RADIUS = 3
INNER = 1024
IMAGES = 4
GRID_ROWS = 48
GRID_COLS = 32
N_DP = 4


def draw_queries(key, part):
    key = jax.random.fold_in(key, 11)
    shape_all = (IMAGES, GRID_ROWS, GRID_COLS, INNER)
    base_draw = jnp.clip(jax.random.normal(key, shape_all, jnp.float32), -4.0, 4.0)
    return base_draw.astype(jnp.bfloat16)


def draw_keyvals(key, part):
    key = jax.random.fold_in(key, 12)
    shape_all = (IMAGES, 2, GRID_ROWS, GRID_COLS, INNER)
    base_draw = jnp.clip(jax.random.normal(key, shape_all, jnp.float32), -4.0, 4.0)
    return base_draw.astype(jnp.bfloat16)


def plant(array, rng, least, largest):
    extent = array.shape
    spot = [jax.random.randint(jax.random.fold_in(rng, axis), (), 0, extent[axis]) for axis in range(len(extent))]
    array = array.at[tuple(spot)].set(least)
    longest = extent.index(max(extent))
    spot[longest] = (spot[longest] + 1) % extent[longest]
    return array.at[tuple(spot)].set(largest)


def block_levels(stream_key, dims, pieces, smallest, largest):
    def one(dim, blocks):
        draws = jax.random.uniform(jax.random.fold_in(jax.random.fold_in(stream_key, 6), dim), (blocks,), jnp.float32, smallest / len(pieces), largest / len(pieces))
        return jnp.repeat(jnp.exp(draws), dims[dim] // blocks).reshape((-1,) + (1,) * (len(dims) - dim - 1))

    factor_of = one(*pieces[0])
    for cut in pieces[1:]:
        factor_of = factor_of * one(*cut)
    return factor_of


def centred(rng, dims, scale, most, pieces=(), kind=jnp.bfloat16):
    array = scale * jax.random.normal(rng, dims, jnp.float32)
    if pieces:
        array = array * block_levels(rng, dims, pieces, -0.22, 0.18)
    return jnp.clip(array, -most, most).astype(kind)


def setup_inputs(seed: int = 0) -> dict:
    key_of = jax.random.split(jax.random.key(seed), 9)
    queries = draw_queries(jax.random.fold_in(key_of[8], 71), 0)
    keyvals = draw_keyvals(jax.random.fold_in(key_of[8], 71), 0)
    out_weight = centred(key_of[2], (IMAGES, INNER, D), (INNER // 16) ** -0.5, 0.75, ((0, 4), (1, 8)))
    gate_weight = centred(key_of[3], (IMAGES, D, D), D ** -0.5, 0.125, ((0, 4), (1, 8)))
    class_table = centred(key_of[4], (IMAGES, CLASSES, D), 1.0, 5.0, ((0, 4), (2, 8)))
    labels = plant(jax.random.randint(key_of[5], (IMAGES,), 0, CLASSES), jax.random.fold_in(key_of[5], 1), 0, CLASSES - 1).astype(jnp.int32)
    timesteps = plant(jax.random.randint(key_of[6], (IMAGES,), 0, 1000), jax.random.fold_in(key_of[6], 1), 0, 999).astype(jnp.int32)
    round_index = jax.random.randint(key_of[7], (1,), 0, 997).astype(jnp.int32)
    return dict(queries=queries, keyvals=keyvals, out_weight=out_weight, gate_weight=gate_weight, class_table=class_table, labels=labels, timesteps=timesteps, round_index=round_index)


def time_embed(step_value, width):
    half_width = width // 2
    positions = jnp.arange(width)
    freq_index = (positions % half_width).astype(jnp.float32)
    frequency = jnp.exp(-math.log(10000.0) * freq_index / half_width)
    angle_value = step_value * frequency
    return jnp.where(positions < half_width, jnp.cos(angle_value), jnp.sin(angle_value))

def mix_params(params, distance):
    shifted = jnp.roll(params, distance, axis=0)
    return (0.5 * (params.astype(jnp.float32) + shifted.astype(jnp.float32))).astype(jnp.bfloat16)

def attend(query_img, keyval_img):
    rows_total = query_img.shape[0]
    cols_total = query_img.shape[1]
    window = 2 * RADIUS + 1
    score_scale = 1.0 / math.sqrt(HDIM)
    query_heads = query_img.reshape(rows_total, cols_total, HEADS, HDIM).astype(jnp.float32)
    padded = jnp.pad(keyval_img, ((0, 0), (RADIUS, RADIUS), (RADIUS, RADIUS), (0, 0)))
    padded = padded.reshape(2, rows_total + 2 * RADIUS, cols_total + 2 * RADIUS, HEADS, HDIM)
    inside = jnp.pad(jnp.ones((rows_total, cols_total), jnp.bool_), RADIUS)
    score_list = []
    for row_off in range(window):
        for col_off in range(window):
            key_here = padded[0, row_off:row_off + rows_total, col_off:col_off + cols_total].astype(jnp.float32)
            score_here = jnp.einsum('xyhd,xyhd->xyh', query_heads, key_here) * score_scale
            valid = inside[row_off:row_off + rows_total, col_off:col_off + cols_total]
            score_list.append(jnp.where(valid[:, :, None], score_here, jnp.float32(-1e+30)))
    scores = jnp.stack(score_list, axis=-1)
    row_max = lax.optimization_barrier(jnp.max(scores, axis=-1, keepdims=True))
    exponent = jnp.exp(scores - row_max)
    probs = (exponent / lax.optimization_barrier(jnp.sum(exponent, axis=-1, keepdims=True))).astype(jnp.bfloat16)
    attended = jnp.zeros((rows_total, cols_total, HEADS, HDIM), jnp.float32)
    for row_off in range(window):
        for col_off in range(window):
            value_here = padded[1, row_off:row_off + rows_total, col_off:col_off + cols_total].astype(jnp.float32)
            weight_here = probs[..., row_off * window + col_off].astype(jnp.float32)
            attended = attended + weight_here[..., None] * value_here
    return attended.astype(jnp.bfloat16).reshape(rows_total * cols_total, HEADS * HDIM)

def reference(queries, keyvals, out_weight, gate_weight, class_table, labels, timesteps, round_index):
    bit_count = int(N_DP).bit_length() - 1
    distance = jnp.left_shift(jnp.int32(1), (round_index[0] % bit_count).astype(jnp.int32))
    out_mixed = mix_params(out_weight, distance)
    gate_mixed = mix_params(gate_weight, distance)
    table_mixed = mix_params(class_table, distance)

    def one_image(bundle):
        query_img, keyval_img, out_img, gate_img, table_img, label_img, step_img = bundle
        class_row = lax.dynamic_index_in_dim(table_img, label_img.astype(jnp.int32), 0, keepdims=False)
        embed = time_embed(step_img.astype(jnp.float32), D)
        cond = jax.nn.silu(class_row.astype(jnp.float32) + embed).astype(jnp.bfloat16)
        gate = jnp.dot(cond[None, :], gate_img, preferred_element_type=jnp.float32)[0]
        attended = attend(query_img, keyval_img)
        projected = jnp.dot(attended, out_img, preferred_element_type=jnp.float32)
        result = (gate[None, :] * projected).astype(jnp.bfloat16)
        return result.reshape(query_img.shape[0], query_img.shape[1], D)
    return lax.map(one_image, (queries, keyvals, out_mixed, gate_mixed, table_mixed, labels, timesteps))
```

```python
import functools
import math

import jax
import jax.numpy as jnp
from jax import lax
from jax.experimental import pallas as pl
from jax.experimental.pallas import tpu as pltpu
from jax.sharding import PartitionSpec as P

HDIM = 128
RADIUS = 3
CHUNKS = 4
GROUP = 4
MESH = pl.DeviceIdType.MESH
F32 = jnp.float32
BF16 = jnp.bfloat16


def remote(src, dst, send, recv, **where):
    return pltpu.make_async_remote_copy(
        src_ref=src, dst_ref=dst, send_sem=send, recv_sem=recv, device_id=where, device_id_type=MESH
    )


def kernel(
    sizes, distance,
    q_hbm, kv_hbm, o_hbm, g_hbm, t_hbm, label_ref, step_ref,
    out_hbm,
    q_buf, kv_buf, bias, att, o_own, o_peer, w_buf, out_buf, g_buf, t_buf,
    pack_out, pack_in, reply_out, reply_in, gates,
    local_sem, out_sem, gossip_send, gossip_recv, w_up, w_down, w_side, w_recv,
    halo_send, halo_recv, side_send, side_recv, note_send, note_recv, gate_send, gate_recv,
):
    n_dp, n_row, n_col = sizes
    group = n_row * n_col
    tile_rows, tile_cols, inner = kv_hbm.shape[2:]
    shard, width = o_hbm.shape[1:]
    cut = width // CHUNKS
    span = t_hbm.shape[2]
    slot = pack_out.shape[1] // 3
    classes = t_hbm.shape[1]
    heads = inner // HDIM
    sides = [1] if n_col == 2 else [n_col - 1, 1]
    wide = kv_buf.shape[2]

    p, r, c = lax.axis_index("dp"), lax.axis_index("row"), lax.axis_index("col")
    me = r * n_col + c
    ahead, behind = lax.rem(p + distance, n_dp), lax.rem(p + n_dp - distance, n_dp)
    has_up, has_down = r > 0, r < n_row - 1

    def col_of(step):
        return lax.rem(c + step, n_col)

    loads = [
        pltpu.make_async_copy(t_hbm.at[0], t_buf, local_sem.at[0]),
        pltpu.make_async_copy(o_hbm.at[0], o_own, local_sem.at[1]),
        pltpu.make_async_copy(g_hbm.at[0], g_buf, local_sem.at[2]),
        pltpu.make_async_copy(q_hbm.at[0], q_buf, local_sem.at[3]),
        pltpu.make_async_copy(
            kv_hbm.at[0], kv_buf.at[:, pl.ds(RADIUS, tile_rows), pl.ds(0, tile_cols)], local_sem.at[4]
        ),
    ]
    for load in loads:
        load.start()

    barrier = pltpu.get_barrier_semaphore()
    for step in range(1, group):
        other = lax.rem(me + step, group)
        pl.semaphore_signal(
            barrier, inc=1, device_id={"row": other // n_col, "col": lax.rem(other, n_col)}, device_id_type=MESH
        )
    pl.semaphore_signal(barrier, inc=1, device_id={"dp": ahead}, device_id_type=MESH)
    greeted = group
    if (2 * distance) % n_dp:
        pl.semaphore_signal(barrier, inc=1, device_id={"dp": behind}, device_id_type=MESH)
        greeted += 1
    pl.semaphore_wait(barrier, greeted)

    def halo(which):
        first, place = ((0, tile_rows + RADIUS), (tile_rows - RADIUS, 0))[which]
        return remote(
            kv_hbm.at[0, :, pl.ds(first, RADIUS)],
            kv_buf.at[:, pl.ds(place, RADIUS), pl.ds(0, tile_cols)],
            halo_send.at[which], halo_recv.at[which], row=(r - 1, r + 1)[which],
        )

    def side(i):
        return remote(
            kv_hbm.at[0],
            kv_buf.at[:, pl.ds(RADIUS, tile_rows), pl.ds((i + 1) * tile_cols, tile_cols)],
            side_send.at[0, i], side_recv.at[0, i], col=col_of(sides[i]),
        )

    def corner(which, i):
        place = (tile_rows + RADIUS, 0)[which]
        rows = pl.ds(place, RADIUS)
        return remote(
            kv_buf.at[:, rows, pl.ds(0, tile_cols)],
            kv_buf.at[:, rows, pl.ds((i + 1) * tile_cols, tile_cols)],
            side_send.at[1 + which, i], side_recv.at[1 + which, i], col=col_of(sides[i]),
        )

    def gossip(k):
        return remote(
            o_hbm.at[0, :, pl.ds(k * cut, cut)], o_peer.at[k], gossip_send.at[k], gossip_recv.at[k], dp=ahead
        )

    gossip(0).start()
    pl.when(has_up)(lambda: halo(0).start())
    pl.when(has_down)(lambda: halo(1).start())
    for k in range(1, CHUNKS):
        gossip(k).start()
    for i in range(len(sides)):
        side(i).start()

    def class_row(label):
        rows = lax.broadcasted_iota(jnp.int32, (classes, span), 0).astype(F32)
        table = t_buf[...].astype(F32)
        return jnp.sum(jnp.where(rows == label, table, 0.0), axis=0, keepdims=True)

    loads[0].wait()
    label_here = jnp.full((1, span), label_ref[0], jnp.int32).astype(F32)
    pack_out[:, pl.ds(0, span)] = label_here
    pack_out[:, pl.ds(slot, span)] = jnp.full((1, span), step_ref[0], jnp.int32).astype(F32)
    pack_out[:, pl.ds(2 * slot, span)] = class_row(label_here)
    ask = remote(pack_out, pack_in, note_send.at[0], note_recv.at[0], dp=behind)
    ask.start()

    def w_copy(owner, k, sem, **where):
        rows = pl.ds(pl.multiple_of(owner * shard, shard), shard)
        place = w_buf.at[k, rows]
        return remote(place, place, sem, w_recv.at[owner, k], **where)

    def up_copy(row, k):
        return w_copy(row * n_col + c, k, w_up.at[row, k], row=r - 1)

    def down_copy(row, k):
        return w_copy(row * n_col + c, k, w_down.at[row, k], row=r + 1)

    def side_copy(row, k, step):
        return w_copy(row * n_col + c, k, w_side.at[step - 1, row, k], col=col_of(step))

    def spread(row, k):
        for step in range(1, n_col):
            side_copy(row, k, step).start()

    def own_chunk(k):
        gossip(k).wait_recv()
        both = o_own[:, pl.ds(k * cut, cut)].astype(F32) + o_peer[k].astype(F32)
        w_buf[k, pl.ds(pl.multiple_of(me * shard, shard), shard), :] = (0.5 * both).astype(BF16)
        pl.when(has_up)(lambda: up_copy(r, k).start())
        pl.when(has_down)(lambda: down_copy(r, k).start())
        spread(r, k)

    loads[1].wait()
    own_chunk(0)

    def against_gate(cond):
        tall = jnp.broadcast_to(cond, (16, span)).astype(BF16)
        return jnp.dot(tall, g_buf[...], preferred_element_type=F32)[0:1]

    half = width // 2
    position = me * span + lax.broadcasted_iota(jnp.int32, (1, span), 1)
    freq_index = jnp.where(position < half, position, position - half).astype(F32)
    frequency = jnp.exp(-math.log(10000.0) * freq_index / half)
    ask.wait_recv()
    mixed_row = 0.5 * (pack_in[:, pl.ds(2 * slot, span)] + class_row(pack_in[:, pl.ds(0, span)]))
    angle = pack_in[:, pl.ds(slot, span)] * frequency
    embed = jnp.where(position < half, jnp.cos(angle), jnp.sin(angle))
    value = mixed_row.astype(BF16).astype(F32) + embed
    cond = (value / (1.0 + jnp.exp(-value))).astype(BF16).astype(F32)
    loads[2].wait()
    reply_out[:, pl.ds(0, width)] = against_gate(cond)
    reply_out[:, pl.ds(width, span)] = cond
    answer = remote(reply_out, reply_in, note_send.at[1], note_recv.at[1], dp=ahead)
    answer.start()

    own_chunk(1)

    edge = jnp.zeros((2, RADIUS, wide, inner), BF16)

    @pl.when(jnp.logical_not(has_up))
    def _():
        kv_buf[:, pl.ds(0, RADIUS)] = edge

    @pl.when(jnp.logical_not(has_down))
    def _():
        kv_buf[:, pl.ds(tile_rows + RADIUS, RADIUS)] = edge

    n_q, n_k = GROUP * tile_cols, (GROUP + 2 * RADIUS) * wide
    blocks = wide // tile_cols
    q_index = lax.broadcasted_iota(jnp.int32, (n_q, n_k), 0)
    k_index = lax.broadcasted_iota(jnp.int32, (n_q, n_k), 1)
    q_row, q_col = q_index // tile_cols, lax.rem(q_index, tile_cols)
    k_block = k_index // tile_cols
    k_row = (k_block * -(-512 // blocks)) // 512
    k_block = k_block - k_row * blocks
    k_col = lax.rem(k_index, tile_cols)
    if n_col == 2:
        k_shift = jnp.where(k_block == 1, 1 - 2 * c, 0)
    else:
        k_shift = jnp.where(k_block == 1, 1, jnp.where(k_block == 2, -1, 0))
    k_col = k_col + k_shift * tile_cols
    near = (jnp.abs(k_col - q_col) <= RADIUS) & (k_row >= q_row) & (k_row <= q_row + 2 * RADIUS)
    k_col = k_col + c * tile_cols
    near = near & (k_col >= 0) & (k_col < n_col * tile_cols)
    for g in range(tile_rows // GROUP):
        row_here = k_row + (r * tile_rows + g * GROUP - RADIUS)
        seen = near & (row_here >= 0) & (row_here < n_row * tile_rows)
        bias[g] = seen.astype(F32)

    @pl.when(has_down)
    def _():
        halo(0).wait_recv()
        for i in range(len(sides)):
            corner(0, i).start()

    @pl.when(has_up)
    def _():
        halo(1).wait_recv()
        for i in range(len(sides)):
            corner(1, i).start()

    own_chunk(2)

    answer.wait_recv()
    share = 0.5 * (reply_in[:, pl.ds(0, width)] + against_gate(reply_in[:, pl.ds(width, span)]))
    gates[me] = share

    def gate_copy(owner, step):
        other = lax.rem(me + step, group)
        return remote(
            gates.at[owner], gates.at[owner], gate_send.at[step - 1], gate_recv.at[owner],
            row=other // n_col, col=lax.rem(other, n_col),
        )

    for step in range(1, group):
        gate_copy(me, step).start()

    for k in range(3, CHUNKS):
        own_chunk(k)

    loads[3].wait()
    loads[4].wait()
    for i in range(len(sides)):
        side(i).wait_recv()
        pl.when(has_down)(lambda i=i: corner(0, i).wait_recv())
        pl.when(has_up)(lambda i=i: corner(1, i).wait_recv())

    scale = 1.0 / math.sqrt(HDIM)

    def attend(head):
        lanes = pl.ds(pl.multiple_of(head * HDIM, HDIM), HDIM)
        for g in range(tile_rows // GROUP):
            rows = pl.ds(g * GROUP, GROUP)
            near_rows = pl.ds(g * GROUP, GROUP + 2 * RADIUS)
            query = q_buf[rows, :, lanes].reshape(n_q, HDIM)
            key = kv_buf[0, near_rows, :, lanes].reshape(n_k, HDIM)
            val = kv_buf[1, near_rows, :, lanes].reshape(n_k, HDIM)
            score = lax.dot_general(query, key, (((1,), (1,)), ((), ())), preferred_element_type=F32)
            score = jnp.where(bias[g] > 0.5, score, -1e30)
            top = jnp.max(score, axis=1, keepdims=True)
            weight = jnp.exp((score - top) * scale)
            total = jnp.sum(weight, axis=1, keepdims=True)
            mean = jnp.dot(weight.astype(BF16), val, preferred_element_type=F32) / total
            att[pl.ds(g * n_q, n_q), lanes] = mean.astype(BF16)

    def event(e, carry):
        hop, k = e // CHUNKS + 1, lax.rem(e, CHUNKS)

        @pl.when(r + hop < n_row)
        def _():
            row = r + hop
            up_copy(row, k).wait_recv()
            pl.when(has_up)(lambda: up_copy(row, k).start())
            spread(row, k)

        @pl.when((r - hop >= 0) & (hop < n_row))
        def _():
            row = r - hop
            down_copy(row, k).wait_recv()
            pl.when(has_down)(lambda: down_copy(row, k).start())
            spread(row, k)

        pl.when(e < heads)(lambda: attend(e))
        return carry

    before_last = max(heads, (n_row - 2) * CHUNKS)
    lax.fori_loop(0, before_last, event, 0)

    for step in range(1, group):
        owner = lax.rem(me + step, group)
        gate_copy(owner, step).wait_recv()
    gate = gates[0]
    for i in range(1, group):
        gate = gate + gates[i]

    def out_copy(k):
        return pltpu.make_async_copy(out_buf.at[k], out_hbm.at[:, pl.ds(k * cut, cut)], out_sem.at[k])

    for k in range(CHUNKS):
        e = (n_row - 2) * CHUNKS + k
        if e >= before_last:
            event(e, 0)
        for row in range(n_row):
            for step in range(1, n_col):
                owner = row * n_col + col_of(step)
                w_copy(owner, k, w_side.at[step - 1, row, k], col=col_of(step)).wait_recv()
        product = jnp.dot(att[...], w_buf[k], preferred_element_type=F32)
        out_buf[k] = (gate[:, k * cut : (k + 1) * cut] * product).astype(BF16)
        out_copy(k).start()

    for k in range(CHUNKS):
        out_copy(k).wait()
        gossip(k).wait_send()
        for row in range(n_row):
            pl.when(has_up & (r <= row))(lambda row=row, k=k: up_copy(row, k).wait_send())
            pl.when(has_down & (r >= row))(lambda row=row, k=k: down_copy(row, k).wait_send())
            for step in range(1, n_col):
                side_copy(row, k, step).wait_send()
    pl.when(has_up)(lambda: halo(0).wait_send())
    pl.when(has_down)(lambda: halo(1).wait_send())
    for i in range(len(sides)):
        side(i).wait_send()
        pl.when(has_down)(lambda i=i: corner(0, i).wait_send())
        pl.when(has_up)(lambda i=i: corner(1, i).wait_send())
    ask.wait_send()
    answer.wait_send()
    for step in range(1, group):
        gate_copy(me, step).wait_send()


def layer(sizes, distance, number, queries, keyvals, out_weight, gate_weight, class_table, labels, timesteps):
    n_dp, n_row, n_col = sizes
    group = n_row * n_col
    _, tile_rows, tile_cols, inner = queries.shape
    _, shard, width = out_weight.shape
    span = gate_weight.shape[1]
    classes = class_table.shape[1]
    cut = width // CHUNKS
    slot = max(span, 128)
    n_side = 1 if n_col == 2 else 2
    wide = tile_cols * (1 + n_side)
    tokens = tile_rows * tile_cols
    n_q, n_k = GROUP * tile_cols, (GROUP + 2 * RADIUS) * wide
    dma = pltpu.SemaphoreType.DMA
    return pl.pallas_call(
        functools.partial(kernel, sizes, distance),
        out_shape=jax.ShapeDtypeStruct((tokens, width), BF16),
        in_specs=[pl.BlockSpec(memory_space=pl.ANY)] * 5 + [pl.BlockSpec(memory_space=pltpu.SMEM)] * 2,
        out_specs=pl.BlockSpec(memory_space=pl.ANY),
        scratch_shapes=[
            pltpu.VMEM((tile_rows, tile_cols, inner), BF16),
            pltpu.VMEM((2, tile_rows + 2 * RADIUS, wide, inner), BF16),
            pltpu.VMEM((tile_rows // GROUP, n_q, n_k), F32),
            pltpu.VMEM((tokens, inner), BF16),
            pltpu.VMEM((shard, width), BF16),
            pltpu.VMEM((CHUNKS, shard, cut), BF16),
            pltpu.VMEM((CHUNKS, group * shard, cut), BF16),
            pltpu.VMEM((CHUNKS, tokens, cut), BF16),
            pltpu.VMEM((span, width), BF16),
            pltpu.VMEM((classes, span), BF16),
            pltpu.VMEM((1, 3 * slot), F32),
            pltpu.VMEM((1, 3 * slot), F32),
            pltpu.VMEM((1, width + slot), F32),
            pltpu.VMEM((1, width + slot), F32),
            pltpu.VMEM((group, 1, width), F32),
            dma((5,)),
            dma((CHUNKS,)),
            dma((CHUNKS,)),
            dma((CHUNKS,)),
            dma((n_row, CHUNKS)),
            dma((n_row, CHUNKS)),
            dma((n_col - 1, n_row, CHUNKS)),
            dma((group, CHUNKS)),
            dma((2,)),
            dma((2,)),
            dma((3, n_side)),
            dma((3, n_side)),
            dma((2,)),
            dma((2,)),
            dma((group - 1,)),
            dma((group,)),
        ],
        compiler_params=pltpu.CompilerParams(
            collective_id=number, has_side_effects=True, vmem_limit_bytes=48 * 2**20
        ),
        cost_estimate=pl.CostEstimate(flops=2 * tokens * inner * width, bytes_accessed=2**22, transcendentals=0),
        name=f"sublayer_distance_{distance}",
    )(queries, keyvals, out_weight, gate_weight, class_table, labels, timesteps)


def solution(mesh):
    sizes = tuple(mesh.shape[name] for name in ("dp", "row", "col"))
    bit_count = sizes[0].bit_length() - 1

    def local(queries, keyvals, out_weight, gate_weight, class_table, labels, timesteps, round_index):
        branches = [functools.partial(layer, sizes, 2**power, power) for power in range(bit_count)]
        operands = (queries, keyvals, out_weight, gate_weight, class_table, labels, timesteps)
        result = lax.switch(round_index[0] % bit_count, branches, *operands)
        return result.reshape(queries.shape[:3] + (out_weight.shape[2],))

    placed = (
        P("dp", "row", "col", None),
        P("dp", None, "row", "col", None),
        P("dp", ("row", "col"), None),
        P("dp", ("row", "col"), None),
        P("dp", None, ("row", "col")),
        P("dp"),
        P("dp"),
        P(),
    )
    return jax.shard_map(
        local, mesh=mesh, in_specs=placed, out_specs=P("dp", "row", "col", None), check_vma=False
    )
```

```python
import functools
import math

import jax
import jax.numpy as jnp
from jax import lax
from jax.experimental import pallas as pl
from jax.experimental.pallas import tpu as pltpu
from jax.sharding import PartitionSpec as P

HDIM = 128
RADIUS = 3
CHUNKS = 8
GROUP = 6
MESH = pl.DeviceIdType.MESH
F32 = jnp.float32
BF16 = jnp.bfloat16


def remote(src, dst, send, recv, **where):
    return pltpu.make_async_remote_copy(
        src_ref=src, dst_ref=dst, send_sem=send, recv_sem=recv, device_id=where, device_id_type=MESH
    )


def kernel(
    sizes, distance,
    q_hbm, kv_hbm, o_hbm, g_hbm, t_hbm, label_ref, step_ref,
    out_hbm,
    q_buf, kv_buf, bias, att, o_own, o_peer, w_buf, out_buf, g_buf, t_buf,
    pack_out, pack_in, reply_out, reply_in, gates, gate_sum, mate_out,
    local_sem, out_sem, gossip_send, gossip_recv, w_send, w_side, w_recv, att_send, att_recv, mate_send, mate_recv,
    halo_send, halo_recv, side_send, side_recv, note_send, note_recv, gate_send, gate_recv,
):
    n_dp, n_row, n_col = sizes
    group = n_row * n_col
    tile_rows, tile_cols, inner = kv_hbm.shape[2:]
    shard, width = o_hbm.shape[1:]
    cut = width // CHUNKS
    span = t_hbm.shape[2]
    slot = pack_out.shape[1] // 3
    classes = t_hbm.shape[1]
    heads = inner // HDIM
    sides = [1] if n_col == 2 else [n_col - 1, 1]
    wide = kv_buf.shape[2]

    p, r, c = lax.axis_index("dp"), lax.axis_index("row"), lax.axis_index("col")
    me = r * n_col + c
    ahead, behind = lax.rem(p + distance, n_dp), lax.rem(p + n_dp - distance, n_dp)
    has_up, has_down = r > 0, r < n_row - 1
    is_outer = (r == 0) | (r == n_row - 1)
    is_inner = jnp.logical_not(is_outer)
    mate = r + 1 - 2 * lax.rem(r, 2)
    onward = 1 + lax.rem(r, 2)
    tokens = tile_rows * tile_cols

    def col_of(step):
        return lax.rem(c + step, n_col)

    loads = [
        pltpu.make_async_copy(t_hbm.at[0], t_buf, local_sem.at[0]),
        pltpu.make_async_copy(o_hbm.at[0], o_own, local_sem.at[1]),
        pltpu.make_async_copy(g_hbm.at[0], g_buf, local_sem.at[2]),
        pltpu.make_async_copy(q_hbm.at[0], q_buf, local_sem.at[3]),
        pltpu.make_async_copy(
            kv_hbm.at[0], kv_buf.at[:, pl.ds(RADIUS, tile_rows), pl.ds(0, tile_cols)], local_sem.at[4]
        ),
    ]
    for load in loads:
        load.start()

    barrier = pltpu.get_barrier_semaphore()
    for step in range(1, group):
        other = lax.rem(me + step, group)
        pl.semaphore_signal(
            barrier, inc=1, device_id={"row": other // n_col, "col": lax.rem(other, n_col)}, device_id_type=MESH
        )
    pl.semaphore_signal(barrier, inc=1, device_id={"dp": ahead}, device_id_type=MESH)
    greeted = group
    if (2 * distance) % n_dp:
        pl.semaphore_signal(barrier, inc=1, device_id={"dp": behind}, device_id_type=MESH)
        greeted += 1
    pl.semaphore_wait(barrier, greeted)

    def halo(which):
        first, place = ((0, tile_rows + RADIUS), (tile_rows - RADIUS, 0))[which]
        return remote(
            kv_hbm.at[0, :, pl.ds(first, RADIUS)],
            kv_buf.at[:, pl.ds(place, RADIUS), pl.ds(0, tile_cols)],
            halo_send.at[which], halo_recv.at[which], row=(r - 1, r + 1)[which],
        )

    def side(i):
        return remote(
            kv_hbm.at[0],
            kv_buf.at[:, pl.ds(RADIUS, tile_rows), pl.ds((i + 1) * tile_cols, tile_cols)],
            side_send.at[0, i], side_recv.at[0, i], col=col_of(sides[i]),
        )

    def corner(which, i):
        place = (tile_rows + RADIUS, 0)[which]
        rows = pl.ds(place, RADIUS)
        return remote(
            kv_buf.at[:, rows, pl.ds(0, tile_cols)],
            kv_buf.at[:, rows, pl.ds((i + 1) * tile_cols, tile_cols)],
            side_send.at[1 + which, i], side_recv.at[1 + which, i], col=col_of(sides[i]),
        )

    def gossip(k):
        columns = pl.ds(k * cut, cut) if isinstance(k, int) else pl.ds(pl.multiple_of(k * cut, cut), cut)
        return remote(o_hbm.at[0, :, columns], o_peer.at[k], gossip_send.at[k], gossip_recv.at[k], dp=ahead)

    gossip(0).start()
    pl.when(has_up)(lambda: halo(0).start())
    pl.when(has_down)(lambda: halo(1).start())
    for k in range(1, CHUNKS):
        gossip(k).start()
    for i in range(len(sides)):
        side(i).start()

    def class_row(label):
        rows = lax.broadcasted_iota(jnp.int32, (classes, span), 0).astype(F32)
        table = t_buf[...].astype(F32)
        return jnp.sum(jnp.where(rows == label, table, 0.0), axis=0, keepdims=True)

    loads[0].wait()
    label_here = jnp.full((1, span), label_ref[0], jnp.int32).astype(F32)
    pack_out[:, pl.ds(0, span)] = label_here
    pack_out[:, pl.ds(slot, span)] = jnp.full((1, span), step_ref[0], jnp.int32).astype(F32)
    pack_out[:, pl.ds(2 * slot, span)] = class_row(label_here)
    ask = remote(pack_out, pack_in, note_send.at[0], note_recv.at[0], dp=behind)
    ask.start()

    def w_copy(owner, k, sem, **where):
        rows = pl.ds(pl.multiple_of(owner * shard, shard), shard)
        place = w_buf.at[k, rows]
        return remote(place, place, sem, w_recv.at[owner, k], **where)

    def onward_copy(row, k):
        return w_copy(row * n_col + c, k, w_send.at[row, k], row=onward)

    def side_copy(row, k, step):
        return w_copy(row * n_col + c, k, w_side.at[step - 1, row, k], col=col_of(step))

    def spread(row, k):
        for step in range(1, n_col):
            side_copy(row, k, step).start()

    def own_chunk(k):
        gossip(k).wait_recv()
        columns = pl.ds(pl.multiple_of(k * cut, cut), cut)
        both = o_own[:, columns].astype(F32) + o_peer[k].astype(F32)
        w_buf[k, pl.ds(pl.multiple_of(me * shard, shard), shard), :] = (0.5 * both).astype(BF16)
        onward_copy(r, k).start()
        pl.when(is_inner)(lambda: spread(r, k))

    def hand_on(row, k):
        onward_copy(row, k).wait_recv()
        spread(row, k)

    def mate_chunk(k):
        @pl.when(is_inner)
        def _():
            onward_copy(mate, k).wait_recv()
            onward_copy(mate, k).start()
            spread(mate, k)

    loads[1].wait()
    own_chunk(0)

    def against_gate(cond):
        tall = jnp.broadcast_to(cond, (16, span)).astype(BF16)
        return jnp.dot(tall, g_buf[...], preferred_element_type=F32)[0:1]

    half = width // 2
    position = me * span + lax.broadcasted_iota(jnp.int32, (1, span), 1)
    freq_index = jnp.where(position < half, position, position - half).astype(F32)
    frequency = jnp.exp(-math.log(10000.0) * freq_index / half)
    ask.wait_recv()
    mixed_row = 0.5 * (pack_in[:, pl.ds(2 * slot, span)] + class_row(pack_in[:, pl.ds(0, span)]))
    angle = pack_in[:, pl.ds(slot, span)] * frequency
    embed = jnp.where(position < half, jnp.cos(angle), jnp.sin(angle))
    value = mixed_row.astype(BF16).astype(F32) + embed
    cond = (value / (1.0 + jnp.exp(-value))).astype(BF16).astype(F32)
    loads[2].wait()
    reply_out[:, pl.ds(0, width)] = against_gate(cond)
    reply_out[:, pl.ds(width, span)] = cond
    answer = remote(reply_out, reply_in, note_send.at[1], note_recv.at[1], dp=ahead)
    answer.start()

    own_chunk(1)

    edge = jnp.zeros((2, RADIUS, wide, inner), BF16)

    @pl.when(jnp.logical_not(has_up))
    def _():
        kv_buf[:, pl.ds(0, RADIUS)] = edge

    @pl.when(jnp.logical_not(has_down))
    def _():
        kv_buf[:, pl.ds(tile_rows + RADIUS, RADIUS)] = edge

    n_q, n_k = GROUP * tile_cols, (GROUP + 2 * RADIUS) * wide
    blocks = wide // tile_cols
    q_index = lax.broadcasted_iota(jnp.int32, (n_q, n_k), 0)
    k_index = lax.broadcasted_iota(jnp.int32, (n_q, n_k), 1)
    q_row, q_col = q_index // tile_cols, lax.rem(q_index, tile_cols)
    k_block = k_index // tile_cols
    k_row = (k_block * -(-512 // blocks)) // 512
    k_block = k_block - k_row * blocks
    k_col = lax.rem(k_index, tile_cols)
    if n_col == 2:
        k_shift = jnp.where(k_block == 1, 1 - 2 * c, 0)
    else:
        k_shift = jnp.where(k_block == 1, 1, jnp.where(k_block == 2, -1, 0))
    k_col = k_col + k_shift * tile_cols
    near = (jnp.abs(k_col - q_col) <= RADIUS) & (k_row >= q_row) & (k_row <= q_row + 2 * RADIUS)
    k_col = k_col + c * tile_cols
    near = near & (k_col >= 0) & (k_col < n_col * tile_cols)
    for g in range(tile_rows // GROUP):
        row_here = k_row + (r * tile_rows + g * GROUP - RADIUS)
        seen = near & (row_here >= 0) & (row_here < n_row * tile_rows)
        bias[g] = jnp.where(seen, 0.0, -1e30)

    @pl.when(has_down)
    def _():
        halo(0).wait_recv()
        for i in range(len(sides)):
            corner(0, i).start()

    @pl.when(has_up)
    def _():
        halo(1).wait_recv()
        for i in range(len(sides)):
            corner(1, i).start()

    own_chunk(2)
    mate_chunk(0)
    mate_chunk(1)

    answer.wait_recv()
    share = 0.5 * (reply_in[:, pl.ds(0, width)] + against_gate(reply_in[:, pl.ds(width, span)]))
    gates[me] = share

    def gate_copy(owner, step):
        other = lax.rem(me + step, group)
        return remote(
            gates.at[owner], gates.at[owner], gate_send.at[step - 1], gate_recv.at[owner],
            row=other // n_col, col=lax.rem(other, n_col),
        )

    for step in range(1, group):
        gate_copy(me, step).start()

    own_chunk(3)
    mate_chunk(2)

    loads[3].wait()
    loads[4].wait()
    for i in range(len(sides)):
        side(i).wait_recv()
        pl.when(has_down)(lambda i=i: corner(0, i).wait_recv())
        pl.when(has_up)(lambda i=i: corner(1, i).wait_recv())

    scale = 1.0 / math.sqrt(HDIM)

    def attend(head):
        lanes = pl.ds(pl.multiple_of(head * HDIM, HDIM), HDIM)
        for g in range(tile_rows // GROUP):
            rows = pl.ds(g * GROUP, GROUP)
            near_rows = pl.ds(g * GROUP, GROUP + 2 * RADIUS)
            query = q_buf[rows, :, lanes].reshape(n_q, HDIM)
            key = kv_buf[0, near_rows, :, lanes].reshape(n_k, HDIM)
            val = kv_buf[1, near_rows, :, lanes].reshape(n_k, HDIM)
            score = lax.dot_general(query, key, (((1,), (1,)), ((), ())), preferred_element_type=F32)
            score = score + bias[g]
            top = jnp.max(score, axis=1, keepdims=True)
            weight = jnp.exp((score - top) * scale)
            total = jnp.sum(weight, axis=1, keepdims=True)
            mean = jnp.dot(weight.astype(BF16), val, preferred_element_type=F32) / total
            att[pl.ds(g * n_q, n_q), lanes] = mean.astype(BF16)

    pairs = heads // 2

    def att_copy(j):
        lanes = pl.ds(pl.multiple_of(j * 2 * HDIM, 2 * HDIM), 2 * HDIM)
        return remote(
            att.at[pl.ds(0, tokens), lanes], att.at[pl.ds(tokens, tokens), lanes],
            att_send.at[j], att_recv.at[j], row=mate,
        )

    def attend_pair(j, carry):
        @pl.when(j + 4 < CHUNKS)
        def _():
            own_chunk(j + 4)
            mate_chunk(j + 3)

        attend(2 * j)
        attend(2 * j + 1)
        pl.when(is_outer)(lambda: att_copy(j).start())
        return carry

    lax.fori_loop(0, pairs, attend_pair, 0)
    mate_chunk(CHUNKS - 1)

    for step in range(1, group):
        owner = lax.rem(me + step, group)
        gate_copy(owner, step).wait_recv()
    gate = gates[0]
    for i in range(1, group):
        gate = gate + gates[i]
    for k in range(CHUNKS):
        gate_sum[k] = gate[:, k * cut : (k + 1) * cut]

    def out_copy(k):
        return pltpu.make_async_copy(
            out_buf.at[k], out_hbm.at[:, pl.ds(pl.multiple_of(k * cut, cut), cut)], out_sem.at[k]
        )

    def mate_copy(k):
        return remote(
            mate_out.at[k], out_hbm.at[:, pl.ds(pl.multiple_of(k * cut, cut), cut)],
            mate_send.at[k], mate_recv.at[k], row=mate,
        )

    def project(k, carry):
        hand_on(n_row - 1 - r, k)
        hand_on(n_row - 1 - mate, k)
        for row in range(n_row):
            for step in range(1, n_col):
                owner = row * n_col + col_of(step)
                w_copy(owner, k, w_side.at[step - 1, row, k], col=col_of(step)).wait_recv()
        product = jnp.dot(att[...], w_buf[k], preferred_element_type=F32)
        product = (gate_sum[k] * product).astype(BF16)
        mate_out[k] = product[tokens:]
        mate_copy(k).start()
        out_buf[k] = product[:tokens]
        out_copy(k).start()
        return carry

    @pl.when(is_inner)
    def _():
        for j in range(pairs):
            att_copy(j).wait_recv()
        lax.fori_loop(0, CHUNKS, project, 0)

    @pl.when(is_outer)
    def _():
        for k in range(CHUNKS):
            mate_copy(k).wait_recv()

    def sent(k, carry):
        gossip(k).wait_send()
        onward_copy(r, k).wait_send()

        @pl.when(is_inner)
        def _():
            out_copy(k).wait()
            mate_copy(k).wait_send()
            onward_copy(mate, k).wait_send()
            for row in range(n_row):
                for step in range(1, n_col):
                    side_copy(row, k, step).wait_send()

        return carry

    lax.fori_loop(0, CHUNKS, sent, 0)

    @pl.when(is_outer)
    def _():
        for j in range(pairs):
            att_copy(j).wait_send()

    pl.when(has_up)(lambda: halo(0).wait_send())
    pl.when(has_down)(lambda: halo(1).wait_send())
    for i in range(len(sides)):
        side(i).wait_send()
        pl.when(has_down)(lambda i=i: corner(0, i).wait_send())
        pl.when(has_up)(lambda i=i: corner(1, i).wait_send())
    ask.wait_send()
    answer.wait_send()
    for step in range(1, group):
        gate_copy(me, step).wait_send()


def layer(sizes, distance, number, queries, keyvals, out_weight, gate_weight, class_table, labels, timesteps):
    n_dp, n_row, n_col = sizes
    group = n_row * n_col
    _, tile_rows, tile_cols, inner = queries.shape
    _, shard, width = out_weight.shape
    span = gate_weight.shape[1]
    classes = class_table.shape[1]
    cut = width // CHUNKS
    slot = max(span, 128)
    n_side = 1 if n_col == 2 else 2
    wide = tile_cols * (1 + n_side)
    tokens = tile_rows * tile_cols
    n_q, n_k = GROUP * tile_cols, (GROUP + 2 * RADIUS) * wide
    dma = pltpu.SemaphoreType.DMA
    return pl.pallas_call(
        functools.partial(kernel, sizes, distance),
        out_shape=jax.ShapeDtypeStruct((tokens, width), BF16),
        in_specs=[pl.BlockSpec(memory_space=pl.ANY)] * 5 + [pl.BlockSpec(memory_space=pltpu.SMEM)] * 2,
        out_specs=pl.BlockSpec(memory_space=pl.ANY),
        scratch_shapes=[
            pltpu.VMEM((tile_rows, tile_cols, inner), BF16),
            pltpu.VMEM((2, tile_rows + 2 * RADIUS, wide, inner), BF16),
            pltpu.VMEM((tile_rows // GROUP, n_q, n_k), F32),
            pltpu.VMEM((2 * tokens, inner), BF16),
            pltpu.VMEM((shard, width), BF16),
            pltpu.VMEM((CHUNKS, shard, cut), BF16),
            pltpu.VMEM((CHUNKS, group * shard, cut), BF16),
            pltpu.VMEM((CHUNKS, tokens, cut), BF16),
            pltpu.VMEM((span, width), BF16),
            pltpu.VMEM((classes, span), BF16),
            pltpu.VMEM((1, 3 * slot), F32),
            pltpu.VMEM((1, 3 * slot), F32),
            pltpu.VMEM((1, width + slot), F32),
            pltpu.VMEM((1, width + slot), F32),
            pltpu.VMEM((group, 1, width), F32),
            pltpu.VMEM((CHUNKS, 1, cut), F32),
            pltpu.VMEM((CHUNKS, tokens, cut), BF16),
            dma((5,)),
            dma((CHUNKS,)),
            dma((CHUNKS,)),
            dma((CHUNKS,)),
            dma((n_row, CHUNKS)),
            dma((n_col - 1, n_row, CHUNKS)),
            dma((group, CHUNKS)),
            dma((inner // HDIM // 2,)),
            dma((inner // HDIM // 2,)),
            dma((CHUNKS,)),
            dma((CHUNKS,)),
            dma((2,)),
            dma((2,)),
            dma((3, n_side)),
            dma((3, n_side)),
            dma((2,)),
            dma((2,)),
            dma((group - 1,)),
            dma((group,)),
        ],
        compiler_params=pltpu.CompilerParams(
            collective_id=number, has_side_effects=True, vmem_limit_bytes=48 * 2**20
        ),
        cost_estimate=pl.CostEstimate(flops=2 * tokens * inner * width, bytes_accessed=2**22, transcendentals=0),
        name=f"sublayer_distance_{distance}",
    )(queries, keyvals, out_weight, gate_weight, class_table, labels, timesteps)


def solution(mesh):
    sizes = tuple(mesh.shape[name] for name in ("dp", "row", "col"))
    bit_count = sizes[0].bit_length() - 1

    def local(queries, keyvals, out_weight, gate_weight, class_table, labels, timesteps, round_index):
        branches = [functools.partial(layer, sizes, 2**power, power) for power in range(bit_count)]
        operands = (queries, keyvals, out_weight, gate_weight, class_table, labels, timesteps)
        result = lax.switch(round_index[0] % bit_count, branches, *operands)
        return result.reshape(queries.shape[:3] + (out_weight.shape[2],))

    placed = (
        P("dp", "row", "col", None),
        P("dp", None, "row", "col", None),
        P("dp", ("row", "col"), None),
        P("dp", ("row", "col"), None),
        P("dp", None, ("row", "col")),
        P("dp"),
        P("dp"),
        P(),
    )
    return jax.shard_map(
        local, mesh=mesh, in_specs=placed, out_specs=P("dp", "row", "col", None), check_vma=False
    )
```

```python
import functools
import math

import jax
import jax.numpy as jnp
from jax import lax
from jax.experimental import pallas as pl
from jax.experimental.pallas import tpu as pltpu
from jax.sharding import PartitionSpec as P

HDIM = 128
RADIUS = 3
CHUNKS = 8
AHEAD = 2
GROUP = 6
MESH = pl.DeviceIdType.MESH
F32 = jnp.float32
BF16 = jnp.bfloat16


def remote(src, dst, send, recv, **where):
    return pltpu.make_async_remote_copy(
        src_ref=src, dst_ref=dst, send_sem=send, recv_sem=recv, device_id=where, device_id_type=MESH
    )


def kernel(
    sizes, distance,
    q_hbm, kv_hbm, o_hbm, g_hbm, t_hbm, label_ref, step_ref,
    out_hbm,
    q_buf, kv_buf, bias, att, o_own, o_peer, w_buf, out_buf, g_buf, t_buf,
    pack_out, pack_in, reply_out, reply_in, gates, gate_sum, mate_out,
    local_sem, out_sem, gossip_send, gossip_recv, w_send, w_side, w_recv, att_send, att_recv, mate_send, mate_recv,
    halo_send, halo_recv, side_send, side_recv, note_send, note_recv, gate_send, gate_recv,
):
    n_dp, n_row, n_col = sizes
    group = n_row * n_col
    tile_rows, tile_cols, inner = kv_hbm.shape[2:]
    shard, width = o_hbm.shape[1:]
    cut = width // CHUNKS
    span = t_hbm.shape[2]
    slot = pack_out.shape[1] // 3
    classes = t_hbm.shape[1]
    heads = inner // HDIM
    sides = [1] if n_col == 2 else [n_col - 1, 1]
    wide = kv_buf.shape[2]

    p, r, c = lax.axis_index("dp"), lax.axis_index("row"), lax.axis_index("col")
    me = r * n_col + c
    ahead, behind = lax.rem(p + distance, n_dp), lax.rem(p + n_dp - distance, n_dp)
    has_up, has_down = r > 0, r < n_row - 1
    is_outer = (r == 0) | (r == n_row - 1)
    is_inner = jnp.logical_not(is_outer)
    mate = r + 1 - 2 * lax.rem(r, 2)
    onward = 1 + lax.rem(r, 2)
    tokens = tile_rows * tile_cols

    def col_of(step):
        return lax.rem(c + step, n_col)

    loads = [
        pltpu.make_async_copy(t_hbm.at[0], t_buf, local_sem.at[0]),
        pltpu.make_async_copy(o_hbm.at[0], o_own, local_sem.at[1]),
        pltpu.make_async_copy(g_hbm.at[0], g_buf, local_sem.at[2]),
        pltpu.make_async_copy(q_hbm.at[0], q_buf, local_sem.at[3]),
        pltpu.make_async_copy(
            kv_hbm.at[0], kv_buf.at[:, pl.ds(RADIUS, tile_rows), pl.ds(0, tile_cols)], local_sem.at[4]
        ),
    ]
    for load in loads:
        load.start()

    barrier = pltpu.get_barrier_semaphore()
    for step in range(1, group):
        other = lax.rem(me + step, group)
        pl.semaphore_signal(
            barrier, inc=1, device_id={"row": other // n_col, "col": lax.rem(other, n_col)}, device_id_type=MESH
        )
    pl.semaphore_signal(barrier, inc=1, device_id={"dp": ahead}, device_id_type=MESH)
    greeted = group
    if (2 * distance) % n_dp:
        pl.semaphore_signal(barrier, inc=1, device_id={"dp": behind}, device_id_type=MESH)
        greeted += 1
    def class_row(label):
        rows = lax.broadcasted_iota(jnp.int32, (classes, span), 0).astype(F32)
        table = t_buf[...].astype(F32)
        return jnp.sum(jnp.where(rows == label, table, 0.0), axis=0, keepdims=True)

    loads[0].wait()
    label_here = jnp.full((1, span), label_ref[0], jnp.int32).astype(F32)
    pack_out[:, pl.ds(0, span)] = label_here
    pack_out[:, pl.ds(slot, span)] = jnp.full((1, span), step_ref[0], jnp.int32).astype(F32)
    pack_out[:, pl.ds(2 * slot, span)] = class_row(label_here)
    pl.semaphore_wait(barrier, greeted)

    def halo(which):
        first, place = ((0, tile_rows + RADIUS), (tile_rows - RADIUS, 0))[which]
        return remote(
            kv_hbm.at[0, :, pl.ds(first, RADIUS)],
            kv_buf.at[:, pl.ds(place, RADIUS), pl.ds(0, tile_cols)],
            halo_send.at[which], halo_recv.at[which], row=(r - 1, r + 1)[which],
        )

    def side(i):
        return remote(
            kv_hbm.at[0],
            kv_buf.at[:, pl.ds(RADIUS, tile_rows), pl.ds((i + 1) * tile_cols, tile_cols)],
            side_send.at[0, i], side_recv.at[0, i], col=col_of(sides[i]),
        )

    def corner(which, i):
        place = (tile_rows + RADIUS, 0)[which]
        rows = pl.ds(place, RADIUS)
        return remote(
            kv_buf.at[:, rows, pl.ds(0, tile_cols)],
            kv_buf.at[:, rows, pl.ds((i + 1) * tile_cols, tile_cols)],
            side_send.at[1 + which, i], side_recv.at[1 + which, i], col=col_of(sides[i]),
        )

    def gossip(k):
        columns = pl.ds(k * cut, cut) if isinstance(k, int) else pl.ds(pl.multiple_of(k * cut, cut), cut)
        return remote(o_hbm.at[0, :, columns], o_peer.at[k], gossip_send.at[k], gossip_recv.at[k], dp=ahead)

    ask = remote(pack_out, pack_in, note_send.at[0], note_recv.at[0], dp=behind)
    ask.start()
    for k in range(AHEAD):
        gossip(k).start()
    pl.when(has_up)(lambda: halo(0).start())
    pl.when(has_down)(lambda: halo(1).start())
    for i in range(len(sides)):
        side(i).start()

    edge = jnp.zeros((2, RADIUS, wide, inner), BF16)

    @pl.when(jnp.logical_not(has_up))
    def _():
        kv_buf[:, pl.ds(0, RADIUS)] = edge

    @pl.when(jnp.logical_not(has_down))
    def _():
        kv_buf[:, pl.ds(tile_rows + RADIUS, RADIUS)] = edge

    n_q, n_k = GROUP * tile_cols, (GROUP + 2 * RADIUS) * wide
    blocks = wide // tile_cols
    q_index = lax.broadcasted_iota(jnp.int32, (n_q, n_k), 0)
    k_index = lax.broadcasted_iota(jnp.int32, (n_q, n_k), 1)
    q_row, q_col = q_index // tile_cols, lax.rem(q_index, tile_cols)
    k_block = k_index // tile_cols
    k_row = (k_block * -(-512 // blocks)) // 512
    k_block = k_block - k_row * blocks
    k_col = lax.rem(k_index, tile_cols)
    if n_col == 2:
        k_shift = jnp.where(k_block == 1, 1 - 2 * c, 0)
    else:
        k_shift = jnp.where(k_block == 1, 1, jnp.where(k_block == 2, -1, 0))
    k_col = k_col + k_shift * tile_cols
    near = (jnp.abs(k_col - q_col) <= RADIUS) & (k_row >= q_row) & (k_row <= q_row + 2 * RADIUS)
    k_col = k_col + c * tile_cols
    near = near & (k_col >= 0) & (k_col < n_col * tile_cols)
    for g in range(tile_rows // GROUP):
        row_here = k_row + (r * tile_rows + g * GROUP - RADIUS)
        seen = near & (row_here >= 0) & (row_here < n_row * tile_rows)
        bias[g] = jnp.where(seen, 0.0, -1e30)

    def w_copy(owner, k, sem, **where):
        rows = pl.ds(pl.multiple_of(owner * shard, shard), shard)
        place = w_buf.at[k, rows]
        return remote(place, place, sem, w_recv.at[owner, k], **where)

    def onward_copy(row, k):
        return w_copy(row * n_col + c, k, w_send.at[row, k], row=onward)

    def side_copy(row, k, step):
        return w_copy(row * n_col + c, k, w_side.at[step - 1, row, k], col=col_of(step))

    def spread(row, k):
        for step in range(1, n_col):
            side_copy(row, k, step).start()

    def own_chunk(k):
        gossip(k).wait_recv()
        gossip(k).wait_send()

        @pl.when(k + AHEAD < CHUNKS)
        def _():
            gossip(k + AHEAD).start()

        columns = pl.ds(pl.multiple_of(k * cut, cut), cut)
        both = o_own[:, columns].astype(F32) + o_peer[k].astype(F32)
        w_buf[k, pl.ds(pl.multiple_of(me * shard, shard), shard), :] = (0.5 * both).astype(BF16)
        onward_copy(r, k).start()
        pl.when(is_inner)(lambda: spread(r, k))

    def hand_on(row, k):
        onward_copy(row, k).wait_recv()
        spread(row, k)

    def mate_chunk(k):
        @pl.when(is_inner)
        def _():
            onward_copy(mate, k).wait_recv()
            onward_copy(mate, k).start()
            spread(mate, k)

    loads[1].wait()
    own_chunk(0)

    own_chunk(1)
    mate_chunk(0)

    @pl.when(has_down)
    def _():
        halo(0).wait_recv()
        for i in range(len(sides)):
            corner(0, i).start()

    @pl.when(has_up)
    def _():
        halo(1).wait_recv()
        for i in range(len(sides)):
            corner(1, i).start()

    def against_gate(cond):
        tall = jnp.broadcast_to(cond, (16, span)).astype(BF16)
        return jnp.dot(tall, g_buf[...], preferred_element_type=F32)[0:1]

    half = width // 2
    position = me * span + lax.broadcasted_iota(jnp.int32, (1, span), 1)
    freq_index = jnp.where(position < half, position, position - half).astype(F32)
    frequency = jnp.exp(-math.log(10000.0) * freq_index / half)
    ask.wait_recv()
    mixed_row = 0.5 * (pack_in[:, pl.ds(2 * slot, span)] + class_row(pack_in[:, pl.ds(0, span)]))
    angle = pack_in[:, pl.ds(slot, span)] * frequency
    embed = jnp.where(position < half, jnp.cos(angle), jnp.sin(angle))
    value = mixed_row.astype(BF16).astype(F32) + embed
    cond = (value / (1.0 + jnp.exp(-value))).astype(BF16).astype(F32)
    loads[2].wait()
    reply_out[:, pl.ds(0, width)] = against_gate(cond)
    reply_out[:, pl.ds(width, span)] = cond
    answer = remote(reply_out, reply_in, note_send.at[1], note_recv.at[1], dp=ahead)
    answer.start()


    own_chunk(2)
    mate_chunk(1)

    answer.wait_recv()
    share = 0.5 * (reply_in[:, pl.ds(0, width)] + against_gate(reply_in[:, pl.ds(width, span)]))
    gates[me] = share

    def gate_copy(owner, step):
        other = lax.rem(me + step, group)
        return remote(
            gates.at[owner], gates.at[owner], gate_send.at[step - 1], gate_recv.at[owner],
            row=other // n_col, col=lax.rem(other, n_col),
        )

    for step in range(1, group):
        gate_copy(me, step).start()

    own_chunk(3)
    mate_chunk(2)

    loads[3].wait()
    loads[4].wait()
    for i in range(len(sides)):
        side(i).wait_recv()
        pl.when(has_down)(lambda i=i: corner(0, i).wait_recv())
        pl.when(has_up)(lambda i=i: corner(1, i).wait_recv())

    scale = 1.0 / math.sqrt(HDIM)

    def attend(head):
        lanes = pl.ds(pl.multiple_of(head * HDIM, HDIM), HDIM)
        for g in range(tile_rows // GROUP):
            rows = pl.ds(g * GROUP, GROUP)
            near_rows = pl.ds(g * GROUP, GROUP + 2 * RADIUS)
            query = q_buf[rows, :, lanes].reshape(n_q, HDIM)
            key = kv_buf[0, near_rows, :, lanes].reshape(n_k, HDIM)
            val = kv_buf[1, near_rows, :, lanes].reshape(n_k, HDIM)
            score = lax.dot_general(query, key, (((1,), (1,)), ((), ())), preferred_element_type=F32)
            score = score + bias[g]
            top = jnp.max(score, axis=1, keepdims=True)
            weight = jnp.exp((score - top) * scale)
            total = jnp.sum(weight, axis=1, keepdims=True)
            mean = jnp.dot(weight.astype(BF16), val, preferred_element_type=F32) / total
            att[pl.ds(g * n_q, n_q), lanes] = mean.astype(BF16)

    pairs = heads // 2

    def other_half(k):
        @pl.when(is_inner)
        def _():
            hand_on(n_row - 1 - r, k)
            hand_on(n_row - 1 - mate, k)

    def att_copy(j):
        lanes = pl.ds(pl.multiple_of(j * 2 * HDIM, 2 * HDIM), 2 * HDIM)
        return remote(
            att.at[pl.ds(0, tokens), lanes], att.at[pl.ds(tokens, tokens), lanes],
            att_send.at[j], att_recv.at[j], row=mate,
        )

    def attend_pair(j, carry):
        @pl.when(j + 4 < CHUNKS)
        def _():
            own_chunk(j + 4)
            mate_chunk(j + 3)

        pl.when(j > 0)(lambda: other_half(j - 1))
        attend(2 * j)
        attend(2 * j + 1)
        pl.when(is_outer)(lambda: att_copy(j).start())
        return carry

    lax.fori_loop(0, pairs, attend_pair, 0)
    mate_chunk(CHUNKS - 1)
    other_half(pairs - 1)

    for step in range(1, group):
        owner = lax.rem(me + step, group)
        gate_copy(owner, step).wait_recv()
    gate = gates[0]
    for i in range(1, group):
        gate = gate + gates[i]
    for k in range(CHUNKS):
        gate_sum[k] = gate[:, k * cut : (k + 1) * cut]

    def out_copy(k):
        return pltpu.make_async_copy(
            out_buf.at[k], out_hbm.at[:, pl.ds(pl.multiple_of(k * cut, cut), cut)], out_sem.at[k]
        )

    def mate_copy(k):
        return remote(
            mate_out.at[k], out_hbm.at[:, pl.ds(pl.multiple_of(k * cut, cut), cut)],
            mate_send.at[k], mate_recv.at[k], row=mate,
        )

    def project(k, carry):
        pl.when((k + 1 >= pairs) & (k + 1 < CHUNKS))(lambda: other_half(k + 1))
        for row in range(n_row):
            for step in range(1, n_col):
                owner = row * n_col + col_of(step)
                w_copy(owner, k, w_side.at[step - 1, row, k], col=col_of(step)).wait_recv()
        product = jnp.dot(att[...], w_buf[k], preferred_element_type=F32)
        product = (gate_sum[k] * product).astype(BF16)
        mate_out[k] = product[tokens:]
        mate_copy(k).start()
        out_buf[k] = product[:tokens]
        out_copy(k).start()
        return carry

    @pl.when(is_inner)
    def _():
        for j in range(pairs):
            att_copy(j).wait_recv()
        lax.fori_loop(0, CHUNKS, project, 0)

    @pl.when(is_outer)
    def _():
        for k in range(CHUNKS):
            mate_copy(k).wait_recv()

    def sent(k, carry):
        onward_copy(r, k).wait_send()

        @pl.when(is_inner)
        def _():
            out_copy(k).wait()
            mate_copy(k).wait_send()
            onward_copy(mate, k).wait_send()
            for row in range(n_row):
                for step in range(1, n_col):
                    side_copy(row, k, step).wait_send()

        return carry

    lax.fori_loop(0, CHUNKS, sent, 0)

    @pl.when(is_outer)
    def _():
        for j in range(pairs):
            att_copy(j).wait_send()

    pl.when(has_up)(lambda: halo(0).wait_send())
    pl.when(has_down)(lambda: halo(1).wait_send())
    for i in range(len(sides)):
        side(i).wait_send()
        pl.when(has_down)(lambda i=i: corner(0, i).wait_send())
        pl.when(has_up)(lambda i=i: corner(1, i).wait_send())
    ask.wait_send()
    answer.wait_send()
    for step in range(1, group):
        gate_copy(me, step).wait_send()


def layer(sizes, distance, number, queries, keyvals, out_weight, gate_weight, class_table, labels, timesteps):
    n_dp, n_row, n_col = sizes
    group = n_row * n_col
    _, tile_rows, tile_cols, inner = queries.shape
    _, shard, width = out_weight.shape
    span = gate_weight.shape[1]
    classes = class_table.shape[1]
    cut = width // CHUNKS
    slot = max(span, 128)
    n_side = 1 if n_col == 2 else 2
    wide = tile_cols * (1 + n_side)
    tokens = tile_rows * tile_cols
    n_q, n_k = GROUP * tile_cols, (GROUP + 2 * RADIUS) * wide
    dma = pltpu.SemaphoreType.DMA
    return pl.pallas_call(
        functools.partial(kernel, sizes, distance),
        out_shape=jax.ShapeDtypeStruct((tokens, width), BF16),
        in_specs=[pl.BlockSpec(memory_space=pl.ANY)] * 5 + [pl.BlockSpec(memory_space=pltpu.SMEM)] * 2,
        out_specs=pl.BlockSpec(memory_space=pl.ANY),
        scratch_shapes=[
            pltpu.VMEM((tile_rows, tile_cols, inner), BF16),
            pltpu.VMEM((2, tile_rows + 2 * RADIUS, wide, inner), BF16),
            pltpu.VMEM((tile_rows // GROUP, n_q, n_k), F32),
            pltpu.VMEM((2 * tokens, inner), BF16),
            pltpu.VMEM((shard, width), BF16),
            pltpu.VMEM((CHUNKS, shard, cut), BF16),
            pltpu.VMEM((CHUNKS, group * shard, cut), BF16),
            pltpu.VMEM((CHUNKS, tokens, cut), BF16),
            pltpu.VMEM((span, width), BF16),
            pltpu.VMEM((classes, span), BF16),
            pltpu.VMEM((1, 3 * slot), F32),
            pltpu.VMEM((1, 3 * slot), F32),
            pltpu.VMEM((1, width + slot), F32),
            pltpu.VMEM((1, width + slot), F32),
            pltpu.VMEM((group, 1, width), F32),
            pltpu.VMEM((CHUNKS, 1, cut), F32),
            pltpu.VMEM((CHUNKS, tokens, cut), BF16),
            dma((5,)),
            dma((CHUNKS,)),
            dma((CHUNKS,)),
            dma((CHUNKS,)),
            dma((n_row, CHUNKS)),
            dma((n_col - 1, n_row, CHUNKS)),
            dma((group, CHUNKS)),
            dma((inner // HDIM // 2,)),
            dma((inner // HDIM // 2,)),
            dma((CHUNKS,)),
            dma((CHUNKS,)),
            dma((2,)),
            dma((2,)),
            dma((3, n_side)),
            dma((3, n_side)),
            dma((2,)),
            dma((2,)),
            dma((group - 1,)),
            dma((group,)),
        ],
        compiler_params=pltpu.CompilerParams(
            collective_id=number, has_side_effects=True, vmem_limit_bytes=48 * 2**20
        ),
        cost_estimate=pl.CostEstimate(flops=2 * tokens * inner * width, bytes_accessed=2**22, transcendentals=0),
        name=f"sublayer_distance_{distance}",
    )(queries, keyvals, out_weight, gate_weight, class_table, labels, timesteps)


def solution(mesh):
    sizes = tuple(mesh.shape[name] for name in ("dp", "row", "col"))
    bit_count = sizes[0].bit_length() - 1

    def local(queries, keyvals, out_weight, gate_weight, class_table, labels, timesteps, round_index):
        branches = [functools.partial(layer, sizes, 2**power, power) for power in range(bit_count)]
        operands = (queries, keyvals, out_weight, gate_weight, class_table, labels, timesteps)
        result = lax.switch(round_index[0] % bit_count, branches, *operands)
        return result.reshape(queries.shape[:3] + (out_weight.shape[2],))

    placed = (
        P("dp", "row", "col", None),
        P("dp", None, "row", "col", None),
        P("dp", ("row", "col"), None),
        P("dp", ("row", "col"), None),
        P("dp", None, ("row", "col")),
        P("dp"),
        P("dp"),
        P(),
    )
    return jax.shard_map(
        local, mesh=mesh, in_specs=placed, out_specs=P("dp", "row", "col", None), check_vma=False
    )
```

```python
import functools
import math

import jax
import jax.numpy as jnp
from jax import lax
from jax.experimental import pallas as pl
from jax.experimental.pallas import tpu as pltpu
from jax.sharding import PartitionSpec as P

HDIM = 128
RADIUS = 3
CHUNKS = 8
AHEAD = 2
OUTER = 2
GROUP = 6
MESH = pl.DeviceIdType.MESH
F32 = jnp.float32
BF16 = jnp.bfloat16


def remote(src, dst, send, recv, **where):
    return pltpu.make_async_remote_copy(
        src_ref=src, dst_ref=dst, send_sem=send, recv_sem=recv, device_id=where, device_id_type=MESH
    )


def kernel(
    sizes, distance,
    q_hbm, kv_hbm, o_hbm, g_hbm, t_hbm, label_ref, step_ref,
    out_hbm,
    q_buf, kv_buf, bias, att, o_own, o_peer, w_buf, out_buf, g_buf, t_buf,
    pack_out, pack_in, reply_out, reply_in, gates, gate_sum, mate_out,
    local_sem, out_sem, gossip_send, gossip_recv, w_send, w_back, w_side, w_recv, att_send, att_recv, mate_send, mate_recv,
    halo_send, halo_recv, side_send, side_recv, note_send, note_recv, gate_send, gate_recv,
):
    n_dp, n_row, n_col = sizes
    group = n_row * n_col
    tile_rows, tile_cols, inner = kv_hbm.shape[2:]
    shard, width = o_hbm.shape[1:]
    cut = width // CHUNKS
    span = t_hbm.shape[2]
    slot = pack_out.shape[1] // 3
    classes = t_hbm.shape[1]
    heads = inner // HDIM
    sides = [1] if n_col == 2 else [n_col - 1, 1]
    wide = kv_buf.shape[2]

    p, r, c = lax.axis_index("dp"), lax.axis_index("row"), lax.axis_index("col")
    me = r * n_col + c
    ahead, behind = lax.rem(p + distance, n_dp), lax.rem(p + n_dp - distance, n_dp)
    has_up, has_down = r > 0, r < n_row - 1
    is_outer = (r == 0) | (r == n_row - 1)
    is_inner = jnp.logical_not(is_outer)
    mate = r + 1 - 2 * lax.rem(r, 2)
    onward = 1 + lax.rem(r, 2)
    tokens = tile_rows * tile_cols

    def col_of(step):
        return lax.rem(c + step, n_col)

    loads = [
        pltpu.make_async_copy(t_hbm.at[0], t_buf, local_sem.at[0]),
        pltpu.make_async_copy(o_hbm.at[0], o_own, local_sem.at[1]),
        pltpu.make_async_copy(g_hbm.at[0], g_buf, local_sem.at[2]),
        pltpu.make_async_copy(q_hbm.at[0], q_buf, local_sem.at[3]),
        pltpu.make_async_copy(
            kv_hbm.at[0], kv_buf.at[:, pl.ds(RADIUS, tile_rows), pl.ds(0, tile_cols)], local_sem.at[4]
        ),
    ]
    for load in loads:
        load.start()

    barrier = pltpu.get_barrier_semaphore()
    for step in range(1, group):
        other = lax.rem(me + step, group)
        pl.semaphore_signal(
            barrier, inc=1, device_id={"row": other // n_col, "col": lax.rem(other, n_col)}, device_id_type=MESH
        )
    pl.semaphore_signal(barrier, inc=1, device_id={"dp": ahead}, device_id_type=MESH)
    greeted = group
    if (2 * distance) % n_dp:
        pl.semaphore_signal(barrier, inc=1, device_id={"dp": behind}, device_id_type=MESH)
        greeted += 1
    def class_row(label):
        rows = lax.broadcasted_iota(jnp.int32, (classes, span), 0).astype(F32)
        table = t_buf[...].astype(F32)
        return jnp.sum(jnp.where(rows == label, table, 0.0), axis=0, keepdims=True)

    loads[0].wait()
    label_here = jnp.full((1, span), label_ref[0], jnp.int32).astype(F32)
    pack_out[:, pl.ds(0, span)] = label_here
    pack_out[:, pl.ds(slot, span)] = jnp.full((1, span), step_ref[0], jnp.int32).astype(F32)
    pack_out[:, pl.ds(2 * slot, span)] = class_row(label_here)
    pl.semaphore_wait(barrier, greeted)

    def halo(which):
        first, place = ((0, tile_rows + RADIUS), (tile_rows - RADIUS, 0))[which]
        return remote(
            kv_hbm.at[0, :, pl.ds(first, RADIUS)],
            kv_buf.at[:, pl.ds(place, RADIUS), pl.ds(0, tile_cols)],
            halo_send.at[which], halo_recv.at[which], row=(r - 1, r + 1)[which],
        )

    def side(i):
        return remote(
            kv_hbm.at[0],
            kv_buf.at[:, pl.ds(RADIUS, tile_rows), pl.ds((i + 1) * tile_cols, tile_cols)],
            side_send.at[0, i], side_recv.at[0, i], col=col_of(sides[i]),
        )

    def corner(which, i):
        place = (tile_rows + RADIUS, 0)[which]
        rows = pl.ds(place, RADIUS)
        return remote(
            kv_buf.at[:, rows, pl.ds(0, tile_cols)],
            kv_buf.at[:, rows, pl.ds((i + 1) * tile_cols, tile_cols)],
            side_send.at[1 + which, i], side_recv.at[1 + which, i], col=col_of(sides[i]),
        )

    def gossip(k):
        columns = pl.ds(k * cut, cut) if isinstance(k, int) else pl.ds(pl.multiple_of(k * cut, cut), cut)
        return remote(o_hbm.at[0, :, columns], o_peer.at[k], gossip_send.at[k], gossip_recv.at[k], dp=ahead)

    ask = remote(pack_out, pack_in, note_send.at[0], note_recv.at[0], dp=behind)
    ask.start()
    for k in range(AHEAD):
        gossip(k).start()
    pl.when(has_up)(lambda: halo(0).start())
    pl.when(has_down)(lambda: halo(1).start())
    for i in range(len(sides)):
        side(i).start()

    edge = jnp.zeros((2, RADIUS, wide, inner), BF16)

    @pl.when(jnp.logical_not(has_up))
    def _():
        kv_buf[:, pl.ds(0, RADIUS)] = edge

    @pl.when(jnp.logical_not(has_down))
    def _():
        kv_buf[:, pl.ds(tile_rows + RADIUS, RADIUS)] = edge

    n_q, n_k = GROUP * tile_cols, (GROUP + 2 * RADIUS) * wide
    blocks = wide // tile_cols
    q_index = lax.broadcasted_iota(jnp.int32, (n_q, n_k), 0)
    k_index = lax.broadcasted_iota(jnp.int32, (n_q, n_k), 1)
    q_row, q_col = q_index // tile_cols, lax.rem(q_index, tile_cols)
    k_block = k_index // tile_cols
    k_row = (k_block * -(-512 // blocks)) // 512
    k_block = k_block - k_row * blocks
    k_col = lax.rem(k_index, tile_cols)
    if n_col == 2:
        k_shift = jnp.where(k_block == 1, 1 - 2 * c, 0)
    else:
        k_shift = jnp.where(k_block == 1, 1, jnp.where(k_block == 2, -1, 0))
    k_col = k_col + k_shift * tile_cols
    near = (jnp.abs(k_col - q_col) <= RADIUS) & (k_row >= q_row) & (k_row <= q_row + 2 * RADIUS)
    k_col = k_col + c * tile_cols
    near = near & (k_col >= 0) & (k_col < n_col * tile_cols)
    for g in range(tile_rows // GROUP):
        row_here = k_row + (r * tile_rows + g * GROUP - RADIUS)
        seen = near & (row_here >= 0) & (row_here < n_row * tile_rows)
        bias[g] = jnp.where(seen, 0.0, -1e30)

    def w_copy(owner, k, sem, **where):
        rows = pl.ds(pl.multiple_of(owner * shard, shard), shard)
        place = w_buf.at[k, rows]
        return remote(place, place, sem, w_recv.at[owner, k], **where)

    def onward_copy(row, k):
        return w_copy(row * n_col + c, k, w_send.at[row, k], row=onward)

    def back_copy(row, k):
        return w_copy(row * n_col + c, k, w_back.at[row, k], row=mate)

    def side_copy(row, k, step):
        return w_copy(row * n_col + c, k, w_side.at[step - 1, row, k], col=col_of(step))

    def spread(row, k):
        for step in range(1, n_col):
            side_copy(row, k, step).start()

    def own_chunk(k):
        gossip(k).wait_recv()
        gossip(k).wait_send()

        @pl.when(k + AHEAD < CHUNKS)
        def _():
            gossip(k + AHEAD).start()

        columns = pl.ds(pl.multiple_of(k * cut, cut), cut)
        both = o_own[:, columns].astype(F32) + o_peer[k].astype(F32)
        w_buf[k, pl.ds(pl.multiple_of(me * shard, shard), shard), :] = (0.5 * both).astype(BF16)
        onward_copy(r, k).start()
        pl.when(is_inner | (k < OUTER))(lambda: spread(r, k))
        pl.when(is_inner & (k < OUTER))(lambda: back_copy(r, k).start())

    def hand_on(row, k):
        onward_copy(row, k).wait_recv()
        spread(row, k)

    def mate_chunk(k):
        @pl.when(is_inner)
        def _():
            onward_copy(mate, k).wait_recv()
            onward_copy(mate, k).start()
            spread(mate, k)

    loads[1].wait()
    own_chunk(0)

    own_chunk(1)
    mate_chunk(0)

    @pl.when(has_down)
    def _():
        halo(0).wait_recv()
        for i in range(len(sides)):
            corner(0, i).start()

    @pl.when(has_up)
    def _():
        halo(1).wait_recv()
        for i in range(len(sides)):
            corner(1, i).start()

    def against_gate(cond):
        tall = jnp.broadcast_to(cond, (16, span)).astype(BF16)
        return jnp.dot(tall, g_buf[...], preferred_element_type=F32)[0:1]

    half = width // 2
    position = me * span + lax.broadcasted_iota(jnp.int32, (1, span), 1)
    freq_index = jnp.where(position < half, position, position - half).astype(F32)
    frequency = jnp.exp(-math.log(10000.0) * freq_index / half)
    ask.wait_recv()
    mixed_row = 0.5 * (pack_in[:, pl.ds(2 * slot, span)] + class_row(pack_in[:, pl.ds(0, span)]))
    angle = pack_in[:, pl.ds(slot, span)] * frequency
    embed = jnp.where(position < half, jnp.cos(angle), jnp.sin(angle))
    value = mixed_row.astype(BF16).astype(F32) + embed
    cond = (value / (1.0 + jnp.exp(-value))).astype(BF16).astype(F32)
    loads[2].wait()
    reply_out[:, pl.ds(0, width)] = against_gate(cond)
    reply_out[:, pl.ds(width, span)] = cond
    answer = remote(reply_out, reply_in, note_send.at[1], note_recv.at[1], dp=ahead)
    answer.start()


    own_chunk(2)
    mate_chunk(1)

    answer.wait_recv()
    share = 0.5 * (reply_in[:, pl.ds(0, width)] + against_gate(reply_in[:, pl.ds(width, span)]))
    gates[me] = share

    def gate_copy(owner, step):
        other = lax.rem(me + step, group)
        return remote(
            gates.at[owner], gates.at[owner], gate_send.at[step - 1], gate_recv.at[owner],
            row=other // n_col, col=lax.rem(other, n_col),
        )

    for step in range(1, group):
        gate_copy(me, step).start()

    own_chunk(3)
    mate_chunk(2)

    loads[3].wait()
    loads[4].wait()
    for i in range(len(sides)):
        side(i).wait_recv()
        pl.when(has_down)(lambda i=i: corner(0, i).wait_recv())
        pl.when(has_up)(lambda i=i: corner(1, i).wait_recv())

    scale = 1.0 / math.sqrt(HDIM)

    def attend(first):
        parts = [(first + i, g) for i in range(2) for g in range(tile_rows // GROUP)]

        def lanes(head):
            return pl.ds(pl.multiple_of(head * HDIM, HDIM), HDIM)

        def near_rows(which, head, g):
            return kv_buf[which, pl.ds(g * GROUP, GROUP + 2 * RADIUS), :, lanes(head)].reshape(n_k, HDIM)

        scores = []
        for head, g in parts:
            query = q_buf[pl.ds(g * GROUP, GROUP), :, lanes(head)].reshape(n_q, HDIM)
            score = lax.dot_general(
                query, near_rows(0, head, g), (((1,), (1,)), ((), ())), preferred_element_type=F32
            )
            scores.append(score + bias[g])
        tops = [jnp.max(score, axis=1, keepdims=True) for score in scores]
        weights = [jnp.exp((score - top) * scale) for score, top in zip(scores, tops)]
        totals = [jnp.sum(weight, axis=1, keepdims=True) for weight in weights]
        sums = [
            jnp.dot(weight.astype(BF16), near_rows(1, head, g), preferred_element_type=F32)
            for weight, (head, g) in zip(weights, parts)
        ]
        means = [(part / total).astype(BF16) for part, total in zip(sums, totals)]
        for mean, (head, g) in zip(means, parts):
            att[pl.ds(g * n_q, n_q), lanes(head)] = mean

    pairs = heads // 2

    def other_half(k):
        @pl.when(is_inner)
        def _():
            for row in (n_row - 1 - r, n_row - 1 - mate):
                hand_on(row, k)
                pl.when(k < OUTER)(lambda row=row: back_copy(row, k).start())

    def att_copy(j):
        lanes = pl.ds(pl.multiple_of(j * 2 * HDIM, 2 * HDIM), 2 * HDIM)
        return remote(
            att.at[pl.ds(0, tokens), lanes], att.at[pl.ds(tokens, tokens), lanes],
            att_send.at[j], att_recv.at[j], row=mate,
        )

    def attend_pair(j, carry):
        @pl.when(j + 4 < CHUNKS)
        def _():
            own_chunk(j + 4)
            mate_chunk(j + 3)

        pl.when(j > 0)(lambda: other_half(j - 1))
        attend(2 * j)
        pl.when(is_outer)(lambda: att_copy(j).start())
        return carry

    lax.fori_loop(0, pairs, attend_pair, 0)
    mate_chunk(CHUNKS - 1)
    other_half(pairs - 1)

    for step in range(1, group):
        owner = lax.rem(me + step, group)
        gate_copy(owner, step).wait_recv()
    gate = gates[0]
    for i in range(1, group):
        gate = gate + gates[i]
    for k in range(CHUNKS):
        gate_sum[k] = gate[:, k * cut : (k + 1) * cut]

    def out_copy(k):
        return pltpu.make_async_copy(
            out_buf.at[k], out_hbm.at[:, pl.ds(pl.multiple_of(k * cut, cut), cut)], out_sem.at[k]
        )

    def mate_copy(k):
        return remote(
            mate_out.at[k], out_hbm.at[:, pl.ds(pl.multiple_of(k * cut, cut), cut)],
            mate_send.at[k], mate_recv.at[k], row=mate,
        )

    def from_side(k):
        for row in range(n_row):
            for step in range(1, n_col):
                owner = row * n_col + col_of(step)
                w_copy(owner, k, w_side.at[step - 1, row, k], col=col_of(step)).wait_recv()

    def rows_of(start, k):
        product = jnp.dot(att[pl.ds(start, tokens)], w_buf[k], preferred_element_type=F32)
        return (gate_sum[k] * product).astype(BF16)

    def own_rows(k):
        out_buf[k] = rows_of(0, k)
        out_copy(k).start()

    def project(k, carry):
        pl.when((k + 1 >= pairs) & (k + 1 < CHUNKS))(lambda: other_half(k + 1))
        from_side(k)

        @pl.when(k == OUTER)
        def _():
            for j in range(pairs):
                att_copy(j).wait_recv()

        @pl.when(k >= OUTER)
        def _():
            mate_out[k] = rows_of(tokens, k)
            mate_copy(k).start()

        own_rows(k)
        return carry

    @pl.when(is_inner)
    def _():
        lax.fori_loop(0, CHUNKS, project, 0)

    @pl.when(is_outer)
    def _():
        for k in range(OUTER):
            for row in (mate, n_row - 1 - mate, n_row - 1 - r):
                back_copy(row, k).wait_recv()
                spread(row, k)
        for k in range(OUTER):
            from_side(k)
            own_rows(k)
        for k in range(OUTER, CHUNKS):
            mate_copy(k).wait_recv()

    def sent(k, carry):
        onward_copy(r, k).wait_send()

        @pl.when(is_inner | (k < OUTER))
        def _():
            out_copy(k).wait()
            for row in range(n_row):
                for step in range(1, n_col):
                    side_copy(row, k, step).wait_send()

        @pl.when(is_inner)
        def _():
            onward_copy(mate, k).wait_send()
            pl.when(k >= OUTER)(lambda: mate_copy(k).wait_send())

            @pl.when(k < OUTER)
            def _():
                for row in (r, n_row - 1 - r, n_row - 1 - mate):
                    back_copy(row, k).wait_send()

        return carry

    lax.fori_loop(0, CHUNKS, sent, 0)

    @pl.when(is_outer)
    def _():
        for j in range(pairs):
            att_copy(j).wait_send()

    pl.when(has_up)(lambda: halo(0).wait_send())
    pl.when(has_down)(lambda: halo(1).wait_send())
    for i in range(len(sides)):
        side(i).wait_send()
        pl.when(has_down)(lambda i=i: corner(0, i).wait_send())
        pl.when(has_up)(lambda i=i: corner(1, i).wait_send())
    ask.wait_send()
    answer.wait_send()
    for step in range(1, group):
        gate_copy(me, step).wait_send()


def layer(sizes, distance, number, queries, keyvals, out_weight, gate_weight, class_table, labels, timesteps):
    n_dp, n_row, n_col = sizes
    group = n_row * n_col
    _, tile_rows, tile_cols, inner = queries.shape
    _, shard, width = out_weight.shape
    span = gate_weight.shape[1]
    classes = class_table.shape[1]
    cut = width // CHUNKS
    slot = max(span, 128)
    n_side = 1 if n_col == 2 else 2
    wide = tile_cols * (1 + n_side)
    tokens = tile_rows * tile_cols
    n_q, n_k = GROUP * tile_cols, (GROUP + 2 * RADIUS) * wide
    dma = pltpu.SemaphoreType.DMA
    return pl.pallas_call(
        functools.partial(kernel, sizes, distance),
        out_shape=jax.ShapeDtypeStruct((tokens, width), BF16),
        in_specs=[pl.BlockSpec(memory_space=pl.ANY)] * 5 + [pl.BlockSpec(memory_space=pltpu.SMEM)] * 2,
        out_specs=pl.BlockSpec(memory_space=pl.ANY),
        scratch_shapes=[
            pltpu.VMEM((tile_rows, tile_cols, inner), BF16),
            pltpu.VMEM((2, tile_rows + 2 * RADIUS, wide, inner), BF16),
            pltpu.VMEM((tile_rows // GROUP, n_q, n_k), F32),
            pltpu.VMEM((2 * tokens, inner), BF16),
            pltpu.VMEM((shard, width), BF16),
            pltpu.VMEM((CHUNKS, shard, cut), BF16),
            pltpu.VMEM((CHUNKS, group * shard, cut), BF16),
            pltpu.VMEM((CHUNKS, tokens, cut), BF16),
            pltpu.VMEM((span, width), BF16),
            pltpu.VMEM((classes, span), BF16),
            pltpu.VMEM((1, 3 * slot), F32),
            pltpu.VMEM((1, 3 * slot), F32),
            pltpu.VMEM((1, width + slot), F32),
            pltpu.VMEM((1, width + slot), F32),
            pltpu.VMEM((group, 1, width), F32),
            pltpu.VMEM((CHUNKS, 1, cut), F32),
            pltpu.VMEM((CHUNKS, tokens, cut), BF16),
            dma((5,)),
            dma((CHUNKS,)),
            dma((CHUNKS,)),
            dma((CHUNKS,)),
            dma((n_row, CHUNKS)),
            dma((n_row, CHUNKS)),
            dma((n_col - 1, n_row, CHUNKS)),
            dma((group, CHUNKS)),
            dma((inner // HDIM // 2,)),
            dma((inner // HDIM // 2,)),
            dma((CHUNKS,)),
            dma((CHUNKS,)),
            dma((2,)),
            dma((2,)),
            dma((3, n_side)),
            dma((3, n_side)),
            dma((2,)),
            dma((2,)),
            dma((group - 1,)),
            dma((group,)),
        ],
        compiler_params=pltpu.CompilerParams(
            collective_id=number, has_side_effects=True, vmem_limit_bytes=48 * 2**20
        ),
        cost_estimate=pl.CostEstimate(flops=2 * tokens * inner * width, bytes_accessed=2**22, transcendentals=0),
        name=f"sublayer_distance_{distance}",
    )(queries, keyvals, out_weight, gate_weight, class_table, labels, timesteps)


def solution(mesh):
    sizes = tuple(mesh.shape[name] for name in ("dp", "row", "col"))
    bit_count = sizes[0].bit_length() - 1

    def local(queries, keyvals, out_weight, gate_weight, class_table, labels, timesteps, round_index):
        branches = [functools.partial(layer, sizes, 2**power, power) for power in range(bit_count)]
        operands = (queries, keyvals, out_weight, gate_weight, class_table, labels, timesteps)
        result = lax.switch(round_index[0] % bit_count, branches, *operands)
        return result.reshape(queries.shape[:3] + (out_weight.shape[2],))

    placed = (
        P("dp", "row", "col", None),
        P("dp", None, "row", "col", None),
        P("dp", ("row", "col"), None),
        P("dp", ("row", "col"), None),
        P("dp", None, ("row", "col")),
        P("dp"),
        P("dp"),
        P(),
    )
    return jax.shard_map(
        local, mesh=mesh, in_specs=placed, out_specs=P("dp", "row", "col", None), check_vma=False
    )
```

```python
import functools
import math

import jax
import jax.numpy as jnp
from jax import lax
from jax.experimental import pallas as pl
from jax.experimental.pallas import tpu as pltpu
from jax.sharding import PartitionSpec as P

HDIM = 128
RADIUS = 3
CHUNKS = 8
AHEAD = 2
OUTER = 2
MESH = pl.DeviceIdType.MESH
F32 = jnp.float32
BF16 = jnp.bfloat16


def remote(src, dst, send, recv, **where):
    return pltpu.make_async_remote_copy(
        src_ref=src, dst_ref=dst, send_sem=send, recv_sem=recv, device_id=where, device_id_type=MESH
    )


def kernel(
    sizes, distance,
    q_hbm, kv_hbm, o_hbm, g_hbm, t_hbm, label_ref, step_ref,
    out_hbm,
    q_buf, kv_buf, bias_mid, bias_edge, att, o_own, o_peer, w_buf, out_buf, g_buf, t_buf,
    pack_out, pack_in, reply_out, reply_in, gates, gate_sum, mate_out,
    local_sem, out_sem, gossip_send, gossip_recv, w_send, w_back, w_side, w_recv, att_send, att_recv, mate_send, mate_recv,
    halo_send, halo_recv, side_send, side_recv, note_send, note_recv, gate_send, gate_recv,
):
    n_dp, n_row, n_col = sizes
    group = n_row * n_col
    tile_rows, tile_cols, inner = kv_hbm.shape[2:]
    shard, width = o_hbm.shape[1:]
    cut = width // CHUNKS
    span = t_hbm.shape[2]
    slot = pack_out.shape[1] // 3
    classes = t_hbm.shape[1]
    heads = inner // HDIM
    sides = [1] if n_col == 2 else [n_col - 1, 1]
    wide = kv_buf.shape[2]

    p, r, c = lax.axis_index("dp"), lax.axis_index("row"), lax.axis_index("col")
    me = r * n_col + c
    ahead, behind = lax.rem(p + distance, n_dp), lax.rem(p + n_dp - distance, n_dp)
    has_up, has_down = r > 0, r < n_row - 1
    is_outer = (r == 0) | (r == n_row - 1)
    is_inner = jnp.logical_not(is_outer)
    mate = r + 1 - 2 * lax.rem(r, 2)
    onward = 1 + lax.rem(r, 2)
    tokens = tile_rows * tile_cols

    def col_of(step):
        return lax.rem(c + step, n_col)

    loads = [
        pltpu.make_async_copy(t_hbm.at[0], t_buf, local_sem.at[0]),
        pltpu.make_async_copy(o_hbm.at[0], o_own, local_sem.at[1]),
        pltpu.make_async_copy(g_hbm.at[0], g_buf, local_sem.at[2]),
        pltpu.make_async_copy(q_hbm.at[0], q_buf, local_sem.at[3]),
        pltpu.make_async_copy(
            kv_hbm.at[0], kv_buf.at[:, pl.ds(RADIUS, tile_rows), pl.ds(0, tile_cols)], local_sem.at[4]
        ),
    ]
    for load in loads:
        load.start()

    barrier = pltpu.get_barrier_semaphore()
    for step in range(1, group):
        other = lax.rem(me + step, group)
        pl.semaphore_signal(
            barrier, inc=1, device_id={"row": other // n_col, "col": lax.rem(other, n_col)}, device_id_type=MESH
        )
    pl.semaphore_signal(barrier, inc=1, device_id={"dp": ahead}, device_id_type=MESH)
    greeted = group
    if (2 * distance) % n_dp:
        pl.semaphore_signal(barrier, inc=1, device_id={"dp": behind}, device_id_type=MESH)
        greeted += 1
    def class_row(label):
        rows = lax.broadcasted_iota(jnp.int32, (classes, span), 0).astype(F32)
        table = t_buf[...].astype(F32)
        return jnp.sum(jnp.where(rows == label, table, 0.0), axis=0, keepdims=True)

    loads[0].wait()
    label_here = jnp.full((1, span), label_ref[0], jnp.int32).astype(F32)
    pack_out[:, pl.ds(0, span)] = label_here
    pack_out[:, pl.ds(slot, span)] = jnp.full((1, span), step_ref[0], jnp.int32).astype(F32)
    pack_out[:, pl.ds(2 * slot, span)] = class_row(label_here)
    pl.semaphore_wait(barrier, greeted)

    def halo(which):
        first, place = ((0, tile_rows + RADIUS), (tile_rows - RADIUS, 0))[which]
        return remote(
            kv_hbm.at[0, :, pl.ds(first, RADIUS)],
            kv_buf.at[:, pl.ds(place, RADIUS), pl.ds(0, tile_cols)],
            halo_send.at[which], halo_recv.at[which], row=(r - 1, r + 1)[which],
        )

    def side(i):
        return remote(
            kv_hbm.at[0],
            kv_buf.at[:, pl.ds(RADIUS, tile_rows), pl.ds((i + 1) * tile_cols, tile_cols)],
            side_send.at[0, i], side_recv.at[0, i], col=col_of(sides[i]),
        )

    def corner(which, i):
        place = (tile_rows + RADIUS, 0)[which]
        rows = pl.ds(place, RADIUS)
        return remote(
            kv_buf.at[:, rows, pl.ds(0, tile_cols)],
            kv_buf.at[:, rows, pl.ds((i + 1) * tile_cols, tile_cols)],
            side_send.at[1 + which, i], side_recv.at[1 + which, i], col=col_of(sides[i]),
        )

    def gossip(k):
        columns = pl.ds(k * cut, cut) if isinstance(k, int) else pl.ds(pl.multiple_of(k * cut, cut), cut)
        return remote(o_hbm.at[0, :, columns], o_peer.at[k], gossip_send.at[k], gossip_recv.at[k], dp=ahead)

    ask = remote(pack_out, pack_in, note_send.at[0], note_recv.at[0], dp=behind)
    ask.start()
    for k in range(AHEAD):
        gossip(k).start()
    pl.when(has_up)(lambda: halo(0).start())
    pl.when(has_down)(lambda: halo(1).start())
    for i in range(len(sides)):
        side(i).start()

    edge = jnp.zeros((2, RADIUS, wide, inner), BF16)

    @pl.when(jnp.logical_not(has_up))
    def _():
        kv_buf[:, pl.ds(0, RADIUS)] = edge

    @pl.when(jnp.logical_not(has_down))
    def _():
        kv_buf[:, pl.ds(tile_rows + RADIUS, RADIUS)] = edge

    blocks = wide // tile_cols
    mid_rows = tile_rows - 2 * RADIUS

    def allowed(q_start, q_rows, k_start):
        extent = (q_rows * tile_cols, tile_rows * wide)
        q_index = lax.broadcasted_iota(jnp.int32, extent, 0)
        k_index = lax.broadcasted_iota(jnp.int32, extent, 1)
        q_row, q_col = q_start + q_index // tile_cols, lax.rem(q_index, tile_cols)
        k_block = k_index // tile_cols
        k_row = (k_block * -(-512 // blocks)) // 512
        k_block = k_block - k_row * blocks
        k_row = k_row + k_start
        k_col = lax.rem(k_index, tile_cols)
        if n_col == 2:
            k_shift = jnp.where(k_block == 1, 1 - 2 * c, 0)
        else:
            k_shift = jnp.where(k_block == 1, 1, jnp.where(k_block == 2, -1, 0))
        k_col = k_col + k_shift * tile_cols
        near = (jnp.abs(k_col - q_col) <= RADIUS) & (k_row >= q_row) & (k_row <= q_row + 2 * RADIUS)
        k_col = k_col + c * tile_cols
        k_row = k_row + (r * tile_rows - RADIUS)
        inside = (k_col >= 0) & (k_col < n_col * tile_cols) & (k_row >= 0) & (k_row < n_row * tile_rows)
        return jnp.where(near & inside, 0.0, -1e30)

    middle = (RADIUS, mid_rows, RADIUS, bias_mid)
    edges = (
        (0, RADIUS, 0, bias_edge.at[0]),
        (tile_rows - RADIUS, RADIUS, 2 * RADIUS, bias_edge.at[1]),
    )
    for q_start, q_rows, k_start, mask in (middle,) + edges:
        mask[...] = allowed(q_start, q_rows, k_start)

    def w_copy(owner, k, sem, **where):
        rows = pl.ds(pl.multiple_of(owner * shard, shard), shard)
        place = w_buf.at[k, rows]
        return remote(place, place, sem, w_recv.at[owner, k], **where)

    def onward_copy(row, k):
        return w_copy(row * n_col + c, k, w_send.at[row, k], row=onward)

    def back_copy(row, k):
        return w_copy(row * n_col + c, k, w_back.at[row, k], row=mate)

    def side_copy(row, k, step):
        return w_copy(row * n_col + c, k, w_side.at[step - 1, row, k], col=col_of(step))

    def spread(row, k):
        for step in range(1, n_col):
            side_copy(row, k, step).start()

    def own_chunk(k):
        gossip(k).wait_recv()
        gossip(k).wait_send()

        @pl.when(k + AHEAD < CHUNKS)
        def _():
            gossip(k + AHEAD).start()

        columns = pl.ds(pl.multiple_of(k * cut, cut), cut)
        both = o_own[:, columns].astype(F32) + o_peer[k].astype(F32)
        w_buf[k, pl.ds(pl.multiple_of(me * shard, shard), shard), :] = (0.5 * both).astype(BF16)
        onward_copy(r, k).start()
        pl.when(is_inner | (k < OUTER))(lambda: spread(r, k))
        pl.when(is_inner & (k < OUTER))(lambda: back_copy(r, k).start())

    def hand_on(row, k):
        onward_copy(row, k).wait_recv()
        spread(row, k)

    def mate_chunk(k):
        @pl.when(is_inner)
        def _():
            onward_copy(mate, k).wait_recv()
            onward_copy(mate, k).start()
            spread(mate, k)

    scale = 1.0 / math.sqrt(HDIM)

    def attend(parts):
        def lanes(head):
            return pl.ds(pl.multiple_of(head * HDIM, HDIM), HDIM)

        def near_rows(which, head, k_start):
            return kv_buf[which, pl.ds(k_start, tile_rows), :, lanes(head)].reshape(tile_rows * wide, HDIM)

        scores = []
        for head, (q_start, q_rows, k_start, mask) in parts:
            query = q_buf[pl.ds(q_start, q_rows), :, lanes(head)].reshape(q_rows * tile_cols, HDIM)
            score = lax.dot_general(
                query, near_rows(0, head, k_start), (((1,), (1,)), ((), ())), preferred_element_type=F32
            )
            scores.append(score + mask[...])
        tops = [jnp.max(score, axis=1, keepdims=True) for score in scores]
        weights = [jnp.exp((score - top) * scale) for score, top in zip(scores, tops)]
        totals = [jnp.sum(weight, axis=1, keepdims=True) for weight in weights]
        sums = [
            jnp.dot(weight.astype(BF16), near_rows(1, head, k_start), preferred_element_type=F32)
            for weight, (head, (_, _, k_start, _)) in zip(weights, parts)
        ]
        means = [(part / total).astype(BF16) for part, total in zip(sums, totals)]
        for mean, (head, (q_start, q_rows, _, _)) in zip(means, parts):
            att[pl.ds(q_start * tile_cols, q_rows * tile_cols), lanes(head)] = mean

    loads[1].wait()
    own_chunk(0)
    loads[3].wait()
    loads[4].wait()
    for i in range(len(sides)):
        side(i).wait_recv()

    own_chunk(1)
    attend([(head, middle) for head in range(heads // 2)])

    @pl.when(has_down)
    def _():
        halo(0).wait_recv()
        for i in range(len(sides)):
            corner(0, i).start()

    @pl.when(has_up)
    def _():
        halo(1).wait_recv()
        for i in range(len(sides)):
            corner(1, i).start()

    own_chunk(2)
    mate_chunk(0)
    attend([(head, middle) for head in range(heads // 2, heads)])
    own_chunk(3)
    mate_chunk(1)

    def against_gate(cond):
        tall = jnp.broadcast_to(cond, (16, span)).astype(BF16)
        return jnp.dot(tall, g_buf[...], preferred_element_type=F32)[0:1]

    half = width // 2
    position = me * span + lax.broadcasted_iota(jnp.int32, (1, span), 1)
    freq_index = jnp.where(position < half, position, position - half).astype(F32)
    frequency = jnp.exp(-math.log(10000.0) * freq_index / half)
    ask.wait_recv()
    mixed_row = 0.5 * (pack_in[:, pl.ds(2 * slot, span)] + class_row(pack_in[:, pl.ds(0, span)]))
    angle = pack_in[:, pl.ds(slot, span)] * frequency
    embed = jnp.where(position < half, jnp.cos(angle), jnp.sin(angle))
    value = mixed_row.astype(BF16).astype(F32) + embed
    cond = (value / (1.0 + jnp.exp(-value))).astype(BF16).astype(F32)
    loads[2].wait()
    reply_out[:, pl.ds(0, width)] = against_gate(cond)
    reply_out[:, pl.ds(width, span)] = cond
    answer = remote(reply_out, reply_in, note_send.at[1], note_recv.at[1], dp=ahead)
    answer.start()


    for i in range(len(sides)):
        pl.when(has_down)(lambda i=i: corner(0, i).wait_recv())
        pl.when(has_up)(lambda i=i: corner(1, i).wait_recv())

    pairs = heads // 2

    def other_half(k):
        @pl.when(is_inner)
        def _():
            for row in (n_row - 1 - r, n_row - 1 - mate):
                hand_on(row, k)
                pl.when(k < OUTER)(lambda row=row: back_copy(row, k).start())

    def att_copy(j):
        lanes = pl.ds(pl.multiple_of(j * 2 * HDIM, 2 * HDIM), 2 * HDIM)
        return remote(
            att.at[pl.ds(0, tokens), lanes], att.at[pl.ds(tokens, tokens), lanes],
            att_send.at[j], att_recv.at[j], row=mate,
        )

    def gate_copy(owner, step):
        other = lax.rem(me + step, group)
        return remote(
            gates.at[owner], gates.at[owner], gate_send.at[step - 1], gate_recv.at[owner],
            row=other // n_col, col=lax.rem(other, n_col),
        )

    def send_share():
        answer.wait_recv()
        share = 0.5 * (reply_in[:, pl.ds(0, width)] + against_gate(reply_in[:, pl.ds(width, span)]))
        gates[me] = share
        for step in range(1, group):
            gate_copy(me, step).start()

    def attend_pair(j, carry):
        @pl.when(j + 4 < CHUNKS)
        def _():
            own_chunk(j + 4)
            mate_chunk(j + 2)

        pl.when(j == 1)(send_share)
        pl.when(j > 1)(lambda: other_half(j - 2))
        attend([(2 * j + i, edge) for i in range(2) for edge in edges])
        pl.when(is_outer)(lambda: att_copy(j).start())
        return carry

    lax.fori_loop(0, pairs, attend_pair, 0)
    mate_chunk(CHUNKS - 2)
    mate_chunk(CHUNKS - 1)
    other_half(pairs - 2)
    other_half(pairs - 1)

    for step in range(1, group):
        owner = lax.rem(me + step, group)
        gate_copy(owner, step).wait_recv()
    gate = gates[0]
    for i in range(1, group):
        gate = gate + gates[i]
    for k in range(CHUNKS):
        gate_sum[k] = gate[:, k * cut : (k + 1) * cut]

    def out_copy(k):
        return pltpu.make_async_copy(
            out_buf.at[k], out_hbm.at[:, pl.ds(pl.multiple_of(k * cut, cut), cut)], out_sem.at[k]
        )

    def mate_copy(k):
        return remote(
            mate_out.at[k], out_hbm.at[:, pl.ds(pl.multiple_of(k * cut, cut), cut)],
            mate_send.at[k], mate_recv.at[k], row=mate,
        )

    def from_side(k):
        for row in range(n_row):
            for step in range(1, n_col):
                owner = row * n_col + col_of(step)
                w_copy(owner, k, w_side.at[step - 1, row, k], col=col_of(step)).wait_recv()

    def rows_of(count, k):
        product = jnp.dot(att[pl.ds(0, count)], w_buf[k], preferred_element_type=F32)
        return (gate_sum[k] * product).astype(BF16)

    def own_rows(k):
        out_buf[k] = rows_of(tokens, k)
        out_copy(k).start()

    def project(k, carry):
        pl.when((k + 1 >= pairs) & (k + 1 < CHUNKS))(lambda: other_half(k + 1))
        from_side(k)

        @pl.when(k == OUTER)
        def _():
            for j in range(pairs):
                att_copy(j).wait_recv()

        @pl.when(k >= OUTER)
        def _():
            both = rows_of(2 * tokens, k)
            mate_out[k] = both[tokens:]
            mate_copy(k).start()
            out_buf[k] = both[:tokens]
            out_copy(k).start()

        pl.when(k < OUTER)(lambda: own_rows(k))
        return carry

    @pl.when(is_inner)
    def _():
        lax.fori_loop(0, CHUNKS, project, 0)

    @pl.when(is_outer)
    def _():
        for k in range(OUTER):
            for row in (mate, n_row - 1 - mate, n_row - 1 - r):
                back_copy(row, k).wait_recv()
                spread(row, k)
        for k in range(OUTER):
            from_side(k)
            own_rows(k)
        for k in range(OUTER, CHUNKS):
            mate_copy(k).wait_recv()

    def sent(k, carry):
        onward_copy(r, k).wait_send()

        @pl.when(is_inner | (k < OUTER))
        def _():
            out_copy(k).wait()
            for row in range(n_row):
                for step in range(1, n_col):
                    side_copy(row, k, step).wait_send()

        @pl.when(is_inner)
        def _():
            onward_copy(mate, k).wait_send()
            pl.when(k >= OUTER)(lambda: mate_copy(k).wait_send())

            @pl.when(k < OUTER)
            def _():
                for row in (r, n_row - 1 - r, n_row - 1 - mate):
                    back_copy(row, k).wait_send()

        return carry

    lax.fori_loop(0, CHUNKS, sent, 0)

    @pl.when(is_outer)
    def _():
        for j in range(pairs):
            att_copy(j).wait_send()

    pl.when(has_up)(lambda: halo(0).wait_send())
    pl.when(has_down)(lambda: halo(1).wait_send())
    for i in range(len(sides)):
        side(i).wait_send()
        pl.when(has_down)(lambda i=i: corner(0, i).wait_send())
        pl.when(has_up)(lambda i=i: corner(1, i).wait_send())
    ask.wait_send()
    answer.wait_send()
    for step in range(1, group):
        gate_copy(me, step).wait_send()


def layer(sizes, distance, number, queries, keyvals, out_weight, gate_weight, class_table, labels, timesteps):
    n_dp, n_row, n_col = sizes
    group = n_row * n_col
    _, tile_rows, tile_cols, inner = queries.shape
    _, shard, width = out_weight.shape
    span = gate_weight.shape[1]
    classes = class_table.shape[1]
    cut = width // CHUNKS
    slot = max(span, 128)
    n_side = 1 if n_col == 2 else 2
    wide = tile_cols * (1 + n_side)
    tokens = tile_rows * tile_cols
    n_k = tile_rows * wide
    dma = pltpu.SemaphoreType.DMA
    return pl.pallas_call(
        functools.partial(kernel, sizes, distance),
        out_shape=jax.ShapeDtypeStruct((tokens, width), BF16),
        in_specs=[pl.BlockSpec(memory_space=pl.ANY)] * 5 + [pl.BlockSpec(memory_space=pltpu.SMEM)] * 2,
        out_specs=pl.BlockSpec(memory_space=pl.ANY),
        scratch_shapes=[
            pltpu.VMEM((tile_rows, tile_cols, inner), BF16),
            pltpu.VMEM((2, tile_rows + 2 * RADIUS, wide, inner), BF16),
            pltpu.VMEM(((tile_rows - 2 * RADIUS) * tile_cols, n_k), F32),
            pltpu.VMEM((2, RADIUS * tile_cols, n_k), F32),
            pltpu.VMEM((2 * tokens, inner), BF16),
            pltpu.VMEM((shard, width), BF16),
            pltpu.VMEM((CHUNKS, shard, cut), BF16),
            pltpu.VMEM((CHUNKS, group * shard, cut), BF16),
            pltpu.VMEM((CHUNKS, tokens, cut), BF16),
            pltpu.VMEM((span, width), BF16),
            pltpu.VMEM((classes, span), BF16),
            pltpu.VMEM((1, 3 * slot), F32),
            pltpu.VMEM((1, 3 * slot), F32),
            pltpu.VMEM((1, width + slot), F32),
            pltpu.VMEM((1, width + slot), F32),
            pltpu.VMEM((group, 1, width), F32),
            pltpu.VMEM((CHUNKS, 1, cut), F32),
            pltpu.VMEM((CHUNKS, tokens, cut), BF16),
            dma((5,)),
            dma((CHUNKS,)),
            dma((CHUNKS,)),
            dma((CHUNKS,)),
            dma((n_row, CHUNKS)),
            dma((n_row, CHUNKS)),
            dma((n_col - 1, n_row, CHUNKS)),
            dma((group, CHUNKS)),
            dma((inner // HDIM // 2,)),
            dma((inner // HDIM // 2,)),
            dma((CHUNKS,)),
            dma((CHUNKS,)),
            dma((2,)),
            dma((2,)),
            dma((3, n_side)),
            dma((3, n_side)),
            dma((2,)),
            dma((2,)),
            dma((group - 1,)),
            dma((group,)),
        ],
        compiler_params=pltpu.CompilerParams(
            collective_id=number, has_side_effects=True, vmem_limit_bytes=48 * 2**20
        ),
        cost_estimate=pl.CostEstimate(flops=2 * tokens * inner * width, bytes_accessed=2**22, transcendentals=0),
        name=f"sublayer_distance_{distance}",
    )(queries, keyvals, out_weight, gate_weight, class_table, labels, timesteps)


def solution(mesh):
    sizes = tuple(mesh.shape[name] for name in ("dp", "row", "col"))
    bit_count = sizes[0].bit_length() - 1

    def local(queries, keyvals, out_weight, gate_weight, class_table, labels, timesteps, round_index):
        branches = [functools.partial(layer, sizes, 2**power, power) for power in range(bit_count)]
        operands = (queries, keyvals, out_weight, gate_weight, class_table, labels, timesteps)
        result = lax.switch(round_index[0] % bit_count, branches, *operands)
        return result.reshape(queries.shape[:3] + (out_weight.shape[2],))

    placed = (
        P("dp", "row", "col", None),
        P("dp", None, "row", "col", None),
        P("dp", ("row", "col"), None),
        P("dp", ("row", "col"), None),
        P("dp", None, ("row", "col")),
        P("dp"),
        P("dp"),
        P(),
    )
    return jax.shard_map(
        local, mesh=mesh, in_specs=placed, out_specs=P("dp", "row", "col", None), check_vma=False
    )
```

```python
import functools
import math

import jax
import jax.numpy as jnp
from jax import lax
from jax.experimental import pallas as pl
from jax.experimental.pallas import tpu as pltpu
from jax.sharding import PartitionSpec as P

HDIM = 128
RADIUS = 3
CHUNKS = 8
AHEAD = 3
OUTER = 3
MESH = pl.DeviceIdType.MESH
F32 = jnp.float32
BF16 = jnp.bfloat16


def remote(src, dst, send, recv, **where):
    return pltpu.make_async_remote_copy(
        src_ref=src, dst_ref=dst, send_sem=send, recv_sem=recv, device_id=where, device_id_type=MESH
    )


def kernel(
    sizes, distance,
    q_hbm, kv_hbm, o_hbm, g_hbm, t_hbm, label_ref, step_ref,
    out_hbm,
    q_buf, kv_buf, bias_mid, bias_edge, att, o_own, o_peer, w_buf, out_buf, g_buf, t_buf,
    pack_out, pack_in, reply_out, reply_in, gates, gate_sum, mate_out,
    local_sem, out_sem, gossip_send, gossip_recv, w_send, w_back, w_side, w_recv, att_send, att_recv, mate_send, mate_recv,
    halo_send, halo_recv, side_send, side_recv, note_send, note_recv, gate_send, gate_recv,
):
    n_dp, n_row, n_col = sizes
    group = n_row * n_col
    tile_rows, tile_cols, inner = kv_hbm.shape[2:]
    shard, width = o_hbm.shape[1:]
    cut = width // CHUNKS
    span = t_hbm.shape[2]
    slot = pack_out.shape[1] // 3
    classes = t_hbm.shape[1]
    heads = inner // HDIM
    sides = [1] if n_col == 2 else [n_col - 1, 1]
    wide = kv_buf.shape[2]

    p, r, c = lax.axis_index("dp"), lax.axis_index("row"), lax.axis_index("col")
    me = r * n_col + c
    ahead, behind = lax.rem(p + distance, n_dp), lax.rem(p + n_dp - distance, n_dp)
    has_up, has_down = r > 0, r < n_row - 1
    is_outer = (r == 0) | (r == n_row - 1)
    is_inner = jnp.logical_not(is_outer)
    mate = r + 1 - 2 * lax.rem(r, 2)
    onward = 1 + lax.rem(r, 2)
    tokens = tile_rows * tile_cols

    def col_of(step):
        return lax.rem(c + step, n_col)

    loads = [
        pltpu.make_async_copy(t_hbm.at[0], t_buf, local_sem.at[0]),
        pltpu.make_async_copy(o_hbm.at[0], o_own, local_sem.at[1]),
        pltpu.make_async_copy(g_hbm.at[0], g_buf, local_sem.at[2]),
        pltpu.make_async_copy(q_hbm.at[0], q_buf, local_sem.at[3]),
        pltpu.make_async_copy(
            kv_hbm.at[0], kv_buf.at[:, pl.ds(RADIUS, tile_rows), pl.ds(0, tile_cols)], local_sem.at[4]
        ),
    ]
    for load in loads:
        load.start()

    barrier = pltpu.get_barrier_semaphore()
    for step in range(1, group):
        other = lax.rem(me + step, group)
        pl.semaphore_signal(
            barrier, inc=1, device_id={"row": other // n_col, "col": lax.rem(other, n_col)}, device_id_type=MESH
        )
    pl.semaphore_signal(barrier, inc=1, device_id={"dp": ahead}, device_id_type=MESH)
    greeted = group
    if (2 * distance) % n_dp:
        pl.semaphore_signal(barrier, inc=1, device_id={"dp": behind}, device_id_type=MESH)
        greeted += 1
    def class_row(label):
        rows = lax.broadcasted_iota(jnp.int32, (classes, span), 0).astype(F32)
        table = t_buf[...].astype(F32)
        return jnp.sum(jnp.where(rows == label, table, 0.0), axis=0, keepdims=True)

    loads[0].wait()
    label_here = jnp.full((1, span), label_ref[0], jnp.int32).astype(F32)
    pack_out[:, pl.ds(0, span)] = label_here
    pack_out[:, pl.ds(slot, span)] = jnp.full((1, span), step_ref[0], jnp.int32).astype(F32)
    pack_out[:, pl.ds(2 * slot, span)] = class_row(label_here)
    pl.semaphore_wait(barrier, greeted)

    def halo(which):
        first, place = ((0, tile_rows + RADIUS), (tile_rows - RADIUS, 0))[which]
        return remote(
            kv_hbm.at[0, :, pl.ds(first, RADIUS)],
            kv_buf.at[:, pl.ds(place, RADIUS), pl.ds(0, tile_cols)],
            halo_send.at[which], halo_recv.at[which], row=(r - 1, r + 1)[which],
        )

    def side(i):
        return remote(
            kv_hbm.at[0],
            kv_buf.at[:, pl.ds(RADIUS, tile_rows), pl.ds((i + 1) * tile_cols, tile_cols)],
            side_send.at[0, i], side_recv.at[0, i], col=col_of(sides[i]),
        )

    def corner(which, i):
        place = (tile_rows + RADIUS, 0)[which]
        rows = pl.ds(place, RADIUS)
        return remote(
            kv_buf.at[:, rows, pl.ds(0, tile_cols)],
            kv_buf.at[:, rows, pl.ds((i + 1) * tile_cols, tile_cols)],
            side_send.at[1 + which, i], side_recv.at[1 + which, i], col=col_of(sides[i]),
        )

    def gossip(k):
        columns = pl.ds(k * cut, cut) if isinstance(k, int) else pl.ds(pl.multiple_of(k * cut, cut), cut)
        return remote(o_hbm.at[0, :, columns], o_peer.at[k], gossip_send.at[k], gossip_recv.at[k], dp=ahead)

    ask = remote(pack_out, pack_in, note_send.at[0], note_recv.at[0], dp=behind)
    ask.start()
    for k in range(AHEAD):
        gossip(k).start()
    pl.when(has_up)(lambda: halo(0).start())
    pl.when(has_down)(lambda: halo(1).start())
    for i in range(len(sides)):
        side(i).start()

    edge = jnp.zeros((2, RADIUS, wide, inner), BF16)

    @pl.when(jnp.logical_not(has_up))
    def _():
        kv_buf[:, pl.ds(0, RADIUS)] = edge

    @pl.when(jnp.logical_not(has_down))
    def _():
        kv_buf[:, pl.ds(tile_rows + RADIUS, RADIUS)] = edge

    blocks = wide // tile_cols
    mid_rows = tile_rows - 2 * RADIUS

    def allowed(q_start, q_rows, k_start):
        extent = (q_rows * tile_cols, tile_rows * wide)
        q_index = lax.broadcasted_iota(jnp.int32, extent, 0)
        k_index = lax.broadcasted_iota(jnp.int32, extent, 1)
        q_row, q_col = q_start + q_index // tile_cols, lax.rem(q_index, tile_cols)
        k_block = k_index // tile_cols
        k_row = (k_block * -(-512 // blocks)) // 512
        k_block = k_block - k_row * blocks
        k_row = k_row + k_start
        k_col = lax.rem(k_index, tile_cols)
        if n_col == 2:
            k_shift = jnp.where(k_block == 1, 1 - 2 * c, 0)
        else:
            k_shift = jnp.where(k_block == 1, 1, jnp.where(k_block == 2, -1, 0))
        k_col = k_col + k_shift * tile_cols
        near = (jnp.abs(k_col - q_col) <= RADIUS) & (k_row >= q_row) & (k_row <= q_row + 2 * RADIUS)
        k_col = k_col + c * tile_cols
        k_row = k_row + (r * tile_rows - RADIUS)
        inside = (k_col >= 0) & (k_col < n_col * tile_cols) & (k_row >= 0) & (k_row < n_row * tile_rows)
        return jnp.where(near & inside, 0.0, -1e30)

    middle = (RADIUS, mid_rows, RADIUS, bias_mid)
    edges = (
        (0, RADIUS, 0, bias_edge.at[0]),
        (tile_rows - RADIUS, RADIUS, 2 * RADIUS, bias_edge.at[1]),
    )
    for q_start, q_rows, k_start, mask in (middle,) + edges:
        mask[...] = allowed(q_start, q_rows, k_start)

    def w_copy(owner, k, sem, **where):
        rows = pl.ds(pl.multiple_of(owner * shard, shard), shard)
        place = w_buf.at[k, rows]
        return remote(place, place, sem, w_recv.at[owner, k], **where)

    def onward_copy(row, k):
        return w_copy(row * n_col + c, k, w_send.at[row, k], row=onward)

    def back_copy(row, k):
        return w_copy(row * n_col + c, k, w_back.at[row, k], row=mate)

    def side_copy(row, k, step):
        return w_copy(row * n_col + c, k, w_side.at[step - 1, row, k], col=col_of(step))

    def spread(row, k):
        for step in range(1, n_col):
            side_copy(row, k, step).start()

    def own_chunk(k):
        gossip(k).wait_recv()
        gossip(k).wait_send()

        @pl.when(k + AHEAD < CHUNKS)
        def _():
            gossip(k + AHEAD).start()

        columns = pl.ds(pl.multiple_of(k * cut, cut), cut)
        both = o_own[:, columns].astype(F32) + o_peer[k].astype(F32)
        w_buf[k, pl.ds(pl.multiple_of(me * shard, shard), shard), :] = (0.5 * both).astype(BF16)
        onward_copy(r, k).start()
        pl.when(is_inner | (k < OUTER))(lambda: spread(r, k))
        pl.when(is_inner & (k < OUTER))(lambda: back_copy(r, k).start())

    def hand_on(row, k):
        onward_copy(row, k).wait_recv()
        spread(row, k)

    def mate_chunk(k):
        @pl.when(is_inner)
        def _():
            onward_copy(mate, k).wait_recv()
            onward_copy(mate, k).start()
            spread(mate, k)

    scale = 1.0 / math.sqrt(HDIM)

    def attend(parts):
        def lanes(head):
            return pl.ds(pl.multiple_of(head * HDIM, HDIM), HDIM)

        def near_rows(which, head, k_start):
            return kv_buf[which, pl.ds(k_start, tile_rows), :, lanes(head)].reshape(tile_rows * wide, HDIM)

        scores = []
        for head, (q_start, q_rows, k_start, mask) in parts:
            query = q_buf[pl.ds(q_start, q_rows), :, lanes(head)].reshape(q_rows * tile_cols, HDIM)
            score = lax.dot_general(
                query, near_rows(0, head, k_start), (((1,), (1,)), ((), ())), preferred_element_type=F32
            )
            scores.append(score + mask[...])
        tops = [jnp.max(score, axis=1, keepdims=True) for score in scores]
        weights = [jnp.exp((score - top) * scale) for score, top in zip(scores, tops)]
        totals = [jnp.sum(weight, axis=1, keepdims=True) for weight in weights]
        sums = [
            jnp.dot(weight.astype(BF16), near_rows(1, head, k_start), preferred_element_type=F32)
            for weight, (head, (_, _, k_start, _)) in zip(weights, parts)
        ]
        means = [(part / total).astype(BF16) for part, total in zip(sums, totals)]
        for mean, (head, (q_start, q_rows, _, _)) in zip(means, parts):
            att[pl.ds(q_start * tile_cols, q_rows * tile_cols), lanes(head)] = mean

    loads[1].wait()
    own_chunk(0)
    loads[3].wait()
    loads[4].wait()
    for i in range(len(sides)):
        side(i).wait_recv()

    att_parts = (
        (RADIUS * tile_cols, mid_rows * tile_cols),
        (0, RADIUS * tile_cols),
        ((tile_rows - RADIUS) * tile_cols, RADIUS * tile_cols),
    )

    def att_copy(i):
        start, count = att_parts[i]
        return remote(
            att.at[pl.ds(start, count)], att.at[pl.ds(tokens + start, count)],
            att_send.at[i], att_recv.at[i], row=mate,
        )

    quarter = heads // 4

    def attend_middle(i):
        attend([(head, middle) for head in range(i * quarter, (i + 1) * quarter)])

    own_chunk(1)
    attend_middle(0)
    own_chunk(2)
    attend_middle(1)

    @pl.when(has_down)
    def _():
        halo(0).wait_recv()
        for i in range(len(sides)):
            corner(0, i).start()

    @pl.when(has_up)
    def _():
        halo(1).wait_recv()
        for i in range(len(sides)):
            corner(1, i).start()

    own_chunk(3)
    mate_chunk(0)
    attend_middle(2)
    own_chunk(4)
    mate_chunk(1)
    attend_middle(3)
    pl.when(is_outer)(lambda: att_copy(0).start())
    own_chunk(5)
    mate_chunk(2)

    def against_gate(cond):
        tall = jnp.broadcast_to(cond, (16, span)).astype(BF16)
        return jnp.dot(tall, g_buf[...], preferred_element_type=F32)[0:1]

    half = width // 2
    position = me * span + lax.broadcasted_iota(jnp.int32, (1, span), 1)
    freq_index = jnp.where(position < half, position, position - half).astype(F32)
    frequency = jnp.exp(-math.log(10000.0) * freq_index / half)
    ask.wait_recv()
    mixed_row = 0.5 * (pack_in[:, pl.ds(2 * slot, span)] + class_row(pack_in[:, pl.ds(0, span)]))
    angle = pack_in[:, pl.ds(slot, span)] * frequency
    embed = jnp.where(position < half, jnp.cos(angle), jnp.sin(angle))
    value = mixed_row.astype(BF16).astype(F32) + embed
    cond = (value / (1.0 + jnp.exp(-value))).astype(BF16).astype(F32)
    loads[2].wait()
    reply_out[:, pl.ds(0, width)] = against_gate(cond)
    reply_out[:, pl.ds(width, span)] = cond
    answer = remote(reply_out, reply_in, note_send.at[1], note_recv.at[1], dp=ahead)
    answer.start()


    for i in range(len(sides)):
        pl.when(has_down)(lambda i=i: corner(0, i).wait_recv())
        pl.when(has_up)(lambda i=i: corner(1, i).wait_recv())

    pairs = heads // 2

    def other_half(k):
        @pl.when(is_inner)
        def _():
            for row in (n_row - 1 - r, n_row - 1 - mate):
                hand_on(row, k)
                pl.when(k < OUTER)(lambda row=row: back_copy(row, k).start())

    def gate_copy(owner, step):
        other = lax.rem(me + step, group)
        return remote(
            gates.at[owner], gates.at[owner], gate_send.at[step - 1], gate_recv.at[owner],
            row=other // n_col, col=lax.rem(other, n_col),
        )

    def send_share():
        answer.wait_recv()
        share = 0.5 * (reply_in[:, pl.ds(0, width)] + against_gate(reply_in[:, pl.ds(width, span)]))
        gates[me] = share
        for step in range(1, group):
            gate_copy(me, step).start()

    def attend_pair(j, carry):
        @pl.when(j + 6 < CHUNKS)
        def _():
            own_chunk(j + 6)

        mate_chunk(j + 3)

        pl.when(j == 1)(send_share)
        pl.when(j > 1)(lambda: other_half(j - 2))
        attend([(2 * j + i, edge) for i in range(2) for edge in edges])
        return carry

    lax.fori_loop(0, pairs, attend_pair, 0)

    @pl.when(is_outer)
    def _():
        att_copy(1).start()
        att_copy(2).start()

    other_half(2)

    for step in range(1, group):
        owner = lax.rem(me + step, group)
        gate_copy(owner, step).wait_recv()
    gate = gates[0]
    for i in range(1, group):
        gate = gate + gates[i]
    for k in range(CHUNKS):
        gate_sum[k] = gate[:, k * cut : (k + 1) * cut]

    def out_copy(k):
        return pltpu.make_async_copy(
            out_buf.at[k], out_hbm.at[:, pl.ds(pl.multiple_of(k * cut, cut), cut)], out_sem.at[k]
        )

    def mate_copy(k):
        return remote(
            mate_out.at[k], out_hbm.at[:, pl.ds(pl.multiple_of(k * cut, cut), cut)],
            mate_send.at[k], mate_recv.at[k], row=mate,
        )

    def from_side(k):
        for row in range(n_row):
            for step in range(1, n_col):
                owner = row * n_col + col_of(step)
                w_copy(owner, k, w_side.at[step - 1, row, k], col=col_of(step)).wait_recv()

    def rows_of(count, k):
        product = jnp.dot(att[pl.ds(0, count)], w_buf[k], preferred_element_type=F32)
        return (gate_sum[k] * product).astype(BF16)

    def own_rows(k):
        out_buf[k] = rows_of(tokens, k)
        out_copy(k).start()

    def project(k, carry):
        pl.when((k + 1 >= 3) & (k + 1 < CHUNKS))(lambda: other_half(k + 1))
        from_side(k)

        @pl.when(k == OUTER)
        def _():
            for i in range(3):
                att_copy(i).wait_recv()

        @pl.when(k >= OUTER)
        def _():
            both = rows_of(2 * tokens, k)
            mate_out[k] = both[tokens:]
            mate_copy(k).start()
            out_buf[k] = both[:tokens]
            out_copy(k).start()

        pl.when(k < OUTER)(lambda: own_rows(k))
        pl.when(k == 4)(lambda: mate_chunk(CHUNKS - 1))
        return carry

    @pl.when(is_inner)
    def _():
        lax.fori_loop(0, CHUNKS, project, 0)

    @pl.when(is_outer)
    def _():
        for k in range(OUTER):
            for row in (mate, n_row - 1 - mate, n_row - 1 - r):
                back_copy(row, k).wait_recv()
                spread(row, k)
        for k in range(OUTER):
            from_side(k)
            own_rows(k)
        for k in range(OUTER, CHUNKS):
            mate_copy(k).wait_recv()

    def sent(k, carry):
        onward_copy(r, k).wait_send()

        @pl.when(is_inner | (k < OUTER))
        def _():
            out_copy(k).wait()
            for row in range(n_row):
                for step in range(1, n_col):
                    side_copy(row, k, step).wait_send()

        @pl.when(is_inner)
        def _():
            onward_copy(mate, k).wait_send()
            pl.when(k >= OUTER)(lambda: mate_copy(k).wait_send())

            @pl.when(k < OUTER)
            def _():
                for row in (r, n_row - 1 - r, n_row - 1 - mate):
                    back_copy(row, k).wait_send()

        return carry

    lax.fori_loop(0, CHUNKS, sent, 0)

    @pl.when(is_outer)
    def _():
        for i in range(3):
            att_copy(i).wait_send()

    pl.when(has_up)(lambda: halo(0).wait_send())
    pl.when(has_down)(lambda: halo(1).wait_send())
    for i in range(len(sides)):
        side(i).wait_send()
        pl.when(has_down)(lambda i=i: corner(0, i).wait_send())
        pl.when(has_up)(lambda i=i: corner(1, i).wait_send())
    ask.wait_send()
    answer.wait_send()
    for step in range(1, group):
        gate_copy(me, step).wait_send()


def layer(sizes, distance, number, queries, keyvals, out_weight, gate_weight, class_table, labels, timesteps):
    n_dp, n_row, n_col = sizes
    group = n_row * n_col
    _, tile_rows, tile_cols, inner = queries.shape
    _, shard, width = out_weight.shape
    span = gate_weight.shape[1]
    classes = class_table.shape[1]
    cut = width // CHUNKS
    slot = max(span, 128)
    n_side = 1 if n_col == 2 else 2
    wide = tile_cols * (1 + n_side)
    tokens = tile_rows * tile_cols
    n_k = tile_rows * wide
    dma = pltpu.SemaphoreType.DMA
    return pl.pallas_call(
        functools.partial(kernel, sizes, distance),
        out_shape=jax.ShapeDtypeStruct((tokens, width), BF16),
        in_specs=[pl.BlockSpec(memory_space=pl.ANY)] * 5 + [pl.BlockSpec(memory_space=pltpu.SMEM)] * 2,
        out_specs=pl.BlockSpec(memory_space=pl.ANY),
        scratch_shapes=[
            pltpu.VMEM((tile_rows, tile_cols, inner), BF16),
            pltpu.VMEM((2, tile_rows + 2 * RADIUS, wide, inner), BF16),
            pltpu.VMEM(((tile_rows - 2 * RADIUS) * tile_cols, n_k), F32),
            pltpu.VMEM((2, RADIUS * tile_cols, n_k), F32),
            pltpu.VMEM((2 * tokens, inner), BF16),
            pltpu.VMEM((shard, width), BF16),
            pltpu.VMEM((CHUNKS, shard, cut), BF16),
            pltpu.VMEM((CHUNKS, group * shard, cut), BF16),
            pltpu.VMEM((CHUNKS, tokens, cut), BF16),
            pltpu.VMEM((span, width), BF16),
            pltpu.VMEM((classes, span), BF16),
            pltpu.VMEM((1, 3 * slot), F32),
            pltpu.VMEM((1, 3 * slot), F32),
            pltpu.VMEM((1, width + slot), F32),
            pltpu.VMEM((1, width + slot), F32),
            pltpu.VMEM((group, 1, width), F32),
            pltpu.VMEM((CHUNKS, 1, cut), F32),
            pltpu.VMEM((CHUNKS, tokens, cut), BF16),
            dma((5,)),
            dma((CHUNKS,)),
            dma((CHUNKS,)),
            dma((CHUNKS,)),
            dma((n_row, CHUNKS)),
            dma((n_row, CHUNKS)),
            dma((n_col - 1, n_row, CHUNKS)),
            dma((group, CHUNKS)),
            dma((3,)),
            dma((3,)),
            dma((CHUNKS,)),
            dma((CHUNKS,)),
            dma((2,)),
            dma((2,)),
            dma((3, n_side)),
            dma((3, n_side)),
            dma((2,)),
            dma((2,)),
            dma((group - 1,)),
            dma((group,)),
        ],
        compiler_params=pltpu.CompilerParams(
            collective_id=number, has_side_effects=True, vmem_limit_bytes=48 * 2**20
        ),
        cost_estimate=pl.CostEstimate(flops=2 * tokens * inner * width, bytes_accessed=2**22, transcendentals=0),
        name=f"sublayer_distance_{distance}",
    )(queries, keyvals, out_weight, gate_weight, class_table, labels, timesteps)


def solution(mesh):
    sizes = tuple(mesh.shape[name] for name in ("dp", "row", "col"))
    bit_count = sizes[0].bit_length() - 1

    def local(queries, keyvals, out_weight, gate_weight, class_table, labels, timesteps, round_index):
        branches = [functools.partial(layer, sizes, 2**power, power) for power in range(bit_count)]
        operands = (queries, keyvals, out_weight, gate_weight, class_table, labels, timesteps)
        result = lax.switch(round_index[0] % bit_count, branches, *operands)
        return result.reshape(queries.shape[:3] + (out_weight.shape[2],))

    placed = (
        P("dp", "row", "col", None),
        P("dp", None, "row", "col", None),
        P("dp", ("row", "col"), None),
        P("dp", ("row", "col"), None),
        P("dp", None, ("row", "col")),
        P("dp"),
        P("dp"),
        P(),
    )
    return jax.shard_map(
        local, mesh=mesh, in_specs=placed, out_specs=P("dp", "row", "col", None), check_vma=False
    )
```

```python
import functools
import math

import jax
import jax.numpy as jnp
from jax import lax
from jax.experimental import pallas as pl
from jax.experimental.pallas import tpu as pltpu
from jax.sharding import PartitionSpec as P

HDIM = 128
RADIUS = 3
CHUNKS = 8
AHEAD = 3
OUTER = 5
MESH = pl.DeviceIdType.MESH
F32 = jnp.float32
BF16 = jnp.bfloat16


def remote(src, dst, send, recv, **where):
    return pltpu.make_async_remote_copy(
        src_ref=src, dst_ref=dst, send_sem=send, recv_sem=recv, device_id=where, device_id_type=MESH
    )


def kernel(
    sizes, distance,
    q_hbm, kv_hbm, o_hbm, g_hbm, t_hbm, label_ref, step_ref,
    out_hbm,
    q_buf, kv_buf, bias_mid, bias_edge, att, o_own, o_peer, w_buf, out_buf, g_buf, t_buf,
    pack_out, pack_in, reply_out, reply_in, gates, gate_sum, mate_out,
    local_sem, out_sem, gossip_send, gossip_recv, w_send, w_back, w_side, w_recv, att_send, att_recv, mate_send, mate_recv,
    halo_send, halo_recv, side_send, side_recv, note_send, note_recv, gate_send, gate_recv,
):
    n_dp, n_row, n_col = sizes
    group = n_row * n_col
    tile_rows, tile_cols, inner = kv_hbm.shape[2:]
    shard, width = o_hbm.shape[1:]
    cut = width // CHUNKS
    span = t_hbm.shape[2]
    slot = pack_out.shape[1] // 3
    classes = t_hbm.shape[1]
    heads = inner // HDIM
    sides = [1] if n_col == 2 else [n_col - 1, 1]
    wide = kv_buf.shape[2]

    p, r, c = lax.axis_index("dp"), lax.axis_index("row"), lax.axis_index("col")
    me = r * n_col + c
    ahead, behind = lax.rem(p + distance, n_dp), lax.rem(p + n_dp - distance, n_dp)
    has_up, has_down = r > 0, r < n_row - 1
    is_outer = (r == 0) | (r == n_row - 1)
    is_inner = jnp.logical_not(is_outer)
    mate = r + 1 - 2 * lax.rem(r, 2)
    onward = 1 + lax.rem(r, 2)
    tokens = tile_rows * tile_cols

    def col_of(step):
        return lax.rem(c + step, n_col)

    loads = [
        pltpu.make_async_copy(t_hbm.at[0], t_buf, local_sem.at[0]),
        pltpu.make_async_copy(o_hbm.at[0], o_own, local_sem.at[1]),
        pltpu.make_async_copy(g_hbm.at[0], g_buf, local_sem.at[2]),
        pltpu.make_async_copy(q_hbm.at[0], q_buf, local_sem.at[3]),
        pltpu.make_async_copy(
            kv_hbm.at[0], kv_buf.at[:, pl.ds(RADIUS, tile_rows), pl.ds(0, tile_cols)], local_sem.at[4]
        ),
    ]
    for load in loads:
        load.start()

    barrier = pltpu.get_barrier_semaphore()
    for step in range(1, group):
        other = lax.rem(me + step, group)
        pl.semaphore_signal(
            barrier, inc=1, device_id={"row": other // n_col, "col": lax.rem(other, n_col)}, device_id_type=MESH
        )
    pl.semaphore_signal(barrier, inc=1, device_id={"dp": ahead}, device_id_type=MESH)
    greeted = group
    if (2 * distance) % n_dp:
        pl.semaphore_signal(barrier, inc=1, device_id={"dp": behind}, device_id_type=MESH)
        greeted += 1
    def class_row(label):
        rows = lax.broadcasted_iota(jnp.int32, (classes, span), 0).astype(F32)
        table = t_buf[...].astype(F32)
        return jnp.sum(jnp.where(rows == label, table, 0.0), axis=0, keepdims=True)

    loads[0].wait()
    label_here = jnp.full((1, span), label_ref[0], jnp.int32).astype(F32)
    pack_out[:, pl.ds(0, span)] = label_here
    pack_out[:, pl.ds(slot, span)] = jnp.full((1, span), step_ref[0], jnp.int32).astype(F32)
    pack_out[:, pl.ds(2 * slot, span)] = class_row(label_here)
    pl.semaphore_wait(barrier, greeted)

    def halo(which):
        first, place = ((0, tile_rows + RADIUS), (tile_rows - RADIUS, 0))[which]
        return remote(
            kv_hbm.at[0, :, pl.ds(first, RADIUS)],
            kv_buf.at[:, pl.ds(place, RADIUS), pl.ds(0, tile_cols)],
            halo_send.at[which], halo_recv.at[which], row=(r - 1, r + 1)[which],
        )

    def side(i):
        return remote(
            kv_hbm.at[0],
            kv_buf.at[:, pl.ds(RADIUS, tile_rows), pl.ds((i + 1) * tile_cols, tile_cols)],
            side_send.at[0, i], side_recv.at[0, i], col=col_of(sides[i]),
        )

    def corner(which, i):
        place = (tile_rows + RADIUS, 0)[which]
        rows = pl.ds(place, RADIUS)
        return remote(
            kv_buf.at[:, rows, pl.ds(0, tile_cols)],
            kv_buf.at[:, rows, pl.ds((i + 1) * tile_cols, tile_cols)],
            side_send.at[1 + which, i], side_recv.at[1 + which, i], col=col_of(sides[i]),
        )

    def gossip(k):
        columns = pl.ds(k * cut, cut) if isinstance(k, int) else pl.ds(pl.multiple_of(k * cut, cut), cut)
        return remote(o_hbm.at[0, :, columns], o_peer.at[k], gossip_send.at[k], gossip_recv.at[k], dp=ahead)

    ask = remote(pack_out, pack_in, note_send.at[0], note_recv.at[0], dp=behind)
    ask.start()
    for k in range(AHEAD):
        gossip(k).start()
    pl.when(has_up)(lambda: halo(0).start())
    pl.when(has_down)(lambda: halo(1).start())
    for i in range(len(sides)):
        side(i).start()

    edge = jnp.zeros((2, RADIUS, wide, inner), BF16)

    @pl.when(jnp.logical_not(has_up))
    def _():
        kv_buf[:, pl.ds(0, RADIUS)] = edge

    @pl.when(jnp.logical_not(has_down))
    def _():
        kv_buf[:, pl.ds(tile_rows + RADIUS, RADIUS)] = edge

    blocks = wide // tile_cols
    mid_rows = tile_rows - 2 * RADIUS

    def allowed(q_start, q_rows, k_start):
        extent = (q_rows * tile_cols, tile_rows * wide)
        q_index = lax.broadcasted_iota(jnp.int32, extent, 0)
        k_index = lax.broadcasted_iota(jnp.int32, extent, 1)
        q_row, q_col = q_start + q_index // tile_cols, lax.rem(q_index, tile_cols)
        k_block = k_index // tile_cols
        k_row = (k_block * -(-512 // blocks)) // 512
        k_block = k_block - k_row * blocks
        k_row = k_row + k_start
        k_col = lax.rem(k_index, tile_cols)
        if n_col == 2:
            k_shift = jnp.where(k_block == 1, 1 - 2 * c, 0)
        else:
            k_shift = jnp.where(k_block == 1, 1, jnp.where(k_block == 2, -1, 0))
        k_col = k_col + k_shift * tile_cols
        near = (jnp.abs(k_col - q_col) <= RADIUS) & (k_row >= q_row) & (k_row <= q_row + 2 * RADIUS)
        k_col = k_col + c * tile_cols
        k_row = k_row + (r * tile_rows - RADIUS)
        inside = (k_col >= 0) & (k_col < n_col * tile_cols) & (k_row >= 0) & (k_row < n_row * tile_rows)
        return jnp.where(near & inside, 0.0, -1e30)

    middle = (RADIUS, mid_rows, RADIUS, bias_mid)
    edges = (
        (0, RADIUS, 0, bias_edge.at[0]),
        (tile_rows - RADIUS, RADIUS, 2 * RADIUS, bias_edge.at[1]),
    )
    for q_start, q_rows, k_start, mask in (middle,) + edges:
        mask[...] = allowed(q_start, q_rows, k_start)

    def w_copy(owner, k, sem, **where):
        rows = pl.ds(pl.multiple_of(owner * shard, shard), shard)
        place = w_buf.at[k, rows]
        return remote(place, place, sem, w_recv.at[owner, k], **where)

    def onward_copy(row, k):
        return w_copy(row * n_col + c, k, w_send.at[row, k], row=onward)

    def back_copy(row, k):
        return w_copy(row * n_col + c, k, w_back.at[row, k], row=mate)

    def side_copy(row, k, step):
        return w_copy(row * n_col + c, k, w_side.at[step - 1, row, k], col=col_of(step))

    def spread(row, k):
        for step in range(1, n_col):
            side_copy(row, k, step).start()

    def own_chunk(k):
        gossip(k).wait_recv()
        gossip(k).wait_send()

        @pl.when(k + AHEAD < CHUNKS)
        def _():
            gossip(k + AHEAD).start()

        columns = pl.ds(pl.multiple_of(k * cut, cut), cut)
        both = o_own[:, columns].astype(F32) + o_peer[k].astype(F32)
        w_buf[k, pl.ds(pl.multiple_of(me * shard, shard), shard), :] = (0.5 * both).astype(BF16)
        onward_copy(r, k).start()
        pl.when(is_inner | (k < OUTER))(lambda: spread(r, k))
        pl.when(is_inner & (k < OUTER))(lambda: back_copy(r, k).start())

    def hand_on(row, k):
        onward_copy(row, k).wait_recv()
        spread(row, k)

    def mate_chunk(k):
        @pl.when(is_inner)
        def _():
            onward_copy(mate, k).wait_recv()
            onward_copy(mate, k).start()
            spread(mate, k)

    scale = 1.0 / math.sqrt(HDIM)

    def attend(parts):
        def lanes(head):
            return pl.ds(pl.multiple_of(head * HDIM, HDIM), HDIM)

        def near_rows(which, head, k_start):
            return kv_buf[which, pl.ds(k_start, tile_rows), :, lanes(head)].reshape(tile_rows * wide, HDIM)

        scores = []
        for head, (q_start, q_rows, k_start, mask) in parts:
            query = q_buf[pl.ds(q_start, q_rows), :, lanes(head)].reshape(q_rows * tile_cols, HDIM)
            score = lax.dot_general(
                query, near_rows(0, head, k_start), (((1,), (1,)), ((), ())), preferred_element_type=F32
            )
            scores.append(score + mask[...])
        tops = [jnp.max(score, axis=1, keepdims=True) for score in scores]
        weights = [jnp.exp((score - top) * scale) for score, top in zip(scores, tops)]
        totals = [jnp.sum(weight, axis=1, keepdims=True) for weight in weights]
        sums = [
            jnp.dot(weight.astype(BF16), near_rows(1, head, k_start), preferred_element_type=F32)
            for weight, (head, (_, _, k_start, _)) in zip(weights, parts)
        ]
        means = [(part / total).astype(BF16) for part, total in zip(sums, totals)]
        for mean, (head, (q_start, q_rows, _, _)) in zip(means, parts):
            att[pl.ds(q_start * tile_cols, q_rows * tile_cols), lanes(head)] = mean

    loads[1].wait()
    own_chunk(0)
    loads[3].wait()
    loads[4].wait()
    for i in range(len(sides)):
        side(i).wait_recv()

    att_parts = (
        (RADIUS * tile_cols, mid_rows * tile_cols),
        (0, RADIUS * tile_cols),
        ((tile_rows - RADIUS) * tile_cols, RADIUS * tile_cols),
    )

    def att_copy(i):
        start, count = att_parts[i]
        return remote(
            att.at[pl.ds(start, count)], att.at[pl.ds(tokens + start, count)],
            att_send.at[i], att_recv.at[i], row=mate,
        )

    quarter = heads // 4

    def attend_middle(i):
        attend([(head, middle) for head in range(i * quarter, (i + 1) * quarter)])

    own_chunk(1)
    attend_middle(0)
    own_chunk(2)
    attend_middle(1)

    @pl.when(has_down)
    def _():
        halo(0).wait_recv()
        for i in range(len(sides)):
            corner(0, i).start()

    @pl.when(has_up)
    def _():
        halo(1).wait_recv()
        for i in range(len(sides)):
            corner(1, i).start()

    own_chunk(3)
    mate_chunk(0)
    attend_middle(2)
    own_chunk(4)
    mate_chunk(1)
    attend_middle(3)
    pl.when(is_outer)(lambda: att_copy(0).start())
    own_chunk(5)
    mate_chunk(2)

    def against_gate(cond):
        tall = jnp.broadcast_to(cond, (16, span)).astype(BF16)
        return jnp.dot(tall, g_buf[...], preferred_element_type=F32)[0:1]

    half = width // 2
    position = me * span + lax.broadcasted_iota(jnp.int32, (1, span), 1)
    freq_index = jnp.where(position < half, position, position - half).astype(F32)
    frequency = jnp.exp(-math.log(10000.0) * freq_index / half)
    ask.wait_recv()
    mixed_row = 0.5 * (pack_in[:, pl.ds(2 * slot, span)] + class_row(pack_in[:, pl.ds(0, span)]))
    angle = pack_in[:, pl.ds(slot, span)] * frequency
    embed = jnp.where(position < half, jnp.cos(angle), jnp.sin(angle))
    value = mixed_row.astype(BF16).astype(F32) + embed
    cond = (value / (1.0 + jnp.exp(-value))).astype(BF16).astype(F32)
    loads[2].wait()
    reply_out[:, pl.ds(0, width)] = against_gate(cond)
    reply_out[:, pl.ds(width, span)] = cond
    answer = remote(reply_out, reply_in, note_send.at[1], note_recv.at[1], dp=ahead)
    answer.start()


    for i in range(len(sides)):
        pl.when(has_down)(lambda i=i: corner(0, i).wait_recv())
        pl.when(has_up)(lambda i=i: corner(1, i).wait_recv())

    pairs = heads // 2

    def other_half(k):
        @pl.when(is_inner)
        def _():
            for row in (n_row - 1 - r, n_row - 1 - mate):
                hand_on(row, k)
                pl.when(k < OUTER)(lambda row=row: back_copy(row, k).start())

    def gate_copy(owner, step):
        other = lax.rem(me + step, group)
        return remote(
            gates.at[owner], gates.at[owner], gate_send.at[step - 1], gate_recv.at[owner],
            row=other // n_col, col=lax.rem(other, n_col),
        )

    def send_share():
        answer.wait_recv()
        share = 0.5 * (reply_in[:, pl.ds(0, width)] + against_gate(reply_in[:, pl.ds(width, span)]))
        gates[me] = share
        for step in range(1, group):
            gate_copy(me, step).start()

    def attend_pair(j, carry):
        @pl.when(j + 6 < CHUNKS)
        def _():
            own_chunk(j + 6)

        mate_chunk(j + 3)

        pl.when(j == 1)(send_share)
        other_half(j)
        attend([(2 * j + i, edge) for i in range(2) for edge in edges])
        return carry

    lax.fori_loop(0, pairs, attend_pair, 0)

    @pl.when(is_outer)
    def _():
        att_copy(1).start()
        att_copy(2).start()

    mate_chunk(CHUNKS - 1)

    for step in range(1, group):
        owner = lax.rem(me + step, group)
        gate_copy(owner, step).wait_recv()
    gate = gates[0]
    for i in range(1, group):
        gate = gate + gates[i]
    for k in range(CHUNKS):
        gate_sum[k] = gate[:, k * cut : (k + 1) * cut]

    def out_copy(k):
        return pltpu.make_async_copy(
            out_buf.at[k], out_hbm.at[:, pl.ds(pl.multiple_of(k * cut, cut), cut)], out_sem.at[k]
        )

    def mate_copy(k):
        return remote(
            mate_out.at[k], out_hbm.at[:, pl.ds(pl.multiple_of(k * cut, cut), cut)],
            mate_send.at[k], mate_recv.at[k], row=mate,
        )

    def from_side(k):
        for row in range(n_row):
            for step in range(1, n_col):
                owner = row * n_col + col_of(step)
                w_copy(owner, k, w_side.at[step - 1, row, k], col=col_of(step)).wait_recv()

    def rows_of(count, k):
        product = jnp.dot(att[pl.ds(0, count)], w_buf[k], preferred_element_type=F32)
        return (gate_sum[k] * product).astype(BF16)

    def own_rows(k):
        out_buf[k] = rows_of(tokens, k)
        out_copy(k).start()

    def project(k, carry):
        pl.when((k + 1 >= pairs) & (k + 1 < CHUNKS))(lambda: other_half(k + 1))
        from_side(k)

        @pl.when(k == OUTER)
        def _():
            for i in range(3):
                att_copy(i).wait_recv()

        @pl.when(k >= OUTER)
        def _():
            both = rows_of(2 * tokens, k)
            mate_out[k] = both[tokens:]
            mate_copy(k).start()
            out_buf[k] = both[:tokens]
            out_copy(k).start()

        pl.when(k < OUTER)(lambda: own_rows(k))
        return carry

    @pl.when(is_inner)
    def _():
        lax.fori_loop(0, CHUNKS, project, 0)

    @pl.when(is_outer)
    def _():
        for k in range(OUTER + 1):
            if k < OUTER:
                for row in (mate, n_row - 1 - mate, n_row - 1 - r):
                    back_copy(row, k).wait_recv()
                    spread(row, k)
            if k > 0:
                from_side(k - 1)
                own_rows(k - 1)
        for k in range(OUTER, CHUNKS):
            mate_copy(k).wait_recv()

    def sent(k, carry):
        onward_copy(r, k).wait_send()

        @pl.when(is_inner | (k < OUTER))
        def _():
            out_copy(k).wait()
            for row in range(n_row):
                for step in range(1, n_col):
                    side_copy(row, k, step).wait_send()

        @pl.when(is_inner)
        def _():
            onward_copy(mate, k).wait_send()
            pl.when(k >= OUTER)(lambda: mate_copy(k).wait_send())

            @pl.when(k < OUTER)
            def _():
                for row in (r, n_row - 1 - r, n_row - 1 - mate):
                    back_copy(row, k).wait_send()

        return carry

    lax.fori_loop(0, CHUNKS, sent, 0)

    @pl.when(is_outer)
    def _():
        for i in range(3):
            att_copy(i).wait_send()

    pl.when(has_up)(lambda: halo(0).wait_send())
    pl.when(has_down)(lambda: halo(1).wait_send())
    for i in range(len(sides)):
        side(i).wait_send()
        pl.when(has_down)(lambda i=i: corner(0, i).wait_send())
        pl.when(has_up)(lambda i=i: corner(1, i).wait_send())
    ask.wait_send()
    answer.wait_send()
    for step in range(1, group):
        gate_copy(me, step).wait_send()


def layer(sizes, distance, number, queries, keyvals, out_weight, gate_weight, class_table, labels, timesteps):
    n_dp, n_row, n_col = sizes
    group = n_row * n_col
    _, tile_rows, tile_cols, inner = queries.shape
    _, shard, width = out_weight.shape
    span = gate_weight.shape[1]
    classes = class_table.shape[1]
    cut = width // CHUNKS
    slot = max(span, 128)
    n_side = 1 if n_col == 2 else 2
    wide = tile_cols * (1 + n_side)
    tokens = tile_rows * tile_cols
    n_k = tile_rows * wide
    dma = pltpu.SemaphoreType.DMA
    return pl.pallas_call(
        functools.partial(kernel, sizes, distance),
        out_shape=jax.ShapeDtypeStruct((tokens, width), BF16),
        in_specs=[pl.BlockSpec(memory_space=pl.ANY)] * 5 + [pl.BlockSpec(memory_space=pltpu.SMEM)] * 2,
        out_specs=pl.BlockSpec(memory_space=pl.ANY),
        scratch_shapes=[
            pltpu.VMEM((tile_rows, tile_cols, inner), BF16),
            pltpu.VMEM((2, tile_rows + 2 * RADIUS, wide, inner), BF16),
            pltpu.VMEM(((tile_rows - 2 * RADIUS) * tile_cols, n_k), F32),
            pltpu.VMEM((2, RADIUS * tile_cols, n_k), F32),
            pltpu.VMEM((2 * tokens, inner), BF16),
            pltpu.VMEM((shard, width), BF16),
            pltpu.VMEM((CHUNKS, shard, cut), BF16),
            pltpu.VMEM((CHUNKS, group * shard, cut), BF16),
            pltpu.VMEM((CHUNKS, tokens, cut), BF16),
            pltpu.VMEM((span, width), BF16),
            pltpu.VMEM((classes, span), BF16),
            pltpu.VMEM((1, 3 * slot), F32),
            pltpu.VMEM((1, 3 * slot), F32),
            pltpu.VMEM((1, width + slot), F32),
            pltpu.VMEM((1, width + slot), F32),
            pltpu.VMEM((group, 1, width), F32),
            pltpu.VMEM((CHUNKS, 1, cut), F32),
            pltpu.VMEM((CHUNKS, tokens, cut), BF16),
            dma((5,)),
            dma((CHUNKS,)),
            dma((CHUNKS,)),
            dma((CHUNKS,)),
            dma((n_row, CHUNKS)),
            dma((n_row, CHUNKS)),
            dma((n_col - 1, n_row, CHUNKS)),
            dma((group, CHUNKS)),
            dma((3,)),
            dma((3,)),
            dma((CHUNKS,)),
            dma((CHUNKS,)),
            dma((2,)),
            dma((2,)),
            dma((3, n_side)),
            dma((3, n_side)),
            dma((2,)),
            dma((2,)),
            dma((group - 1,)),
            dma((group,)),
        ],
        compiler_params=pltpu.CompilerParams(
            collective_id=number, has_side_effects=True, vmem_limit_bytes=48 * 2**20
        ),
        cost_estimate=pl.CostEstimate(flops=2 * tokens * inner * width, bytes_accessed=2**22, transcendentals=0),
        name=f"sublayer_distance_{distance}",
    )(queries, keyvals, out_weight, gate_weight, class_table, labels, timesteps)


def solution(mesh):
    sizes = tuple(mesh.shape[name] for name in ("dp", "row", "col"))
    bit_count = sizes[0].bit_length() - 1

    def local(queries, keyvals, out_weight, gate_weight, class_table, labels, timesteps, round_index):
        branches = [functools.partial(layer, sizes, 2**power, power) for power in range(bit_count)]
        operands = (queries, keyvals, out_weight, gate_weight, class_table, labels, timesteps)
        result = lax.switch(round_index[0] % bit_count, branches, *operands)
        return result.reshape(queries.shape[:3] + (out_weight.shape[2],))

    placed = (
        P("dp", "row", "col", None),
        P("dp", None, "row", "col", None),
        P("dp", ("row", "col"), None),
        P("dp", ("row", "col"), None),
        P("dp", None, ("row", "col")),
        P("dp"),
        P("dp"),
        P(),
    )
    return jax.shard_map(
        local, mesh=mesh, in_specs=placed, out_specs=P("dp", "row", "col", None), check_vma=False
    )
```

```python
import functools
import math

import jax
import jax.numpy as jnp
from jax import lax
from jax.experimental import pallas as pl
from jax.experimental.pallas import tpu as pltpu
from jax.sharding import PartitionSpec as P

HDIM = 128
RADIUS = 3
CHUNKS = 8
AHEAD = 3
OUTER = 5
MESH = pl.DeviceIdType.MESH
F32 = jnp.float32
BF16 = jnp.bfloat16


def remote(src, dst, send, recv, **where):
    return pltpu.make_async_remote_copy(
        src_ref=src, dst_ref=dst, send_sem=send, recv_sem=recv, device_id=where, device_id_type=MESH
    )


def kernel(
    sizes, distance,
    q_hbm, kv_hbm, o_hbm, g_hbm, t_hbm, label_ref, step_ref,
    out_hbm,
    q_buf, kv_buf, bias_mid, bias_edge, att, o_own, o_peer, w_buf, out_buf, g_buf, t_buf,
    pack_out, pack_in, reply_out, reply_in, gates, gate_sum, mate_out,
    local_sem, out_sem, gossip_send, gossip_recv, w_send, w_back, w_side, w_side_recv, w_recv, att_send, att_recv, mate_send, mate_recv,
    halo_send, halo_recv, side_send, side_recv, note_send, note_recv, gate_send, gate_recv,
):
    n_dp, n_row, n_col = sizes
    group = n_row * n_col
    tile_rows, tile_cols, inner = kv_hbm.shape[2:]
    shard, width = o_hbm.shape[1:]
    cut = width // CHUNKS
    span = t_hbm.shape[2]
    slot = pack_out.shape[1] // 3
    classes = t_hbm.shape[1]
    heads = inner // HDIM
    sides = [1] if n_col == 2 else [n_col - 1, 1]
    wide = kv_buf.shape[2]

    p, r, c = lax.axis_index("dp"), lax.axis_index("row"), lax.axis_index("col")
    me = r * n_col + c
    ahead, behind = lax.rem(p + distance, n_dp), lax.rem(p + n_dp - distance, n_dp)
    has_up, has_down = r > 0, r < n_row - 1
    is_outer = (r == 0) | (r == n_row - 1)
    is_inner = jnp.logical_not(is_outer)
    mate = r + 1 - 2 * lax.rem(r, 2)
    onward = 1 + lax.rem(r, 2)
    near = r - lax.rem(r, 2)
    far = n_row - 2 - near
    tokens = tile_rows * tile_cols

    def col_of(step):
        return lax.rem(c + step, n_col)

    loads = [
        pltpu.make_async_copy(t_hbm.at[0], t_buf, local_sem.at[0]),
        pltpu.make_async_copy(o_hbm.at[0], o_own, local_sem.at[1]),
        pltpu.make_async_copy(g_hbm.at[0], g_buf, local_sem.at[2]),
        pltpu.make_async_copy(q_hbm.at[0], q_buf, local_sem.at[3]),
        pltpu.make_async_copy(
            kv_hbm.at[0], kv_buf.at[:, pl.ds(RADIUS, tile_rows), pl.ds(0, tile_cols)], local_sem.at[4]
        ),
    ]
    for load in loads:
        load.start()

    barrier = pltpu.get_barrier_semaphore()
    for step in range(1, group):
        other = lax.rem(me + step, group)
        pl.semaphore_signal(
            barrier, inc=1, device_id={"row": other // n_col, "col": lax.rem(other, n_col)}, device_id_type=MESH
        )
    pl.semaphore_signal(barrier, inc=1, device_id={"dp": ahead}, device_id_type=MESH)
    greeted = group
    if (2 * distance) % n_dp:
        pl.semaphore_signal(barrier, inc=1, device_id={"dp": behind}, device_id_type=MESH)
        greeted += 1
    def class_row(label):
        rows = lax.broadcasted_iota(jnp.int32, (classes, span), 0).astype(F32)
        table = t_buf[...].astype(F32)
        return jnp.sum(jnp.where(rows == label, table, 0.0), axis=0, keepdims=True)

    loads[0].wait()
    label_here = jnp.full((1, span), label_ref[0], jnp.int32).astype(F32)
    pack_out[:, pl.ds(0, span)] = label_here
    pack_out[:, pl.ds(slot, span)] = jnp.full((1, span), step_ref[0], jnp.int32).astype(F32)
    pack_out[:, pl.ds(2 * slot, span)] = class_row(label_here)
    pl.semaphore_wait(barrier, greeted)

    def halo(which):
        first, place = ((0, tile_rows + RADIUS), (tile_rows - RADIUS, 0))[which]
        return remote(
            kv_hbm.at[0, :, pl.ds(first, RADIUS)],
            kv_buf.at[:, pl.ds(place, RADIUS), pl.ds(0, tile_cols)],
            halo_send.at[which], halo_recv.at[which], row=(r - 1, r + 1)[which],
        )

    def side(i):
        return remote(
            kv_hbm.at[0],
            kv_buf.at[:, pl.ds(RADIUS, tile_rows), pl.ds((i + 1) * tile_cols, tile_cols)],
            side_send.at[0, i], side_recv.at[0, i], col=col_of(sides[i]),
        )

    def corner(which, i):
        place = (tile_rows + RADIUS, 0)[which]
        rows = pl.ds(place, RADIUS)
        return remote(
            kv_buf.at[:, rows, pl.ds(0, tile_cols)],
            kv_buf.at[:, rows, pl.ds((i + 1) * tile_cols, tile_cols)],
            side_send.at[1 + which, i], side_recv.at[1 + which, i], col=col_of(sides[i]),
        )

    def gossip(k):
        columns = pl.ds(k * cut, cut) if isinstance(k, int) else pl.ds(pl.multiple_of(k * cut, cut), cut)
        return remote(o_hbm.at[0, :, columns], o_peer.at[k], gossip_send.at[k], gossip_recv.at[k], dp=ahead)

    ask = remote(pack_out, pack_in, note_send.at[0], note_recv.at[0], dp=behind)
    ask.start()
    for k in range(AHEAD):
        gossip(k).start()
    pl.when(has_up)(lambda: halo(0).start())
    pl.when(has_down)(lambda: halo(1).start())
    for i in range(len(sides)):
        side(i).start()

    edge = jnp.zeros((2, RADIUS, wide, inner), BF16)

    @pl.when(jnp.logical_not(has_up))
    def _():
        kv_buf[:, pl.ds(0, RADIUS)] = edge

    @pl.when(jnp.logical_not(has_down))
    def _():
        kv_buf[:, pl.ds(tile_rows + RADIUS, RADIUS)] = edge

    blocks = wide // tile_cols
    mid_rows = tile_rows - 2 * RADIUS

    def allowed(q_start, q_rows, k_start):
        extent = (q_rows * tile_cols, tile_rows * wide)
        q_index = lax.broadcasted_iota(jnp.int32, extent, 0)
        k_index = lax.broadcasted_iota(jnp.int32, extent, 1)
        q_row, q_col = q_start + q_index // tile_cols, lax.rem(q_index, tile_cols)
        k_block = k_index // tile_cols
        k_row = (k_block * -(-512 // blocks)) // 512
        k_block = k_block - k_row * blocks
        k_row = k_row + k_start
        k_col = lax.rem(k_index, tile_cols)
        if n_col == 2:
            k_shift = jnp.where(k_block == 1, 1 - 2 * c, 0)
        else:
            k_shift = jnp.where(k_block == 1, 1, jnp.where(k_block == 2, -1, 0))
        k_col = k_col + k_shift * tile_cols
        near = (jnp.abs(k_col - q_col) <= RADIUS) & (k_row >= q_row) & (k_row <= q_row + 2 * RADIUS)
        k_col = k_col + c * tile_cols
        k_row = k_row + (r * tile_rows - RADIUS)
        inside = (k_col >= 0) & (k_col < n_col * tile_cols) & (k_row >= 0) & (k_row < n_row * tile_rows)
        return jnp.where(near & inside, 0.0, -1e30)

    middle = (RADIUS, mid_rows, RADIUS, bias_mid)
    edges = (
        (0, RADIUS, 0, bias_edge.at[0]),
        (tile_rows - RADIUS, RADIUS, 2 * RADIUS, bias_edge.at[1]),
    )
    for q_start, q_rows, k_start, mask in (middle,) + edges:
        mask[...] = allowed(q_start, q_rows, k_start)

    def place(k, row, count, col):
        return w_buf.at[k, pl.ds(row, count), col]

    def onward_copy(row, k):
        here = place(k, row, 1, c)
        return remote(here, here, w_send.at[row, k], w_recv.at[row, k], row=onward)

    def back_copy(which, row, count, k):
        here = place(k, row, count, c)
        return remote(here, here, w_back.at[which, k], w_recv.at[row, k], row=mate)

    def side_copy(which, row, count, k, step):
        here = place(k, row, count, c)
        return remote(
            here, here, w_side.at[step - 1, which, k], w_side_recv.at[step - 1, which, k], col=col_of(step)
        )

    def spread(which, row, count, k):
        for step in range(1, n_col):
            side_copy(which, row, count, k, step).start()

    def from_side(which, row, count, k):
        for step in range(1, n_col):
            there = place(k, row, count, col_of(n_col - step))
            remote(
                there, there, w_side.at[step - 1, which, k], w_side_recv.at[step - 1, which, k], col=col_of(step)
            ).wait_recv()

    def own_chunk(k):
        gossip(k).wait_recv()
        gossip(k).wait_send()

        @pl.when(k + AHEAD < CHUNKS)
        def _():
            gossip(k + AHEAD).start()

        columns = pl.ds(pl.multiple_of(k * cut, cut), cut)
        both = o_own[:, columns].astype(F32) + o_peer[k].astype(F32)
        w_buf[k, r, c] = (0.5 * both).astype(BF16)
        onward_copy(r, k).start()
        pl.when(is_inner & (k < OUTER))(lambda: back_copy(0, r, 1, k).start())

    def mate_chunk(k):
        @pl.when(is_inner)
        def _():
            onward_copy(mate, k).wait_recv()
            onward_copy(mate, k).start()
            spread(0, near, 2, k)

    scale = 1.0 / math.sqrt(HDIM)

    def attend(parts):
        def lanes(head):
            return pl.ds(pl.multiple_of(head * HDIM, HDIM), HDIM)

        def near_rows(which, head, k_start):
            return kv_buf[which, pl.ds(k_start, tile_rows), :, lanes(head)].reshape(tile_rows * wide, HDIM)

        scores = []
        for head, (q_start, q_rows, k_start, mask) in parts:
            query = q_buf[pl.ds(q_start, q_rows), :, lanes(head)].reshape(q_rows * tile_cols, HDIM)
            score = lax.dot_general(
                query, near_rows(0, head, k_start), (((1,), (1,)), ((), ())), preferred_element_type=F32
            )
            scores.append(score + mask[...])
        tops = [jnp.max(score, axis=1, keepdims=True) for score in scores]
        weights = [jnp.exp((score - top) * scale) for score, top in zip(scores, tops)]
        ones = jnp.ones((tile_rows * wide, HDIM), BF16)
        sums = [
            jnp.dot(
                weight.astype(BF16),
                jnp.concatenate([near_rows(1, head, k_start), ones], axis=1),
                preferred_element_type=F32,
            )
            for weight, (head, (_, _, k_start, _)) in zip(weights, parts)
        ]
        means = [(both[:, :HDIM] / both[:, HDIM:]).astype(BF16) for both in sums]
        for mean, (head, (q_start, q_rows, _, _)) in zip(means, parts):
            att[pl.ds(q_start * tile_cols, q_rows * tile_cols), lanes(head)] = mean

    loads[1].wait()
    own_chunk(0)
    loads[3].wait()
    loads[4].wait()
    for i in range(len(sides)):
        side(i).wait_recv()

    att_parts = (
        (RADIUS * tile_cols, mid_rows * tile_cols),
        (0, RADIUS * tile_cols),
        ((tile_rows - RADIUS) * tile_cols, RADIUS * tile_cols),
    )

    def att_copy(i):
        start, count = att_parts[i]
        return remote(
            att.at[pl.ds(start, count)], att.at[pl.ds(tokens + start, count)],
            att_send.at[i], att_recv.at[i], row=mate,
        )

    quarter = heads // 4

    def attend_middle(i):
        attend([(head, middle) for head in range(i * quarter, (i + 1) * quarter)])

    own_chunk(1)
    attend_middle(0)
    own_chunk(2)
    attend_middle(1)

    @pl.when(has_down)
    def _():
        halo(0).wait_recv()
        for i in range(len(sides)):
            corner(0, i).start()

    @pl.when(has_up)
    def _():
        halo(1).wait_recv()
        for i in range(len(sides)):
            corner(1, i).start()

    own_chunk(3)
    mate_chunk(0)
    attend_middle(2)
    own_chunk(4)
    mate_chunk(1)
    attend_middle(3)
    pl.when(is_outer)(lambda: att_copy(0).start())
    own_chunk(5)
    mate_chunk(2)

    def against_gate(cond):
        tall = jnp.broadcast_to(cond, (16, span)).astype(BF16)
        return jnp.dot(tall, g_buf[...], preferred_element_type=F32)[0:1]

    half = width // 2
    position = me * span + lax.broadcasted_iota(jnp.int32, (1, span), 1)
    freq_index = jnp.where(position < half, position, position - half).astype(F32)
    frequency = jnp.exp(-math.log(10000.0) * freq_index / half)
    ask.wait_recv()
    mixed_row = 0.5 * (pack_in[:, pl.ds(2 * slot, span)] + class_row(pack_in[:, pl.ds(0, span)]))
    angle = pack_in[:, pl.ds(slot, span)] * frequency
    embed = jnp.where(position < half, jnp.cos(angle), jnp.sin(angle))
    value = mixed_row.astype(BF16).astype(F32) + embed
    cond = (value / (1.0 + jnp.exp(-value))).astype(BF16).astype(F32)
    loads[2].wait()
    reply_out[:, pl.ds(0, width)] = against_gate(cond)
    reply_out[:, pl.ds(width, span)] = cond
    answer = remote(reply_out, reply_in, note_send.at[1], note_recv.at[1], dp=ahead)
    answer.start()


    for i in range(len(sides)):
        pl.when(has_down)(lambda i=i: corner(0, i).wait_recv())
        pl.when(has_up)(lambda i=i: corner(1, i).wait_recv())

    pairs = heads // 2

    def other_half(k):
        @pl.when(is_inner)
        def _():
            onward_copy(n_row - 1 - r, k).wait_recv()
            onward_copy(n_row - 1 - mate, k).wait_recv()
            spread(1, far, 2, k)
            pl.when(k < OUTER)(lambda: back_copy(1, far, 2, k).start())

    def gate_copy(owner, step):
        other = lax.rem(me + step, group)
        return remote(
            gates.at[owner], gates.at[owner], gate_send.at[step - 1], gate_recv.at[owner],
            row=other // n_col, col=lax.rem(other, n_col),
        )

    def send_share():
        answer.wait_recv()
        share = 0.5 * (reply_in[:, pl.ds(0, width)] + against_gate(reply_in[:, pl.ds(width, span)]))
        gates[me] = share
        for step in range(1, group):
            gate_copy(me, step).start()

    def attend_pair(j, carry):
        @pl.when(j + 6 < CHUNKS)
        def _():
            own_chunk(j + 6)

        mate_chunk(j + 3)

        pl.when(j == 1)(send_share)
        other_half(j)
        attend([(2 * j + i, edge) for i in range(2) for edge in edges])
        return carry

    lax.fori_loop(0, pairs, attend_pair, 0)

    @pl.when(is_outer)
    def _():
        att_copy(1).start()
        att_copy(2).start()

    mate_chunk(CHUNKS - 1)

    for step in range(1, group):
        owner = lax.rem(me + step, group)
        gate_copy(owner, step).wait_recv()
    gate = gates[0]
    for i in range(1, group):
        gate = gate + gates[i]
    for k in range(CHUNKS):
        gate_sum[k] = gate[:, k * cut : (k + 1) * cut]

    def out_copy(k):
        return pltpu.make_async_copy(
            out_buf.at[k], out_hbm.at[:, pl.ds(pl.multiple_of(k * cut, cut), cut)], out_sem.at[k]
        )

    def mate_copy(k):
        return remote(
            mate_out.at[k], out_hbm.at[:, pl.ds(pl.multiple_of(k * cut, cut), cut)],
            mate_send.at[k], mate_recv.at[k], row=mate,
        )

    def rows_of(count, k):
        product = jnp.dot(att[pl.ds(0, count)], w_buf[k].reshape(inner, cut), preferred_element_type=F32)
        return (gate_sum[k] * product).astype(BF16)

    def own_rows(k):
        out_buf[k] = rows_of(tokens, k)
        out_copy(k).start()

    def project(k, carry):
        pl.when((k + 1 >= pairs) & (k + 1 < CHUNKS))(lambda: other_half(k + 1))
        from_side(0, near, 2, k)
        from_side(1, far, 2, k)

        @pl.when(k == OUTER)
        def _():
            for i in range(3):
                att_copy(i).wait_recv()

        @pl.when(k >= OUTER)
        def _():
            both = rows_of(2 * tokens, k)
            mate_out[k] = both[tokens:]
            mate_copy(k).start()
            out_buf[k] = both[:tokens]
            out_copy(k).start()

        pl.when(k < OUTER)(lambda: own_rows(k))
        return carry

    @pl.when(is_inner)
    def _():
        lax.fori_loop(0, CHUNKS, project, 0)

    @pl.when(is_outer)
    def _():
        for k in range(OUTER + 1):
            if k < OUTER:
                back_copy(0, mate, 1, k).wait_recv()
                back_copy(1, far, 2, k).wait_recv()
                spread(0, 0, n_row, k)
            if k > 0:
                from_side(0, 0, n_row, k - 1)
                own_rows(k - 1)
        for k in range(OUTER, CHUNKS):
            mate_copy(k).wait_recv()

    def sent(k, carry):
        onward_copy(r, k).wait_send()

        pl.when(is_inner | (k < OUTER))(lambda: out_copy(k).wait())

        @pl.when(is_outer & (k < OUTER))
        def _():
            for step in range(1, n_col):
                side_copy(0, 0, n_row, k, step).wait_send()

        @pl.when(is_inner)
        def _():
            onward_copy(mate, k).wait_send()
            for step in range(1, n_col):
                side_copy(0, near, 2, k, step).wait_send()
                side_copy(1, far, 2, k, step).wait_send()
            pl.when(k >= OUTER)(lambda: mate_copy(k).wait_send())

            @pl.when(k < OUTER)
            def _():
                back_copy(0, r, 1, k).wait_send()
                back_copy(1, far, 2, k).wait_send()

        return carry

    lax.fori_loop(0, CHUNKS, sent, 0)

    @pl.when(is_outer)
    def _():
        for i in range(3):
            att_copy(i).wait_send()

    pl.when(has_up)(lambda: halo(0).wait_send())
    pl.when(has_down)(lambda: halo(1).wait_send())
    for i in range(len(sides)):
        side(i).wait_send()
        pl.when(has_down)(lambda i=i: corner(0, i).wait_send())
        pl.when(has_up)(lambda i=i: corner(1, i).wait_send())
    ask.wait_send()
    answer.wait_send()
    for step in range(1, group):
        gate_copy(me, step).wait_send()


def layer(sizes, distance, number, queries, keyvals, out_weight, gate_weight, class_table, labels, timesteps):
    n_dp, n_row, n_col = sizes
    group = n_row * n_col
    _, tile_rows, tile_cols, inner = queries.shape
    _, shard, width = out_weight.shape
    span = gate_weight.shape[1]
    classes = class_table.shape[1]
    cut = width // CHUNKS
    slot = max(span, 128)
    n_side = 1 if n_col == 2 else 2
    wide = tile_cols * (1 + n_side)
    tokens = tile_rows * tile_cols
    n_k = tile_rows * wide
    dma = pltpu.SemaphoreType.DMA
    return pl.pallas_call(
        functools.partial(kernel, sizes, distance),
        out_shape=jax.ShapeDtypeStruct((tokens, width), BF16),
        in_specs=[pl.BlockSpec(memory_space=pl.ANY)] * 5 + [pl.BlockSpec(memory_space=pltpu.SMEM)] * 2,
        out_specs=pl.BlockSpec(memory_space=pl.ANY),
        scratch_shapes=[
            pltpu.VMEM((tile_rows, tile_cols, inner), BF16),
            pltpu.VMEM((2, tile_rows + 2 * RADIUS, wide, inner), BF16),
            pltpu.VMEM(((tile_rows - 2 * RADIUS) * tile_cols, n_k), F32),
            pltpu.VMEM((2, RADIUS * tile_cols, n_k), F32),
            pltpu.VMEM((2 * tokens, inner), BF16),
            pltpu.VMEM((shard, width), BF16),
            pltpu.VMEM((CHUNKS, shard, cut), BF16),
            pltpu.VMEM((CHUNKS, n_row, n_col, shard, cut), BF16),
            pltpu.VMEM((CHUNKS, tokens, cut), BF16),
            pltpu.VMEM((span, width), BF16),
            pltpu.VMEM((classes, span), BF16),
            pltpu.VMEM((1, 3 * slot), F32),
            pltpu.VMEM((1, 3 * slot), F32),
            pltpu.VMEM((1, width + slot), F32),
            pltpu.VMEM((1, width + slot), F32),
            pltpu.VMEM((group, 1, width), F32),
            pltpu.VMEM((CHUNKS, 1, cut), F32),
            pltpu.VMEM((CHUNKS, tokens, cut), BF16),
            dma((5,)),
            dma((CHUNKS,)),
            dma((CHUNKS,)),
            dma((CHUNKS,)),
            dma((n_row, CHUNKS)),
            dma((2, CHUNKS)),
            dma((n_col - 1, 2, CHUNKS)),
            dma((n_col - 1, 2, CHUNKS)),
            dma((n_row, CHUNKS)),
            dma((3,)),
            dma((3,)),
            dma((CHUNKS,)),
            dma((CHUNKS,)),
            dma((2,)),
            dma((2,)),
            dma((3, n_side)),
            dma((3, n_side)),
            dma((2,)),
            dma((2,)),
            dma((group - 1,)),
            dma((group,)),
        ],
        compiler_params=pltpu.CompilerParams(
            collective_id=number, has_side_effects=True, vmem_limit_bytes=48 * 2**20
        ),
        cost_estimate=pl.CostEstimate(flops=2 * tokens * inner * width, bytes_accessed=2**22, transcendentals=0),
        name=f"sublayer_distance_{distance}",
    )(queries, keyvals, out_weight, gate_weight, class_table, labels, timesteps)


def solution(mesh):
    sizes = tuple(mesh.shape[name] for name in ("dp", "row", "col"))
    bit_count = sizes[0].bit_length() - 1

    def local(queries, keyvals, out_weight, gate_weight, class_table, labels, timesteps, round_index):
        branches = [functools.partial(layer, sizes, 2**power, power) for power in range(bit_count)]
        operands = (queries, keyvals, out_weight, gate_weight, class_table, labels, timesteps)
        result = lax.switch(round_index[0] % bit_count, branches, *operands)
        return result.reshape(queries.shape[:3] + (out_weight.shape[2],))

    placed = (
        P("dp", "row", "col", None),
        P("dp", None, "row", "col", None),
        P("dp", ("row", "col"), None),
        P("dp", ("row", "col"), None),
        P("dp", None, ("row", "col")),
        P("dp"),
        P("dp"),
        P(),
    )
    return jax.shard_map(
        local, mesh=mesh, in_specs=placed, out_specs=P("dp", "row", "col", None), check_vma=False
    )
```

```python
import functools
import math

import jax
import jax.numpy as jnp
from jax import lax
from jax.experimental import pallas as pl
from jax.experimental.pallas import tpu as pltpu
from jax.sharding import PartitionSpec as P

HDIM = 128
RADIUS = 3
CHUNKS = 8
AHEAD = 3
OUTER = 5
MESH = pl.DeviceIdType.MESH
F32 = jnp.float32
BF16 = jnp.bfloat16


def remote(src, dst, send, recv, **where):
    return pltpu.make_async_remote_copy(
        src_ref=src, dst_ref=dst, send_sem=send, recv_sem=recv, device_id=where, device_id_type=MESH
    )


def kernel(
    sizes, distance,
    q_hbm, kv_hbm, o_hbm, g_hbm, t_hbm, label_ref, step_ref,
    out_hbm,
    q_buf, kv_buf, bias_mid, bias_edge, att, o_own, o_peer, w_buf, out_buf, g_buf, t_buf,
    pack_out, pack_in, reply_out, reply_in, gates, gate_sum, mate_out,
    local_sem, out_sem, gossip_send, gossip_recv, w_send, w_back, w_side, w_side_recv, w_recv, att_send, att_recv, mate_send, mate_recv,
    halo_send, halo_recv, side_send, side_recv, note_send, note_recv, gate_send, gate_recv,
):
    n_dp, n_row, n_col = sizes
    group = n_row * n_col
    tile_rows, tile_cols, inner = kv_hbm.shape[2:]
    shard, width = o_hbm.shape[1:]
    cut = width // CHUNKS
    span = t_hbm.shape[2]
    slot = pack_out.shape[1] // 3
    classes = t_hbm.shape[1]
    heads = inner // HDIM
    sides = [1] if n_col == 2 else [n_col - 1, 1]
    wide = kv_buf.shape[2]

    p, r, c = lax.axis_index("dp"), lax.axis_index("row"), lax.axis_index("col")
    me = r * n_col + c
    ahead, behind = lax.rem(p + distance, n_dp), lax.rem(p + n_dp - distance, n_dp)
    has_up, has_down = r > 0, r < n_row - 1
    is_outer = (r == 0) | (r == n_row - 1)
    is_inner = jnp.logical_not(is_outer)
    mate = r + 1 - 2 * lax.rem(r, 2)
    onward = 1 + lax.rem(r, 2)
    near = r - lax.rem(r, 2)
    far = n_row - 2 - near
    tokens = tile_rows * tile_cols

    def col_of(step):
        return lax.rem(c + step, n_col)

    loads = [
        pltpu.make_async_copy(t_hbm.at[0], t_buf, local_sem.at[0]),
        pltpu.make_async_copy(o_hbm.at[0], o_own, local_sem.at[1]),
        pltpu.make_async_copy(g_hbm.at[0], g_buf, local_sem.at[2]),
        pltpu.make_async_copy(q_hbm.at[0], q_buf, local_sem.at[3]),
        pltpu.make_async_copy(
            kv_hbm.at[0], kv_buf.at[:, pl.ds(RADIUS, tile_rows), pl.ds(0, tile_cols)], local_sem.at[4]
        ),
    ]
    for load in loads:
        load.start()

    barrier = pltpu.get_barrier_semaphore()
    for step in range(1, group):
        other = lax.rem(me + step, group)
        pl.semaphore_signal(
            barrier, inc=1, device_id={"row": other // n_col, "col": lax.rem(other, n_col)}, device_id_type=MESH
        )
    pl.semaphore_signal(barrier, inc=1, device_id={"dp": ahead}, device_id_type=MESH)
    greeted = group
    if (2 * distance) % n_dp:
        pl.semaphore_signal(barrier, inc=1, device_id={"dp": behind}, device_id_type=MESH)
        greeted += 1
    def class_row(label):
        rows = lax.broadcasted_iota(jnp.int32, (classes, span), 0).astype(F32)
        table = t_buf[...].astype(F32)
        return jnp.sum(jnp.where(rows == label, table, 0.0), axis=0, keepdims=True)

    loads[0].wait()
    label_here = jnp.full((1, span), label_ref[0], jnp.int32).astype(F32)
    pack_out[:, pl.ds(0, span)] = label_here
    pack_out[:, pl.ds(slot, span)] = jnp.full((1, span), step_ref[0], jnp.int32).astype(F32)
    pack_out[:, pl.ds(2 * slot, span)] = class_row(label_here)
    pl.semaphore_wait(barrier, greeted)

    def halo(which):
        first, place = ((0, tile_rows + RADIUS), (tile_rows - RADIUS, 0))[which]
        return remote(
            kv_hbm.at[0, :, pl.ds(first, RADIUS)],
            kv_buf.at[:, pl.ds(place, RADIUS), pl.ds(0, tile_cols)],
            halo_send.at[which], halo_recv.at[which], row=(r - 1, r + 1)[which],
        )

    def side(i):
        return remote(
            kv_hbm.at[0],
            kv_buf.at[:, pl.ds(RADIUS, tile_rows), pl.ds((i + 1) * tile_cols, tile_cols)],
            side_send.at[0, i], side_recv.at[0, i], col=col_of(sides[i]),
        )

    def corner(which, i):
        place = (tile_rows + RADIUS, 0)[which]
        rows = pl.ds(place, RADIUS)
        return remote(
            kv_buf.at[:, rows, pl.ds(0, tile_cols)],
            kv_buf.at[:, rows, pl.ds((i + 1) * tile_cols, tile_cols)],
            side_send.at[1 + which, i], side_recv.at[1 + which, i], col=col_of(sides[i]),
        )

    def gossip(k):
        columns = pl.ds(k * cut, cut) if isinstance(k, int) else pl.ds(pl.multiple_of(k * cut, cut), cut)
        return remote(o_hbm.at[0, :, columns], o_peer.at[k], gossip_send.at[k], gossip_recv.at[k], dp=ahead)

    ask = remote(pack_out, pack_in, note_send.at[0], note_recv.at[0], dp=behind)
    ask.start()
    for k in range(AHEAD):
        gossip(k).start()
    pl.when(has_up)(lambda: halo(0).start())
    pl.when(has_down)(lambda: halo(1).start())
    for i in range(len(sides)):
        side(i).start()

    edge = jnp.zeros((2, RADIUS, wide, inner), BF16)

    @pl.when(jnp.logical_not(has_up))
    def _():
        kv_buf[:, pl.ds(0, RADIUS)] = edge

    @pl.when(jnp.logical_not(has_down))
    def _():
        kv_buf[:, pl.ds(tile_rows + RADIUS, RADIUS)] = edge

    blocks = wide // tile_cols
    mid_rows = tile_rows - 2 * RADIUS

    def allowed(q_start, q_rows, k_start):
        extent = (q_rows * tile_cols, tile_rows * wide)
        q_index = lax.broadcasted_iota(jnp.int32, extent, 0)
        k_index = lax.broadcasted_iota(jnp.int32, extent, 1)
        q_row, q_col = q_start + q_index // tile_cols, lax.rem(q_index, tile_cols)
        k_block = k_index // tile_cols
        k_row = (k_block * -(-512 // blocks)) // 512
        k_block = k_block - k_row * blocks
        k_row = k_row + k_start
        k_col = lax.rem(k_index, tile_cols)
        if n_col == 2:
            k_shift = jnp.where(k_block == 1, 1 - 2 * c, 0)
        else:
            k_shift = jnp.where(k_block == 1, 1, jnp.where(k_block == 2, -1, 0))
        k_col = k_col + k_shift * tile_cols
        near = (jnp.abs(k_col - q_col) <= RADIUS) & (k_row >= q_row) & (k_row <= q_row + 2 * RADIUS)
        k_col = k_col + c * tile_cols
        k_row = k_row + (r * tile_rows - RADIUS)
        inside = (k_col >= 0) & (k_col < n_col * tile_cols) & (k_row >= 0) & (k_row < n_row * tile_rows)
        return jnp.where(near & inside, 0.0, -1e30)

    middle = (RADIUS, mid_rows, RADIUS, bias_mid)
    edges = (
        (0, RADIUS, 0, bias_edge.at[0]),
        (tile_rows - RADIUS, RADIUS, 2 * RADIUS, bias_edge.at[1]),
    )
    for q_start, q_rows, k_start, mask in (middle,) + edges:
        mask[...] = allowed(q_start, q_rows, k_start)

    def place(k, row, count, col):
        return w_buf.at[k, pl.ds(row, count), col]

    def onward_copy(row, k):
        here = place(k, row, 1, c)
        return remote(here, here, w_send.at[row, k], w_recv.at[row, k], row=onward)

    def back_copy(which, row, count, k):
        here = place(k, row, count, c)
        return remote(here, here, w_back.at[which, k], w_recv.at[row, k], row=mate)

    def side_copy(which, row, count, k, step):
        here = place(k, row, count, c)
        return remote(
            here, here, w_side.at[step - 1, which, k], w_side_recv.at[step - 1, which, k], col=col_of(step)
        )

    def spread(which, row, count, k):
        for step in range(1, n_col):
            side_copy(which, row, count, k, step).start()

    def from_side(which, row, count, k):
        for step in range(1, n_col):
            there = place(k, row, count, col_of(n_col - step))
            remote(
                there, there, w_side.at[step - 1, which, k], w_side_recv.at[step - 1, which, k], col=col_of(step)
            ).wait_recv()

    def own_chunk(k):
        gossip(k).wait_recv()
        gossip(k).wait_send()

        @pl.when(k + AHEAD < CHUNKS)
        def _():
            gossip(k + AHEAD).start()

        columns = pl.ds(pl.multiple_of(k * cut, cut), cut)
        both = o_own[:, columns].astype(F32) + o_peer[k].astype(F32)
        w_buf[k, r, c] = (0.5 * both).astype(BF16)
        onward_copy(r, k).start()
        pl.when(is_inner & (k < OUTER))(lambda: back_copy(0, r, 1, k).start())

    def mate_chunk(k):
        @pl.when(is_inner)
        def _():
            onward_copy(mate, k).wait_recv()
            onward_copy(mate, k).start()
            spread(0, near, 2, k)

    scale = 1.0 / math.sqrt(HDIM)

    def attend(parts):
        def lanes(head):
            return pl.ds(pl.multiple_of(head * HDIM, HDIM), HDIM)

        def near_rows(which, head, k_start):
            return kv_buf[which, pl.ds(k_start, tile_rows), :, lanes(head)].reshape(tile_rows * wide, HDIM)

        scores = []
        for head, (q_start, q_rows, k_start, mask) in parts:
            query = q_buf[pl.ds(q_start, q_rows), :, lanes(head)].reshape(q_rows * tile_cols, HDIM)
            score = lax.dot_general(
                query, near_rows(0, head, k_start), (((1,), (1,)), ((), ())), preferred_element_type=F32
            )
            scores.append(score + mask[...])
        tops = [jnp.max(score, axis=1, keepdims=True) for score in scores]
        weights = [jnp.exp((score - top) * scale) for score, top in zip(scores, tops)]
        ones = jnp.ones((tile_rows * wide, HDIM), BF16)
        sums = [
            jnp.dot(
                weight.astype(BF16),
                jnp.concatenate([near_rows(1, head, k_start), ones], axis=1),
                preferred_element_type=F32,
            )
            for weight, (head, (_, _, k_start, _)) in zip(weights, parts)
        ]
        means = [(both[:, :HDIM] / both[:, HDIM:]).astype(BF16) for both in sums]
        for mean, (head, (q_start, q_rows, _, _)) in zip(means, parts):
            att[pl.ds(q_start * tile_cols, q_rows * tile_cols), lanes(head)] = mean

    loads[1].wait()
    own_chunk(0)
    loads[3].wait()
    loads[4].wait()
    for i in range(len(sides)):
        side(i).wait_recv()

    att_parts = (
        (RADIUS * tile_cols, mid_rows * tile_cols),
        (0, RADIUS * tile_cols),
        ((tile_rows - RADIUS) * tile_cols, RADIUS * tile_cols),
    )

    def att_copy(i):
        start, count = att_parts[i]
        return remote(
            att.at[pl.ds(start, count)], att.at[pl.ds(tokens + start, count)],
            att_send.at[i], att_recv.at[i], row=mate,
        )

    quarter = heads // 4

    def middle_step(i, carry):
        own_chunk(i + 1)

        @pl.when(i == 2)
        def _():
            @pl.when(has_down)
            def _():
                halo(0).wait_recv()
                for i in range(len(sides)):
                    corner(0, i).start()

            @pl.when(has_up)
            def _():
                halo(1).wait_recv()
                for i in range(len(sides)):
                    corner(1, i).start()

        pl.when(i > 1)(lambda: mate_chunk(i - 2))
        attend([(i * quarter + n, middle) for n in range(quarter)])
        return carry

    lax.fori_loop(0, 4, middle_step, 0)
    pl.when(is_outer)(lambda: att_copy(0).start())
    own_chunk(5)
    mate_chunk(2)

    def against_gate(cond):
        tall = jnp.broadcast_to(cond, (16, span)).astype(BF16)
        return jnp.dot(tall, g_buf[...], preferred_element_type=F32)[0:1]

    half = width // 2
    position = me * span + lax.broadcasted_iota(jnp.int32, (1, span), 1)
    freq_index = jnp.where(position < half, position, position - half).astype(F32)
    frequency = jnp.exp(-math.log(10000.0) * freq_index / half)
    ask.wait_recv()
    mixed_row = 0.5 * (pack_in[:, pl.ds(2 * slot, span)] + class_row(pack_in[:, pl.ds(0, span)]))
    angle = pack_in[:, pl.ds(slot, span)] * frequency
    embed = jnp.where(position < half, jnp.cos(angle), jnp.sin(angle))
    value = mixed_row.astype(BF16).astype(F32) + embed
    cond = (value / (1.0 + jnp.exp(-value))).astype(BF16).astype(F32)
    loads[2].wait()
    reply_out[:, pl.ds(0, width)] = against_gate(cond)
    reply_out[:, pl.ds(width, span)] = cond
    answer = remote(reply_out, reply_in, note_send.at[1], note_recv.at[1], dp=ahead)
    answer.start()


    for i in range(len(sides)):
        pl.when(has_down)(lambda i=i: corner(0, i).wait_recv())
        pl.when(has_up)(lambda i=i: corner(1, i).wait_recv())

    pairs = heads // 2

    def other_half(k):
        @pl.when(is_inner)
        def _():
            onward_copy(n_row - 1 - r, k).wait_recv()
            onward_copy(n_row - 1 - mate, k).wait_recv()
            spread(1, far, 2, k)
            pl.when(k < OUTER)(lambda: back_copy(1, far, 2, k).start())

    def gate_copy(owner, step):
        other = lax.rem(me + step, group)
        return remote(
            gates.at[owner], gates.at[owner], gate_send.at[step - 1], gate_recv.at[owner],
            row=other // n_col, col=lax.rem(other, n_col),
        )

    def send_share():
        answer.wait_recv()
        share = 0.5 * (reply_in[:, pl.ds(0, width)] + against_gate(reply_in[:, pl.ds(width, span)]))
        gates[me] = share
        for step in range(1, group):
            gate_copy(me, step).start()

    def attend_pair(j, carry):
        @pl.when(j + 6 < CHUNKS)
        def _():
            own_chunk(j + 6)

        mate_chunk(j + 3)

        pl.when(j == 1)(send_share)
        other_half(j)
        attend([(2 * j + i, edge) for i in range(2) for edge in edges])
        return carry

    lax.fori_loop(0, pairs, attend_pair, 0)

    @pl.when(is_outer)
    def _():
        att_copy(1).start()
        att_copy(2).start()

    mate_chunk(CHUNKS - 1)

    for step in range(1, group):
        owner = lax.rem(me + step, group)
        gate_copy(owner, step).wait_recv()
    gate = gates[0]
    for i in range(1, group):
        gate = gate + gates[i]
    for k in range(CHUNKS):
        gate_sum[k] = gate[:, k * cut : (k + 1) * cut]

    def out_copy(k):
        return pltpu.make_async_copy(
            out_buf.at[k], out_hbm.at[:, pl.ds(pl.multiple_of(k * cut, cut), cut)], out_sem.at[k]
        )

    def mate_copy(k):
        return remote(
            mate_out.at[k], out_hbm.at[:, pl.ds(pl.multiple_of(k * cut, cut), cut)],
            mate_send.at[k], mate_recv.at[k], row=mate,
        )

    def rows_of(count, k):
        product = jnp.dot(att[pl.ds(0, count)], w_buf[k].reshape(inner, cut), preferred_element_type=F32)
        return (gate_sum[k] * product).astype(BF16)

    def own_rows(k):
        out_buf[k] = rows_of(tokens, k)
        out_copy(k).start()

    def project(k, carry):
        pl.when((k + 1 >= pairs) & (k + 1 < CHUNKS))(lambda: other_half(k + 1))
        from_side(0, near, 2, k)
        from_side(1, far, 2, k)

        @pl.when(k == OUTER)
        def _():
            for i in range(3):
                att_copy(i).wait_recv()

        @pl.when(k >= OUTER)
        def _():
            both = rows_of(2 * tokens, k)
            mate_out[k] = both[tokens:]
            mate_copy(k).start()
            out_buf[k] = both[:tokens]
            out_copy(k).start()

        pl.when(k < OUTER)(lambda: own_rows(k))
        return carry

    @pl.when(is_inner)
    def _():
        lax.fori_loop(0, CHUNKS, project, 0)

    @pl.when(is_outer)
    def _():
        def outer_step(k, carry):
            @pl.when(k < OUTER)
            def _():
                back_copy(0, mate, 1, k).wait_recv()
                back_copy(1, far, 2, k).wait_recv()
                spread(0, 0, n_row, k)

            @pl.when(k > 0)
            def _():
                from_side(0, 0, n_row, k - 1)
                own_rows(k - 1)

            return carry

        lax.fori_loop(0, OUTER + 1, outer_step, 0)
        for k in range(OUTER, CHUNKS):
            mate_copy(k).wait_recv()

    def sent(k, carry):
        onward_copy(r, k).wait_send()

        pl.when(is_inner | (k < OUTER))(lambda: out_copy(k).wait())

        @pl.when(is_outer & (k < OUTER))
        def _():
            for step in range(1, n_col):
                side_copy(0, 0, n_row, k, step).wait_send()

        @pl.when(is_inner)
        def _():
            onward_copy(mate, k).wait_send()
            for step in range(1, n_col):
                side_copy(0, near, 2, k, step).wait_send()
                side_copy(1, far, 2, k, step).wait_send()
            pl.when(k >= OUTER)(lambda: mate_copy(k).wait_send())

            @pl.when(k < OUTER)
            def _():
                back_copy(0, r, 1, k).wait_send()
                back_copy(1, far, 2, k).wait_send()

        return carry

    lax.fori_loop(0, CHUNKS, sent, 0)

    @pl.when(is_outer)
    def _():
        for i in range(3):
            att_copy(i).wait_send()

    pl.when(has_up)(lambda: halo(0).wait_send())
    pl.when(has_down)(lambda: halo(1).wait_send())
    for i in range(len(sides)):
        side(i).wait_send()
        pl.when(has_down)(lambda i=i: corner(0, i).wait_send())
        pl.when(has_up)(lambda i=i: corner(1, i).wait_send())
    ask.wait_send()
    answer.wait_send()
    for step in range(1, group):
        gate_copy(me, step).wait_send()


def layer(sizes, distance, number, queries, keyvals, out_weight, gate_weight, class_table, labels, timesteps):
    n_dp, n_row, n_col = sizes
    group = n_row * n_col
    _, tile_rows, tile_cols, inner = queries.shape
    _, shard, width = out_weight.shape
    span = gate_weight.shape[1]
    classes = class_table.shape[1]
    cut = width // CHUNKS
    slot = max(span, 128)
    n_side = 1 if n_col == 2 else 2
    wide = tile_cols * (1 + n_side)
    tokens = tile_rows * tile_cols
    n_k = tile_rows * wide
    dma = pltpu.SemaphoreType.DMA
    return pl.pallas_call(
        functools.partial(kernel, sizes, distance),
        out_shape=jax.ShapeDtypeStruct((tokens, width), BF16),
        in_specs=[pl.BlockSpec(memory_space=pl.ANY)] * 5 + [pl.BlockSpec(memory_space=pltpu.SMEM)] * 2,
        out_specs=pl.BlockSpec(memory_space=pl.ANY),
        scratch_shapes=[
            pltpu.VMEM((tile_rows, tile_cols, inner), BF16),
            pltpu.VMEM((2, tile_rows + 2 * RADIUS, wide, inner), BF16),
            pltpu.VMEM(((tile_rows - 2 * RADIUS) * tile_cols, n_k), F32),
            pltpu.VMEM((2, RADIUS * tile_cols, n_k), F32),
            pltpu.VMEM((2 * tokens, inner), BF16),
            pltpu.VMEM((shard, width), BF16),
            pltpu.VMEM((CHUNKS, shard, cut), BF16),
            pltpu.VMEM((CHUNKS, n_row, n_col, shard, cut), BF16),
            pltpu.VMEM((CHUNKS, tokens, cut), BF16),
            pltpu.VMEM((span, width), BF16),
            pltpu.VMEM((classes, span), BF16),
            pltpu.VMEM((1, 3 * slot), F32),
            pltpu.VMEM((1, 3 * slot), F32),
            pltpu.VMEM((1, width + slot), F32),
            pltpu.VMEM((1, width + slot), F32),
            pltpu.VMEM((group, 1, width), F32),
            pltpu.VMEM((CHUNKS, 1, cut), F32),
            pltpu.VMEM((CHUNKS, tokens, cut), BF16),
            dma((5,)),
            dma((CHUNKS,)),
            dma((CHUNKS,)),
            dma((CHUNKS,)),
            dma((n_row, CHUNKS)),
            dma((2, CHUNKS)),
            dma((n_col - 1, 2, CHUNKS)),
            dma((n_col - 1, 2, CHUNKS)),
            dma((n_row, CHUNKS)),
            dma((3,)),
            dma((3,)),
            dma((CHUNKS,)),
            dma((CHUNKS,)),
            dma((2,)),
            dma((2,)),
            dma((3, n_side)),
            dma((3, n_side)),
            dma((2,)),
            dma((2,)),
            dma((group - 1,)),
            dma((group,)),
        ],
        compiler_params=pltpu.CompilerParams(
            collective_id=number, has_side_effects=True, vmem_limit_bytes=48 * 2**20
        ),
        cost_estimate=pl.CostEstimate(flops=2 * tokens * inner * width, bytes_accessed=2**22, transcendentals=0),
        name=f"sublayer_distance_{distance}",
    )(queries, keyvals, out_weight, gate_weight, class_table, labels, timesteps)


def solution(mesh):
    sizes = tuple(mesh.shape[name] for name in ("dp", "row", "col"))
    bit_count = sizes[0].bit_length() - 1

    def local(queries, keyvals, out_weight, gate_weight, class_table, labels, timesteps, round_index):
        branches = [functools.partial(layer, sizes, 2**power, power) for power in range(bit_count)]
        operands = (queries, keyvals, out_weight, gate_weight, class_table, labels, timesteps)
        result = lax.switch(round_index[0] % bit_count, branches, *operands)
        return result.reshape(queries.shape[:3] + (out_weight.shape[2],))

    placed = (
        P("dp", "row", "col", None),
        P("dp", None, "row", "col", None),
        P("dp", ("row", "col"), None),
        P("dp", ("row", "col"), None),
        P("dp", None, ("row", "col")),
        P("dp"),
        P("dp"),
        P(),
    )
    return jax.shard_map(
        local, mesh=mesh, in_specs=placed, out_specs=P("dp", "row", "col", None), check_vma=False
    )
```

```python
import functools
import math

import jax
import jax.numpy as jnp
from jax import lax
from jax.experimental import pallas as pl
from jax.experimental.pallas import tpu as pltpu
from jax.sharding import PartitionSpec as P

HDIM = 128
RADIUS = 3
CHUNKS = 8
AHEAD = 3
OUTER = 5
MESH = pl.DeviceIdType.MESH
F32 = jnp.float32
BF16 = jnp.bfloat16


def remote(src, dst, send, recv, **where):
    return pltpu.make_async_remote_copy(
        src_ref=src, dst_ref=dst, send_sem=send, recv_sem=recv, device_id=where, device_id_type=MESH
    )


def kernel(
    sizes, distance,
    q_hbm, kv_hbm, o_hbm, g_hbm, t_hbm, label_ref, step_ref,
    out_hbm,
    q_buf, kv_buf, bias_mid, bias_edge, att, o_own, o_peer, w_buf, out_buf, g_buf, t_buf,
    pack_out, pack_in, reply_out, reply_in, gates, gate_sum, mate_out,
    local_sem, out_sem, gossip_send, gossip_recv, w_send, w_back, w_side, w_side_recv, w_recv, att_send, att_recv, mate_send, mate_recv,
    halo_send, halo_recv, side_send, side_recv, note_send, note_recv, gate_send, gate_recv,
):
    n_dp, n_row, n_col = sizes
    group = n_row * n_col
    tile_rows, tile_cols, inner = kv_hbm.shape[2:]
    shard, width = o_hbm.shape[1:]
    cut = width // CHUNKS
    span = t_hbm.shape[2]
    slot = pack_out.shape[1] // 3
    classes = t_hbm.shape[1]
    heads = inner // HDIM
    sides = [1] if n_col == 2 else [n_col - 1, 1]
    wide = kv_buf.shape[2]

    p, r, c = lax.axis_index("dp"), lax.axis_index("row"), lax.axis_index("col")
    me = r * n_col + c
    ahead, behind = lax.rem(p + distance, n_dp), lax.rem(p + n_dp - distance, n_dp)
    has_up, has_down = r > 0, r < n_row - 1
    is_outer = (r == 0) | (r == n_row - 1)
    is_inner = jnp.logical_not(is_outer)
    mate = r + 1 - 2 * lax.rem(r, 2)
    onward = 1 + lax.rem(r, 2)
    near = r - lax.rem(r, 2)
    far = n_row - 2 - near
    tokens = tile_rows * tile_cols

    def col_of(step):
        return lax.rem(c + step, n_col)

    loads = [
        pltpu.make_async_copy(t_hbm.at[0], t_buf, local_sem.at[0]),
        pltpu.make_async_copy(o_hbm.at[0], o_own, local_sem.at[1]),
        pltpu.make_async_copy(g_hbm.at[0], g_buf, local_sem.at[2]),
        pltpu.make_async_copy(q_hbm.at[0], q_buf, local_sem.at[3]),
        pltpu.make_async_copy(
            kv_hbm.at[0], kv_buf.at[:, pl.ds(RADIUS, tile_rows), pl.ds(0, tile_cols)], local_sem.at[4]
        ),
    ]
    for load in loads:
        load.start()

    barrier = pltpu.get_barrier_semaphore()
    for step in range(1, group):
        other = lax.rem(me + step, group)
        pl.semaphore_signal(
            barrier, inc=1, device_id={"row": other // n_col, "col": lax.rem(other, n_col)}, device_id_type=MESH
        )
    pl.semaphore_signal(barrier, inc=1, device_id={"dp": ahead}, device_id_type=MESH)
    greeted = group
    if (2 * distance) % n_dp:
        pl.semaphore_signal(barrier, inc=1, device_id={"dp": behind}, device_id_type=MESH)
        greeted += 1
    def class_row(label):
        rows = lax.broadcasted_iota(jnp.int32, (classes, span), 0).astype(F32)
        table = t_buf[...].astype(F32)
        return jnp.sum(jnp.where(rows == label, table, 0.0), axis=0, keepdims=True)

    loads[0].wait()
    label_here = jnp.full((1, span), label_ref[0], jnp.int32).astype(F32)
    pack_out[:, pl.ds(0, span)] = label_here
    pack_out[:, pl.ds(slot, span)] = jnp.full((1, span), step_ref[0], jnp.int32).astype(F32)
    pack_out[:, pl.ds(2 * slot, span)] = class_row(label_here)
    pl.semaphore_wait(barrier, greeted)

    def halo(which):
        first, place = ((0, tile_rows + RADIUS), (tile_rows - RADIUS, 0))[which]
        return remote(
            kv_hbm.at[0, :, pl.ds(first, RADIUS)],
            kv_buf.at[:, pl.ds(place, RADIUS), pl.ds(0, tile_cols)],
            halo_send.at[which], halo_recv.at[which], row=(r - 1, r + 1)[which],
        )

    def side(i):
        return remote(
            kv_hbm.at[0],
            kv_buf.at[:, pl.ds(RADIUS, tile_rows), pl.ds((i + 1) * tile_cols, tile_cols)],
            side_send.at[0, i], side_recv.at[0, i], col=col_of(sides[i]),
        )

    def corner(which, i):
        place = (tile_rows + RADIUS, 0)[which]
        rows = pl.ds(place, RADIUS)
        return remote(
            kv_buf.at[:, rows, pl.ds(0, tile_cols)],
            kv_buf.at[:, rows, pl.ds((i + 1) * tile_cols, tile_cols)],
            side_send.at[1 + which, i], side_recv.at[1 + which, i], col=col_of(sides[i]),
        )

    def gossip(k):
        columns = pl.ds(k * cut, cut) if isinstance(k, int) else pl.ds(pl.multiple_of(k * cut, cut), cut)
        return remote(o_hbm.at[0, :, columns], o_peer.at[k], gossip_send.at[k], gossip_recv.at[k], dp=ahead)

    ask = remote(pack_out, pack_in, note_send.at[0], note_recv.at[0], dp=behind)
    ask.start()
    for k in range(AHEAD):
        gossip(k).start()
    pl.when(has_up)(lambda: halo(0).start())
    pl.when(has_down)(lambda: halo(1).start())
    for i in range(len(sides)):
        side(i).start()

    edge = jnp.zeros((2, RADIUS, wide, inner), BF16)

    @pl.when(jnp.logical_not(has_up))
    def _():
        kv_buf[:, pl.ds(0, RADIUS)] = edge

    @pl.when(jnp.logical_not(has_down))
    def _():
        kv_buf[:, pl.ds(tile_rows + RADIUS, RADIUS)] = edge

    blocks = wide // tile_cols
    mid_rows = tile_rows - 2 * RADIUS

    def allowed(q_start, q_rows, k_start):
        extent = (q_rows * tile_cols, tile_rows * wide)
        q_index = lax.broadcasted_iota(jnp.int32, extent, 0)
        k_index = lax.broadcasted_iota(jnp.int32, extent, 1)
        q_row, q_col = q_start + q_index // tile_cols, lax.rem(q_index, tile_cols)
        k_block = k_index // tile_cols
        k_row = (k_block * -(-512 // blocks)) // 512
        k_block = k_block - k_row * blocks
        k_row = k_row + k_start
        k_col = lax.rem(k_index, tile_cols)
        if n_col == 2:
            k_shift = jnp.where(k_block == 1, 1 - 2 * c, 0)
        else:
            k_shift = jnp.where(k_block == 1, 1, jnp.where(k_block == 2, -1, 0))
        k_col = k_col + k_shift * tile_cols
        near = (jnp.abs(k_col - q_col) <= RADIUS) & (k_row >= q_row) & (k_row <= q_row + 2 * RADIUS)
        k_col = k_col + c * tile_cols
        k_row = k_row + (r * tile_rows - RADIUS)
        inside = (k_col >= 0) & (k_col < n_col * tile_cols) & (k_row >= 0) & (k_row < n_row * tile_rows)
        return jnp.where(near & inside, 0.0, -1e30)

    middle = (RADIUS, mid_rows, RADIUS, bias_mid)
    edges = (
        (0, RADIUS, 0, bias_edge.at[0]),
        (tile_rows - RADIUS, RADIUS, 2 * RADIUS, bias_edge.at[1]),
    )
    for q_start, q_rows, k_start, mask in (middle,) + edges:
        mask[...] = allowed(q_start, q_rows, k_start)

    def place(k, row, count, col):
        return w_buf.at[k, pl.ds(row, count), col]

    def onward_copy(row, k):
        here = place(k, row, 1, c)
        return remote(here, here, w_send.at[row, k], w_recv.at[row, k], row=onward)

    def back_copy(which, row, count, k):
        here = place(k, row, count, c)
        return remote(here, here, w_back.at[which, k], w_recv.at[row, k], row=mate)

    def side_copy(which, row, count, k, step):
        here = place(k, row, count, c)
        return remote(
            here, here, w_side.at[step - 1, which, k], w_side_recv.at[step - 1, which, k], col=col_of(step)
        )

    def spread(which, row, count, k):
        for step in range(1, n_col):
            side_copy(which, row, count, k, step).start()

    def from_side(which, row, count, k):
        for step in range(1, n_col):
            there = place(k, row, count, col_of(n_col - step))
            remote(
                there, there, w_side.at[step - 1, which, k], w_side_recv.at[step - 1, which, k], col=col_of(step)
            ).wait_recv()

    def own_chunk(k):
        gossip(k).wait_recv()
        gossip(k).wait_send()

        @pl.when(k + AHEAD < CHUNKS)
        def _():
            gossip(k + AHEAD).start()

        columns = pl.ds(pl.multiple_of(k * cut, cut), cut)
        both = o_own[:, columns].astype(F32) + o_peer[k].astype(F32)
        w_buf[k, r, c] = (0.5 * both).astype(BF16)
        onward_copy(r, k).start()
        pl.when(is_inner & (k < OUTER))(lambda: back_copy(0, r, 1, k).start())

    def mate_chunk(k):
        @pl.when(is_inner)
        def _():
            onward_copy(mate, k).wait_recv()
            onward_copy(mate, k).start()
            spread(0, near, 2, k)

    scale = 1.0 / math.sqrt(HDIM)

    def attend(parts):
        def lanes(head):
            return pl.ds(pl.multiple_of(head * HDIM, HDIM), HDIM)

        def near_rows(which, head, k_start):
            return kv_buf[which, pl.ds(k_start, tile_rows), :, lanes(head)].reshape(tile_rows * wide, HDIM)

        scores = []
        for head, (q_start, q_rows, k_start, mask) in parts:
            query = q_buf[pl.ds(q_start, q_rows), :, lanes(head)].reshape(q_rows * tile_cols, HDIM)
            score = lax.dot_general(
                query, near_rows(0, head, k_start), (((1,), (1,)), ((), ())), preferred_element_type=F32
            )
            scores.append(score + mask[...])
        tops = [jnp.max(score, axis=1, keepdims=True) for score in scores]
        weights = [jnp.exp((score - top) * scale) for score, top in zip(scores, tops)]
        ones = jnp.ones((tile_rows * wide, HDIM), BF16)
        sums = [
            jnp.dot(
                weight.astype(BF16),
                jnp.concatenate([near_rows(1, head, k_start), ones], axis=1),
                preferred_element_type=F32,
            )
            for weight, (head, (_, _, k_start, _)) in zip(weights, parts)
        ]
        means = [(both[:, :HDIM] / both[:, HDIM:]).astype(BF16) for both in sums]
        for mean, (head, (q_start, q_rows, _, _)) in zip(means, parts):
            att[pl.ds(q_start * tile_cols, q_rows * tile_cols), lanes(head)] = mean

    loads[1].wait()
    own_chunk(0)
    loads[3].wait()
    loads[4].wait()
    for i in range(len(sides)):
        side(i).wait_recv()

    att_parts = (
        (RADIUS * tile_cols, mid_rows * tile_cols),
        (0, RADIUS * tile_cols),
        ((tile_rows - RADIUS) * tile_cols, RADIUS * tile_cols),
    )

    def att_copy(i):
        start, count = att_parts[i]
        return remote(
            att.at[pl.ds(start, count)], att.at[pl.ds(tokens + start, count)],
            att_send.at[i], att_recv.at[i], row=mate,
        )

    quarter = heads // 4

    def middle_step(i, carry):
        own_chunk(i + 1)

        @pl.when(i == 2)
        def _():
            @pl.when(has_down)
            def _():
                halo(0).wait_recv()
                for i in range(len(sides)):
                    corner(0, i).start()

            @pl.when(has_up)
            def _():
                halo(1).wait_recv()
                for i in range(len(sides)):
                    corner(1, i).start()

        pl.when(i > 1)(lambda: mate_chunk(i - 2))
        attend([(i * quarter + n, middle) for n in range(quarter)])
        return carry

    lax.fori_loop(0, 4, middle_step, 0)
    own_chunk(5)
    mate_chunk(2)

    def against_gate(cond):
        tall = jnp.broadcast_to(cond, (16, span)).astype(BF16)
        return jnp.dot(tall, g_buf[...], preferred_element_type=F32)[0:1]

    half = width // 2
    position = me * span + lax.broadcasted_iota(jnp.int32, (1, span), 1)
    freq_index = jnp.where(position < half, position, position - half).astype(F32)
    frequency = jnp.exp(-math.log(10000.0) * freq_index / half)
    ask.wait_recv()
    mixed_row = 0.5 * (pack_in[:, pl.ds(2 * slot, span)] + class_row(pack_in[:, pl.ds(0, span)]))
    angle = pack_in[:, pl.ds(slot, span)] * frequency
    embed = jnp.where(position < half, jnp.cos(angle), jnp.sin(angle))
    value = mixed_row.astype(BF16).astype(F32) + embed
    cond = (value / (1.0 + jnp.exp(-value))).astype(BF16).astype(F32)
    loads[2].wait()
    reply_out[:, pl.ds(0, width)] = against_gate(cond)
    reply_out[:, pl.ds(width, span)] = cond
    answer = remote(reply_out, reply_in, note_send.at[1], note_recv.at[1], dp=ahead)
    answer.start()


    for i in range(len(sides)):
        pl.when(has_down)(lambda i=i: corner(0, i).wait_recv())
        pl.when(has_up)(lambda i=i: corner(1, i).wait_recv())

    pairs = heads // 2

    def other_half(k):
        @pl.when(is_inner)
        def _():
            onward_copy(n_row - 1 - r, k).wait_recv()
            onward_copy(n_row - 1 - mate, k).wait_recv()
            spread(1, far, 2, k)
            pl.when(k < OUTER)(lambda: back_copy(1, far, 2, k).start())

    def gate_copy(owner, step):
        other = lax.rem(me + step, group)
        return remote(
            gates.at[owner], gates.at[owner], gate_send.at[step - 1], gate_recv.at[owner],
            row=other // n_col, col=lax.rem(other, n_col),
        )

    def send_share():
        answer.wait_recv()
        share = 0.5 * (reply_in[:, pl.ds(0, width)] + against_gate(reply_in[:, pl.ds(width, span)]))
        gates[me] = share
        for step in range(1, group):
            gate_copy(me, step).start()

    def attend_pair(j, carry):
        @pl.when(j + 6 < CHUNKS)
        def _():
            own_chunk(j + 6)

        mate_chunk(j + 3)

        pl.when((j == 1) & is_outer)(lambda: att_copy(0).start())
        pl.when(j == 1)(send_share)
        other_half(j)
        attend([(2 * j + i, edge) for i in range(2) for edge in edges])
        return carry

    lax.fori_loop(0, pairs, attend_pair, 0)

    @pl.when(is_outer)
    def _():
        att_copy(1).start()
        att_copy(2).start()

    mate_chunk(CHUNKS - 1)

    for step in range(1, group):
        owner = lax.rem(me + step, group)
        gate_copy(owner, step).wait_recv()
    gate = gates[0]
    for i in range(1, group):
        gate = gate + gates[i]
    for k in range(CHUNKS):
        gate_sum[k] = gate[:, k * cut : (k + 1) * cut]

    def out_copy(k):
        return pltpu.make_async_copy(
            out_buf.at[k], out_hbm.at[:, pl.ds(pl.multiple_of(k * cut, cut), cut)], out_sem.at[k]
        )

    def mate_copy(k):
        return remote(
            mate_out.at[k], out_hbm.at[:, pl.ds(pl.multiple_of(k * cut, cut), cut)],
            mate_send.at[k], mate_recv.at[k], row=mate,
        )

    def rows_of(count, k):
        product = jnp.dot(att[pl.ds(0, count)], w_buf[k].reshape(inner, cut), preferred_element_type=F32)
        return (gate_sum[k] * product).astype(BF16)

    def own_rows(k):
        out_buf[k] = rows_of(tokens, k)
        out_copy(k).start()

    def project(k, carry):
        pl.when((k + 1 >= pairs) & (k + 1 < CHUNKS))(lambda: other_half(k + 1))
        from_side(0, near, 2, k)
        from_side(1, far, 2, k)

        @pl.when(k == OUTER)
        def _():
            for i in range(3):
                att_copy(i).wait_recv()

        @pl.when(k >= OUTER)
        def _():
            both = rows_of(2 * tokens, k)
            mate_out[k] = both[tokens:]
            mate_copy(k).start()
            out_buf[k] = both[:tokens]
            out_copy(k).start()

        pl.when(k < OUTER)(lambda: own_rows(k))
        return carry

    @pl.when(is_inner)
    def _():
        lax.fori_loop(0, CHUNKS, project, 0)

    @pl.when(is_outer)
    def _():
        def outer_step(k, carry):
            @pl.when(k < OUTER)
            def _():
                back_copy(0, mate, 1, k).wait_recv()
                back_copy(1, far, 2, k).wait_recv()
                spread(0, 0, n_row, k)

            @pl.when(k > 0)
            def _():
                from_side(0, 0, n_row, k - 1)
                own_rows(k - 1)

            return carry

        lax.fori_loop(0, OUTER + 1, outer_step, 0)
        for k in range(OUTER, CHUNKS):
            mate_copy(k).wait_recv()

    def sent(k, carry):
        onward_copy(r, k).wait_send()

        pl.when(is_inner | (k < OUTER))(lambda: out_copy(k).wait())

        @pl.when(is_outer & (k < OUTER))
        def _():
            for step in range(1, n_col):
                side_copy(0, 0, n_row, k, step).wait_send()

        @pl.when(is_inner)
        def _():
            onward_copy(mate, k).wait_send()
            for step in range(1, n_col):
                side_copy(0, near, 2, k, step).wait_send()
                side_copy(1, far, 2, k, step).wait_send()
            pl.when(k >= OUTER)(lambda: mate_copy(k).wait_send())

            @pl.when(k < OUTER)
            def _():
                back_copy(0, r, 1, k).wait_send()
                back_copy(1, far, 2, k).wait_send()

        return carry

    lax.fori_loop(0, CHUNKS, sent, 0)

    @pl.when(is_outer)
    def _():
        for i in range(3):
            att_copy(i).wait_send()

    pl.when(has_up)(lambda: halo(0).wait_send())
    pl.when(has_down)(lambda: halo(1).wait_send())
    for i in range(len(sides)):
        side(i).wait_send()
        pl.when(has_down)(lambda i=i: corner(0, i).wait_send())
        pl.when(has_up)(lambda i=i: corner(1, i).wait_send())
    ask.wait_send()
    answer.wait_send()
    for step in range(1, group):
        gate_copy(me, step).wait_send()


def layer(sizes, distance, number, queries, keyvals, out_weight, gate_weight, class_table, labels, timesteps):
    n_dp, n_row, n_col = sizes
    group = n_row * n_col
    _, tile_rows, tile_cols, inner = queries.shape
    _, shard, width = out_weight.shape
    span = gate_weight.shape[1]
    classes = class_table.shape[1]
    cut = width // CHUNKS
    slot = max(span, 128)
    n_side = 1 if n_col == 2 else 2
    wide = tile_cols * (1 + n_side)
    tokens = tile_rows * tile_cols
    n_k = tile_rows * wide
    dma = pltpu.SemaphoreType.DMA
    return pl.pallas_call(
        functools.partial(kernel, sizes, distance),
        out_shape=jax.ShapeDtypeStruct((tokens, width), BF16),
        in_specs=[pl.BlockSpec(memory_space=pl.ANY)] * 5 + [pl.BlockSpec(memory_space=pltpu.SMEM)] * 2,
        out_specs=pl.BlockSpec(memory_space=pl.ANY),
        scratch_shapes=[
            pltpu.VMEM((tile_rows, tile_cols, inner), BF16),
            pltpu.VMEM((2, tile_rows + 2 * RADIUS, wide, inner), BF16),
            pltpu.VMEM(((tile_rows - 2 * RADIUS) * tile_cols, n_k), F32),
            pltpu.VMEM((2, RADIUS * tile_cols, n_k), F32),
            pltpu.VMEM((2 * tokens, inner), BF16),
            pltpu.VMEM((shard, width), BF16),
            pltpu.VMEM((CHUNKS, shard, cut), BF16),
            pltpu.VMEM((CHUNKS, n_row, n_col, shard, cut), BF16),
            pltpu.VMEM((CHUNKS, tokens, cut), BF16),
            pltpu.VMEM((span, width), BF16),
            pltpu.VMEM((classes, span), BF16),
            pltpu.VMEM((1, 3 * slot), F32),
            pltpu.VMEM((1, 3 * slot), F32),
            pltpu.VMEM((1, width + slot), F32),
            pltpu.VMEM((1, width + slot), F32),
            pltpu.VMEM((group, 1, width), F32),
            pltpu.VMEM((CHUNKS, 1, cut), F32),
            pltpu.VMEM((CHUNKS, tokens, cut), BF16),
            dma((5,)),
            dma((CHUNKS,)),
            dma((CHUNKS,)),
            dma((CHUNKS,)),
            dma((n_row, CHUNKS)),
            dma((2, CHUNKS)),
            dma((n_col - 1, 2, CHUNKS)),
            dma((n_col - 1, 2, CHUNKS)),
            dma((n_row, CHUNKS)),
            dma((3,)),
            dma((3,)),
            dma((CHUNKS,)),
            dma((CHUNKS,)),
            dma((2,)),
            dma((2,)),
            dma((3, n_side)),
            dma((3, n_side)),
            dma((2,)),
            dma((2,)),
            dma((group - 1,)),
            dma((group,)),
        ],
        compiler_params=pltpu.CompilerParams(
            collective_id=number, has_side_effects=True, vmem_limit_bytes=48 * 2**20
        ),
        cost_estimate=pl.CostEstimate(flops=2 * tokens * inner * width, bytes_accessed=2**22, transcendentals=0),
        name=f"sublayer_distance_{distance}",
    )(queries, keyvals, out_weight, gate_weight, class_table, labels, timesteps)


def solution(mesh):
    sizes = tuple(mesh.shape[name] for name in ("dp", "row", "col"))
    bit_count = sizes[0].bit_length() - 1

    def local(queries, keyvals, out_weight, gate_weight, class_table, labels, timesteps, round_index):
        branches = [functools.partial(layer, sizes, 2**power, power) for power in range(bit_count)]
        operands = (queries, keyvals, out_weight, gate_weight, class_table, labels, timesteps)
        result = lax.switch(round_index[0] % bit_count, branches, *operands)
        return result.reshape(queries.shape[:3] + (out_weight.shape[2],))

    placed = (
        P("dp", "row", "col", None),
        P("dp", None, "row", "col", None),
        P("dp", ("row", "col"), None),
        P("dp", ("row", "col"), None),
        P("dp", None, ("row", "col")),
        P("dp"),
        P("dp"),
        P(),
    )
    return jax.shard_map(
        local, mesh=mesh, in_specs=placed, out_specs=P("dp", "row", "col", None), check_vma=False
    )
```
